32 devices in a mesh: dp: 4 (over z), expert: 8 (over y, x, core).
Axes of the slice: x: 2, y: 2, z: 4, core: 2. Of those that a mesh axis runs over, the one named last changes fastest.
Arguments:
- block_input: bfloat16 [2, 4096, 1536], P(None, ('dp', 'expert')), may hold values from -6 to 6
- out_grad: bfloat16 [2, 4096, 1536], P(None, ('dp', 'expert')), may hold values from -6 to 6
- routes: int32 [2, 4096, 6], P(None, ('dp', 'expert')), may hold values from 0 to 31, all different within a row; in each aligned block of 128 rows (0 to 127, 128 to 255, ..., all dimensions but the last counted through in order) at most 36 rows name the same one
- norm_in: bfloat16 [1536], P(('dp', 'expert')), may hold values from 0.5 to 1.5
- in_proj: bfloat16 [1536, 6448], P(('dp', 'expert')), may hold values from -0.15625 to 0.15625
- conv_weight: bfloat16 [4, 3328], replicated, may hold values from -3 to 3
- conv_bias: bfloat16 [3328], replicated, may hold values from -3 to 3
- step_bias: bfloat16 [48], replicated, may hold values from -4 to -1
- log_rate: bfloat16 [48], replicated, may hold values from -3 to 1.5
- skip_gain: bfloat16 [48], replicated, may hold values from 0.5 to 2
- mixer_gain: bfloat16 [3072], P(('dp', 'expert')), may hold values from 0.5 to 1.5
- out_proj: bfloat16 [3072, 1536], P(('dp', 'expert')), may hold values from -0.109375 to 0.109375
- norm_mid: bfloat16 [1536], P(('dp', 'expert')), may hold values from 0.5 to 1.5
- router: bfloat16 [1536, 32], P(('dp', 'expert')), may hold values from -0.078125 to 0.078125
- shared_gate: bfloat16 [1536, 1024], P(('dp', 'expert')), may hold values from -0.15625 to 0.15625
- shared_up: bfloat16 [1536, 1024], P(('dp', 'expert')), may hold values from -0.15625 to 0.15625
- shared_down: bfloat16 [1024, 1536], P(('dp', 'expert')), may hold values from -0.1875 to 0.1875
- expert_gate: bfloat16 [32, 1536, 512], P('expert', 'dp'), may hold values from -0.15625 to 0.15625
- expert_up: bfloat16 [32, 1536, 512], P('expert', 'dp'), may hold values from -0.15625 to 0.15625
- expert_down: bfloat16 [32, 512, 1536], P('expert', 'dp'), may hold values from -0.25 to 0.25
Outputs:
- block_output: bfloat16 [2, 4096, 1536], P(None, ('dp', 'expert'))
- input_grad: float32 [2, 4096, 1536], P(None, ('dp', 'expert'))
- grad_norm_in: float32 [1536], P(('dp', 'expert'))
- grad_in_proj: float32 [1536, 6448], P(('dp', 'expert'))
- grad_conv_weight: float32 [4, 3328], replicated
- grad_conv_bias: float32 [3328], replicated
- grad_step_bias: float32 [48], replicated
- grad_log_rate: float32 [48], replicated
- grad_skip_gain: float32 [48], replicated
- grad_mixer_gain: float32 [3072], P(('dp', 'expert'))
- grad_out_proj: float32 [3072, 1536], P(('dp', 'expert'))
- grad_norm_mid: float32 [1536], P(('dp', 'expert'))
- grad_router: float32 [1536, 32], P(('dp', 'expert'))
- grad_shared_gate: float32 [1536, 1024], P(('dp', 'expert'))
- grad_shared_up: float32 [1536, 1024], P(('dp', 'expert'))
- grad_shared_down: float32 [1024, 1536], P(('dp', 'expert'))
- grad_expert_gate: float32 [32, 1536, 512], P('expert', 'dp')
- grad_expert_up: float32 [32, 1536, 512], P('expert', 'dp')
- grad_expert_down: float32 [32, 512, 1536], P('expert', 'dp')
The draws below stay inside these ranges and needn't reach their ends.
Inputs may be any that keep to these rules, and one draw needn't show every extreme that they name: `routes`: each row names 6 different experts; within the rows of one device in one micro-batch (aligned blocks of 128 rows) no expert is named more than 36 times, a bound that some block reaches.
All inputs are finite; a program needn't handle non-finite values.
Results may differ from the reference program's by a relative error of at most 0.013.
Values may be sent and summed in bfloat16 or wider, within the bound.
A program may use at most 512 MiB of HBM per device.

```python
import math
from functools import partial
import jax
import jax.numpy as jnp
import numpy as np
from jax import lax

D = 1536
H = 48
KC = 4
TOPK = 6
FE = 512
FS = 1024
LEN = 128
MICRO = 2
SPAN = 64
DI = 3072
CONV = 3328
ZW = 6448
E = 32
CAP = 36
TOKENS = 4096


def levels(rng, extent, cuts, smallest, largest):
    def one(dim, parts):
        steps = jax.random.uniform(jax.random.fold_in(jax.random.fold_in(rng, 6), dim), (parts,), jnp.float32, smallest / len(cuts), largest / len(cuts))
        return jnp.repeat(jnp.exp(steps), extent[dim] // parts).reshape((-1,) + (1,) * (len(extent) - dim - 1))

    level = one(*cuts[0])
    for cut in cuts[1:]:
        level = level * one(*cut)
    return level


def deal_out(stream_key, own, number, rows, amount, top, limit, lean):
    order = jax.random.permutation(stream_key, amount)
    crowded, usual = portions_of(amount, rows * top, limit, lean, True), portions_of(amount, rows * top, limit, lean, False)
    places = jnp.arange(amount)

    def named(sizes, rotation):
        used = int((sizes > 0).sum())
        fixed = max(1, used // 4)
        passed = fixed + (places - fixed + rotation * (used - fixed)) % max(1, amount - fixed)
        return jnp.zeros((amount,), jnp.int32).at[order[jnp.where(places < fixed, places, passed)]].set(jnp.asarray(sizes, jnp.int32))

    sizes = jnp.where(number % 4 == 0, named(crowded, number // 4), named(usual, number - number // 4 - 1))
    mixed = jax.random.permutation(jax.random.fold_in(own, 3), amount)
    source_of, sink = mixed[0:amount // 2 * 2:2], mixed[1:amount // 2 * 2:2]
    slack = jnp.minimum(sizes[source_of] - 1, limit - sizes[sink]) // 2
    slack = jnp.where((source_of == order[0]) | (sink == order[0]) | (sizes[sink] == 0), 0, jnp.maximum(slack, 0))
    passed = jax.random.randint(jax.random.fold_in(own, 4), (amount // 2,), 0, 1 << 20) % (slack + 1)
    sizes = sizes.at[source_of].add(-passed).at[sink].add(passed)
    members = jnp.searchsorted(jnp.cumsum(sizes), jnp.arange(rows * top), side="right").astype(jnp.int32)
    table = members.reshape(top, rows).T
    table = table[jax.random.permutation(jax.random.fold_in(own, 1), rows)]
    rotation = jax.random.randint(jax.random.fold_in(own, 2), (rows, 1), 0, top)
    return jnp.take_along_axis(table, (jnp.arange(top)[None, :] + rotation) % top, axis=1)


def portions_of(amount, total, most, skew, full):
    weights = [(1 << 20) // math.isqrt(standing ** skew) + 1 for standing in range(1, amount + 1)]
    largest = most if full else min(most, max(-(-total // amount), total * weights[0] // sum(weights)))
    least = 1 if total - largest >= amount - 1 else 0
    given, surplus = [largest] + [least] * (amount - 1), total - largest - least * (amount - 1)
    while surplus > 0:
        free = [i for i in range(1, amount) if given[i] < largest] or [i for i in range(1, amount) if given[i] < most]
        pool, remaining = sum([weights[i] for i in free]), surplus
        for i in free:
            more = min(most - given[i], max(1, remaining * weights[i] // pool), surplus)
            given[i] = given[i] + more
            surplus = surplus - more
    return np.array(given)


def scatter_about(rng, dims, deviation, most, cuts=(), kind=jnp.bfloat16):
    loudness = levels(rng, dims, cuts, -0.22, 0.18) if cuts else 1.0
    array = jax.random.normal(rng, dims, jnp.float32) * deviation * loudness
    return jnp.minimum(jnp.maximum(array, -most), most).astype(kind)


def setup_inputs(seed: int = 0) -> dict:
    splits = jax.random.split(jax.random.key(seed), 21)
    block_input = scatter_about(splits[0], (MICRO, TOKENS, D), 1.0, 6.0, ((1, 32),))
    out_grad = scatter_about(splits[1], (MICRO, TOKENS, D), 1.0, 6.0, ((1, 32),))
    routes_keys = jax.random.split(jax.random.fold_in(splits[2], 1), MICRO * TOKENS // LEN)
    routes_turns = jax.random.permutation(jax.random.fold_in(splits[2], 3), MICRO * TOKENS // LEN)
    routes = jax.vmap(lambda own, number: deal_out(jax.random.fold_in(splits[2], 2), own, number, LEN, E, TOPK, CAP, 1))(routes_keys, routes_turns).reshape((MICRO, TOKENS, TOPK))
    norm_in = jnp.clip(1.0 + 0.1 * jax.random.normal(splits[3], (D,), jnp.float32), 0.5, 1.5).astype(jnp.bfloat16)
    in_proj = scatter_about(splits[4], (D, ZW), D ** -0.5, 0.15625, ((0, 32),))
    conv_weight = scatter_about(splits[5], (KC, CONV), KC ** -0.5, 3.0)
    conv_bias = scatter_about(splits[6], (CONV,), 0.3, 3.0)
    step_bias = jnp.clip(jax.random.uniform(splits[7], (H,), jnp.float32, -4.0, -1.0), -4.0, -1.0).astype(jnp.bfloat16)
    log_rate = jnp.clip(jax.random.uniform(splits[8], (H,), jnp.float32, -3.0, 1.5), -3.0, 1.5).astype(jnp.bfloat16)
    skip_gain = jnp.clip(jax.random.uniform(splits[9], (H,), jnp.float32, 0.5, 2.0), 0.5, 2.0).astype(jnp.bfloat16)
    mixer_gain = jnp.clip(1.0 + 0.1 * jax.random.normal(splits[10], (DI,), jnp.float32), 0.5, 1.5).astype(jnp.bfloat16)
    out_proj = scatter_about(splits[11], (DI, D), DI ** -0.5, 0.109375, ((0, 32),))
    norm_mid = jnp.clip(1.0 + 0.1 * jax.random.normal(splits[12], (D,), jnp.float32), 0.5, 1.5).astype(jnp.bfloat16)
    router = scatter_about(splits[13], (D, E), (4 * D) ** -0.5, 0.078125, ((0, 32),))
    shared_gate = scatter_about(splits[14], (D, FS), D ** -0.5, 0.15625, ((0, 32),))
    shared_up = scatter_about(splits[15], (D, FS), D ** -0.5, 0.15625, ((0, 32),))
    shared_down = scatter_about(splits[16], (FS, D), FS ** -0.5, 0.1875, ((0, 32),))
    expert_gate = scatter_about(splits[17], (E, D, FE), D ** -0.5, 0.15625, ((0, 8), (1, 4)))
    expert_up = scatter_about(splits[18], (E, D, FE), D ** -0.5, 0.15625, ((0, 8), (1, 4)))
    expert_down = scatter_about(splits[19], (E, FE, D), FE ** -0.5, 0.25, ((0, 8), (1, 4)))
    return dict(block_input=block_input, out_grad=out_grad, routes=routes, norm_in=norm_in, in_proj=in_proj, conv_weight=conv_weight, conv_bias=conv_bias, step_bias=step_bias, log_rate=log_rate, skip_gain=skip_gain, mixer_gain=mixer_gain, out_proj=out_proj, norm_mid=norm_mid, router=router, shared_gate=shared_gate, shared_up=shared_up, shared_down=shared_down, expert_gate=expert_gate, expert_up=expert_up, expert_down=expert_down)


@jax.custom_vjp
def low(v):
    return lax.optimization_barrier(v.astype(jnp.bfloat16)).astype(jnp.float32)

@jax.custom_vjp
def low_back(v):
    return v

def low_keep(v):
    return (low(v), None)

def low_pass(kept, grad):
    return (grad,)

def back_keep(v):
    return (v, None)

def back_low(kept, grad):
    return (low(grad),)
low.defvjp(low_keep, low_pass)
low_back.defvjp(back_keep, back_low)
epsilon = 1e-05
highest = lax.Precision.HIGHEST

def rms_scale(value, gain):
    return value * lax.rsqrt(lax.optimization_barrier(jnp.mean(value * value, axis=-1, keepdims=True)) + epsilon) * gain

def scan_blocks(inputs, input_map, output_map, decay, block):
    length, heads, width = inputs.shape
    number = length // block
    states = input_map.shape[-1]
    inputs = inputs.reshape(number, block, heads, width)
    input_map = input_map.reshape(number, block, states)
    output_map = output_map.reshape(number, block, states)
    cumul = jnp.cumsum(decay.reshape(number, block, heads), axis=1)
    rowidx = lax.broadcasted_iota(jnp.int32, (block, block), 0)
    colidx = lax.broadcasted_iota(jnp.int32, (block, block), 1)
    lower = (rowidx >= colidx)[None, :, :, None]
    spread = cumul[:, :, None, :] - cumul[:, None, :, :]
    weights = jnp.exp(jnp.where(lower, spread, 0.0)) * lower.astype(jnp.float32)
    inner = jnp.einsum('cin,cjn->cij', output_map, input_map, precision=highest)
    local_out = jnp.einsum('cij,cijh,cjhp->cihp', inner, weights, inputs, precision=highest)
    to_end = jnp.exp(cumul[:, -1:, :] - cumul)
    block_state = jnp.einsum('cjn,cjh,cjhp->chnp', input_map, to_end, inputs, precision=highest)
    block_decay = jnp.exp(cumul[:, -1, :])

    def advance(carry, item):
        state_now, decay_now = item
        return (carry * decay_now[:, None, None] + state_now, carry)
    anchor = jnp.zeros((heads, states, width), jnp.float32)
    unused, entering = lax.scan(advance, anchor, (block_state, block_decay))
    carried = jnp.einsum('cin,chnp,cih->cihp', output_map, entering, jnp.exp(cumul), precision=highest)
    return (local_out + carried).reshape(length, heads, width)

def mixer(merged, conv_kernel, conv_shift, step_shift, rate_log, skip_scale, mix_gain, heads, block):
    length = merged.shape[0]
    inner_width = mix_gain.shape[0]
    width = inner_width // heads
    conv_width = conv_shift.shape[0]
    states = (conv_width - inner_width) // 2
    kernel = conv_kernel.shape[0]
    gate_part = merged[:, :inner_width]
    signal = merged[:, inner_width:inner_width + conv_width]
    step_raw = merged[:, inner_width + conv_width:]
    padded = jnp.pad(signal, ((kernel - 1, 0), (0, 0)))
    summed = jnp.zeros_like(signal) + conv_shift
    for shift_at in range(kernel):
        summed = summed + conv_kernel[shift_at] * padded[shift_at:shift_at + length]
    activated = jax.nn.silu(summed)
    values = activated[:, :inner_width].reshape(length, heads, width)
    input_map = activated[:, inner_width:inner_width + states]
    output_map = activated[:, inner_width + states:]
    step = jax.nn.softplus(step_raw + step_shift)
    decay = -jnp.exp(rate_log) * step
    scanned = scan_blocks(values * step[:, :, None], input_map, output_map, decay, block)
    joined = (scanned + skip_scale[None, :, None] * values).reshape(length, inner_width)
    return rms_scale(joined * jax.nn.silu(gate_part), mix_gain)

def group_layer(params, block_in, route_ids, capacity):
    norm_in, in_proj, conv_weight, conv_bias, step_bias, log_rate, skip_gain, mixer_gain, out_proj, norm_mid, router, shared_gate, shared_up, shared_down, expert_gate, expert_up, expert_down = params
    group, length, width = block_in.shape
    experts = router.shape[1]
    picks = route_ids.shape[-1]
    normed = low(rms_scale(block_in, norm_in))
    merged = low_back(jnp.einsum('gld,dz->glz', normed, in_proj, precision=highest))
    mix_one = partial(mixer, conv_kernel=conv_weight, conv_shift=conv_bias, step_shift=step_bias, rate_log=log_rate, skip_scale=skip_gain, mix_gain=mixer_gain, heads=H, block=SPAN)
    mixed = low(jax.vmap(mix_one)(merged))
    mixer_out = low_back(jnp.einsum('glz,zd->gld', mixed, out_proj, precision=highest))
    middle = block_in + mixer_out
    routed = low(rms_scale(middle, norm_mid))
    logits = low_back(jnp.einsum('gld,de->gle', routed, router, precision=highest))
    chosen = (route_ids[..., None] == jnp.arange(experts, dtype=jnp.int32)).astype(jnp.float32)
    picked = lax.optimization_barrier(jnp.sum(chosen * logits[:, :, None, :], axis=-1))
    gates = jax.nn.softmax(picked, axis=-1)
    shared_pre = low_back(jnp.einsum('gld,df->glf', routed, shared_gate, precision=highest))
    shared_lin = low_back(jnp.einsum('gld,df->glf', routed, shared_up, precision=highest))
    shared_hidden = low(jax.nn.silu(shared_pre) * shared_lin)
    shared_out = low_back(jnp.einsum('glf,fd->gld', shared_hidden, shared_down, precision=highest))
    flat_ids = route_ids.reshape(group, length * picks)
    marks = (flat_ids[..., None] == jnp.arange(experts, dtype=jnp.int32)).astype(jnp.int32)
    before = jnp.cumsum(marks, axis=1) - marks
    places = flat_ids * capacity + lax.optimization_barrier(jnp.sum(before * marks, axis=-1))
    copies = low_back(jnp.broadcast_to(routed[:, :, None, :], (group, length, picks, width)))
    copies = copies.reshape(group, length * picks, width)

    def place(rows, where):
        return jnp.zeros((experts * capacity, width), jnp.float32).at[where].set(rows)
    buffers = jax.vmap(place)(copies, places)
    buffers = buffers.reshape(group, experts, capacity, width).transpose(1, 0, 2, 3)
    buffers = buffers.reshape(experts, group * capacity, width)
    pre_gate = low_back(jnp.einsum('erd,edf->erf', buffers, expert_gate, precision=highest))
    pre_up = low_back(jnp.einsum('erd,edf->erf', buffers, expert_up, precision=highest))
    expert_hidden = low(jax.nn.silu(pre_gate) * pre_up)
    produced = low(low_back(jnp.einsum('erf,efd->erd', expert_hidden, expert_down, precision=highest)))
    returned = produced.reshape(experts, group, capacity, width).transpose(1, 0, 2, 3)
    returned = returned.reshape(group, experts * capacity, width)
    taken = jax.vmap(lambda rows, where: rows[where])(returned, places).reshape(group, length, picks, width)
    expert_sum = lax.optimization_barrier(jnp.sum(gates[..., None] * taken, axis=2))
    return middle + expert_sum + shared_out

def reference(block_input, out_grad, routes, norm_in, in_proj, conv_weight, conv_bias, step_bias, log_rate, skip_gain, mixer_gain, out_proj, norm_mid, router, shared_gate, shared_up, shared_down, expert_gate, expert_up, expert_down):
    params = tuple((weight.astype(jnp.float32) for weight in (norm_in, in_proj, conv_weight, conv_bias, step_bias, log_rate, skip_gain, mixer_gain, out_proj, norm_mid, router, shared_gate, shared_up, shared_down, expert_gate, expert_up, expert_down)))
    sequences = TOKENS // LEN
    group = 1
    for size_try in range(1, sequences + 1):
        if sequences % size_try == 0 and size_try * LEN <= 4096:
            group = size_try
    turns = MICRO * sequences // group
    inputs = block_input.astype(jnp.float32).reshape(turns, group, LEN, D)
    cotangents = out_grad.astype(jnp.float32).reshape(turns, group, LEN, D)
    route_turns = routes.reshape(turns, group, LEN, TOPK)

    def advance(totals, item):
        block_in, cotangent, route_ids = item
        result, pullback = jax.vjp(lambda weights, values: group_layer(weights, values, route_ids, CAP), params, block_in)
        weight_grads, in_grads = pullback(cotangent)
        totals = jax.tree.map(lambda a, b: a + b, totals, weight_grads)
        return (totals, (result, in_grads))
    anchor = jax.tree.map(jnp.zeros_like, params)
    totals, (outputs, in_grads) = lax.scan(advance, anchor, (inputs, cotangents, route_turns))
    final_out = outputs.reshape(MICRO, TOKENS, D).astype(jnp.bfloat16)
    return (final_out, in_grads.reshape(MICRO, TOKENS, D), totals[0], totals[1], totals[2], totals[3], totals[4], totals[5], totals[6], totals[7], totals[8], totals[9], totals[10], totals[11], totals[12], totals[13], totals[14], totals[15], totals[16])
```

```python
from functools import partial

import jax
import jax.numpy as jnp
from jax import lax
from jax.experimental import pallas as pl
from jax.experimental.pallas import tpu as pltpu
from jax.sharding import PartitionSpec as P

H = 48
LEN = 128
LANES = 128
epsilon = 1e-05
f32 = jnp.float32
b16 = jnp.bfloat16
highest = lax.Precision.HIGHEST
NT = (((1,), (1,)), ((), ()))


def sigmoid(value):
    return 0.5 * jnp.tanh(0.5 * value) + 0.5


def grids():
    row = lax.broadcasted_iota(jnp.int32, (LEN, LANES), 0)
    lane = lax.broadcasted_iota(jnp.int32, (LEN, LANES), 1)
    return row, lane


def shifted(signal, row):
    return [signal] + [jnp.where(row >= k, pltpu.roll(signal, k, 0), 0.0) for k in (1, 2, 3)]


def convolved(parts, weight_ref, bias_ref, block):
    weight = weight_ref[:, block]
    total = bias_ref[:, block] + weight[3:4] * parts[0]
    for k in (1, 2, 3):
        total = total + weight[3 - k : 4 - k] * parts[k]
    return total


def pick(value, lane):
    low = lane < LANES // 2
    return jnp.concatenate([jnp.where(low, value, 0.0), jnp.where(low, 0.0, value)], axis=0)


def step_terms(merged_ref, step_ref, rate_ref, tail):
    raw = merged_ref[:, tail] + step_ref[...]
    step = jnp.maximum(raw, 0.0) + jnp.log1p(jnp.exp(-jnp.abs(raw)))
    decay = -jnp.exp(rate_ref[...]) * step
    row, lane = grids()
    cumul = jnp.dot(
        (row >= lane).astype(f32), decay, precision=highest, preferred_element_type=f32
    )
    return raw, step, decay, cumul


def forward_kernel(
    pairs,
    merged_ref,
    weight_ref,
    bias_ref,
    step_ref,
    rate_ref,
    skip_ref,
    gain_ref,
    mixed_ref,
    joined_ref,
    square_ref,
    cross_ref,
):
    row, lane = grids()
    tail = pl.ds((2 * pairs + 2) * LANES, LANES)
    raw, step, decay, cumul = step_terms(merged_ref, step_ref, rate_ref, tail)
    cross_ref[...] = cumul.T
    maps = []
    for at in (0, 1):
        signal = merged_ref[:, pl.ds((2 * pairs + at) * LANES, LANES)]
        block = pl.ds((pairs + at) * LANES, LANES)
        conv = convolved(shifted(signal, row), weight_ref, bias_ref, block)
        maps.append((conv * sigmoid(conv)).astype(b16))
    inner = lax.dot_general(maps[1], maps[0], NT, preferred_element_type=f32)
    square = jnp.zeros((LEN, LANES), f32)
    for pair in range(pairs):
        block = pl.ds(pair * LANES, LANES)
        signal = merged_ref[:, pl.ds((pairs + pair) * LANES, LANES)]
        conv = convolved(shifted(signal, row), weight_ref, bias_ref, block)
        values = conv * sigmoid(conv)
        steps, parts = [], []
        for head in (2 * pair, 2 * pair + 1):
            steps.append(step[:, head : head + 1])
            spread = cumul[:, head : head + 1] - cross_ref[head : head + 1, :]
            parts.append(inner * jnp.exp(jnp.where(row >= lane, spread, -1e30)))
        scaled = values * jnp.where(lane < LANES // 2, steps[0], steps[1])
        scanned = jnp.dot(
            jnp.concatenate(parts, axis=1).astype(b16),
            pick(scaled, lane).astype(b16),
            preferred_element_type=f32,
        )
        joined = scanned + skip_ref[:, block] * values
        joined_ref[:, block] = joined
        gate = merged_ref[:, block]
        gated = joined * (gate * sigmoid(gate))
        mixed_ref[:, block] = (gated * gain_ref[:, block]).astype(b16)
        square = square + gated * gated
    square_ref[...] = square


def backward_kernel(
    pairs,
    merged_ref,
    joined_ref,
    grad_ref,
    inward_ref,
    weight_ref,
    bias_ref,
    step_ref,
    rate_ref,
    skip_ref,
    gain_ref,
    out_ref,
    weight_out,
    bias_out,
    skip_out,
    head_out,
    cross_ref,
):
    row, lane = grids()
    low = lane < LANES // 2

    @pl.when(pl.program_id(0) == 0)
    def _():
        weight_out[...] = jnp.zeros_like(weight_out)
        bias_out[...] = jnp.zeros_like(bias_out)
        skip_out[...] = jnp.zeros_like(skip_out)
        head_out[...] = jnp.zeros_like(head_out)

    inward = inward_ref[...]
    tail = pl.ds((2 * pairs + 2) * LANES, LANES)
    raw, step, decay, cumul = step_terms(merged_ref, step_ref, rate_ref, tail)
    cross_ref[...] = cumul.T
    convs, slopes, shifts, maps = [], [], [], []
    for at in (0, 1):
        signal = merged_ref[:, pl.ds((2 * pairs + at) * LANES, LANES)]
        parts = shifted(signal, row)
        conv = convolved(parts, weight_ref, bias_ref, pl.ds((pairs + at) * LANES, LANES))
        sigma = sigmoid(conv)
        shifts.append(parts)
        slopes.append(sigma * (1.0 + conv * (1.0 - sigma)))
        maps.append((conv * sigma).astype(b16))
    flipped = lax.dot_general(maps[0], maps[1], NT, preferred_element_type=f32)
    dinner = jnp.zeros((LEN, LEN), f32)
    dstep = jnp.zeros((LEN, LANES), f32)
    dcum = jnp.zeros((LEN, LANES), f32)

    def back_conv(grad, parts, block, out_block):
        bias_out[:, block] += jnp.sum(grad, axis=0, keepdims=True)
        weight = weight_ref[:, block]
        total = weight[3:4] * grad
        taps = [jnp.sum(grad * parts[3 - k], axis=0, keepdims=True) for k in range(4)]
        weight_out[:, block] += jnp.concatenate(taps, axis=0)
        for k in (1, 2, 3):
            later = jnp.where(row < LEN - k, pltpu.roll(grad, LEN - k, 0), 0.0)
            total = total + weight[3 - k : 4 - k] * later
        out_ref[:, out_block] = total.astype(b16)

    for pair in range(pairs):
        block = pl.ds(pair * LANES, LANES)
        other = pl.ds((pairs + pair) * LANES, LANES)
        gate = merged_ref[:, block]
        joined = joined_ref[:, block]
        sigma = sigmoid(gate)
        soft = gate * sigma
        dgated = grad_ref[:, block] * gain_ref[:, block] - joined * soft * inward
        djoined = dgated * soft
        out_ref[:, block] = (dgated * joined * (sigma + soft * (1.0 - sigma))).astype(b16)

        parts = shifted(merged_ref[:, other], row)
        conv = convolved(parts, weight_ref, bias_ref, block)
        csig = sigmoid(conv)
        values = conv * csig
        skip = skip_ref[:, block]
        skip_out[:, block] += jnp.sum(djoined * values, axis=0, keepdims=True)
        scanned = joined - skip * values
        steps, blends, spreads = [], [], []
        for head in (2 * pair, 2 * pair + 1):
            steps.append(step[:, head : head + 1])
            spread = cumul[:, head : head + 1] - cross_ref[head : head + 1, :]
            spreads.append(jnp.exp(jnp.where(row >= lane, spread, -1e30)))
            blends.append(flipped * jnp.exp(jnp.where(row <= lane, -spread, -1e30)))
        widened = jnp.where(low, steps[0], steps[1])
        scaled = (values * widened).astype(b16)
        dlow = djoined.astype(b16)
        both = pick(djoined, lane).astype(b16)
        dweights = lax.dot_general(both, scaled, NT, preferred_element_type=f32)
        dinner = dinner + dweights[:LEN] * spreads[0] + dweights[LEN:] * spreads[1]
        dscaled = jnp.dot(
            jnp.concatenate(blends, axis=1).astype(b16), both, preferred_element_type=f32
        )
        dvalues = skip * djoined + dscaled * widened
        first = dscaled * values
        second = dlow.astype(f32) * scanned - scaled.astype(f32) * dscaled
        for at in (0, 1):
            mine = low if at == 0 else jnp.logical_not(low)
            here = lane == 2 * pair + at
            total = jnp.sum(jnp.where(mine, first, 0.0), axis=1, keepdims=True)
            dstep = jnp.where(here, total, dstep)
            total = jnp.sum(jnp.where(mine, second, 0.0), axis=1, keepdims=True)
            dcum = jnp.where(here, total, dcum)
        back_conv(dvalues * (csig * (1.0 + conv * (1.0 - csig))), parts, block, other)
    dmaps = (
        jnp.dot(dinner.T.astype(b16), maps[1], preferred_element_type=f32),
        jnp.dot(dinner.astype(b16), maps[0], preferred_element_type=f32),
    )
    for at in (0, 1):
        back_conv(
            dmaps[at] * slopes[at],
            shifts[at],
            pl.ds((pairs + at) * LANES, LANES),
            pl.ds((2 * pairs + at) * LANES, LANES),
        )
    ddecay = jnp.dot(
        (row <= lane).astype(f32), dcum, precision=highest, preferred_element_type=f32
    )
    dstep = dstep - ddecay * jnp.exp(rate_ref[...])
    draw = jnp.where(lane < 2 * pairs, dstep * sigmoid(raw), 0.0)
    out_ref[:, tail] = draw.astype(b16)
    head_out[0:1, :] += jnp.sum(draw, axis=0, keepdims=True)
    head_out[1:2, :] += jnp.sum(ddecay * decay, axis=0, keepdims=True)


def rows_of(columns):
    return pl.BlockSpec((LEN, columns), lambda s: (s, 0))


def fixed(rows, columns):
    return pl.BlockSpec((rows, columns), lambda s: (0, 0))


def mix_forward(merged, params):
    tokens, columns = merged.shape
    width = params[-1].shape[1]
    return pl.pallas_call(
        partial(forward_kernel, width // LANES),
        grid=(tokens // LEN,),
        in_specs=[rows_of(columns)] + [fixed(*p.shape) for p in params],
        out_specs=[rows_of(width), rows_of(width), rows_of(LANES)],
        out_shape=[
            jax.ShapeDtypeStruct((tokens, width), b16),
            jax.ShapeDtypeStruct((tokens, width), f32),
            jax.ShapeDtypeStruct((tokens, LANES), f32),
        ],
        scratch_shapes=[pltpu.VMEM((LANES, LEN), f32)],
        compiler_params=pltpu.CompilerParams(vmem_limit_bytes=32 << 20),
        cost_estimate=pl.CostEstimate(
            flops=tokens * width * 9000, bytes_accessed=tokens * columns * 8, transcendentals=0
        ),
    )(merged, *params)


def mix_backward(merged, joined, grad, inward, params):
    tokens, columns = merged.shape
    width = params[-1].shape[1]
    conv = params[0].shape[1]
    return pl.pallas_call(
        partial(backward_kernel, width // LANES),
        grid=(tokens // LEN,),
        in_specs=[rows_of(columns), rows_of(width), rows_of(width), rows_of(1)]
        + [fixed(*p.shape) for p in params],
        out_specs=[
            rows_of(columns),
            fixed(4, conv),
            fixed(1, conv),
            fixed(1, width),
            fixed(8, LANES),
        ],
        out_shape=[
            jax.ShapeDtypeStruct((tokens, columns), b16),
            jax.ShapeDtypeStruct((4, conv), f32),
            jax.ShapeDtypeStruct((1, conv), f32),
            jax.ShapeDtypeStruct((1, width), f32),
            jax.ShapeDtypeStruct((8, LANES), f32),
        ],
        scratch_shapes=[pltpu.VMEM((LANES, LEN), f32)],
        compiler_params=pltpu.CompilerParams(vmem_limit_bytes=32 << 20),
        cost_estimate=pl.CostEstimate(
            flops=tokens * width * 18000, bytes_accessed=tokens * columns * 12, transcendentals=0
        ),
    )(merged, joined, grad, inward, *params)


MESH = pl.DeviceIdType.MESH


def neighbours(me):
    core, column, line = me % 2, (me // 2) % 2, me // 4
    return 1 - 2 * core, 2 - 4 * column, 4 - 8 * line


def greet(peers):
    barrier = pltpu.get_barrier_semaphore()
    for peer in peers:
        pl.semaphore_signal(barrier, inc=1, device_id={"expert": peer}, device_id_type=MESH)
    pl.semaphore_wait(barrier, len(peers))


def gather_kernel(own_ref, out_ref, send_sem, recv_sem, copy_sem):
    me = lax.axis_index("expert")
    core, column, line = neighbours(me)
    rows = own_ref.shape[0]
    top, bottom = pl.ds(0, rows // 2), pl.ds(rows // 2, rows // 2)
    greet((me + core, me + column, me + line))

    def copy(at, src, dst, peer):
        return pltpu.make_async_remote_copy(
            src_ref=src,
            dst_ref=dst,
            send_sem=send_sem.at[at],
            recv_sem=recv_sem.at[at],
            device_id={"expert": peer},
            device_id_type=MESH,
        )

    here = pltpu.make_async_copy(own_ref, out_ref.at[me], copy_sem)
    to_x = copy(0, own_ref, out_ref.at[me], me + column)
    to_y = copy(1, own_ref, out_ref.at[me], me + line)
    to_core = copy(2, own_ref, out_ref.at[me], me + core)
    to_x.start()
    to_y.start()
    to_core.start()
    here.start()
    x_block, y_block = out_ref.at[me + column], out_ref.at[me + line]
    diagonal = out_ref.at[me + column + line]
    to_x.wait_recv()
    x_relay = copy(3, x_block.at[top], x_block.at[top], me + line)
    x_relay.start()
    x_core = copy(5, x_block, x_block, me + core)
    x_core.start()
    to_y.wait_recv()
    y_relay = copy(4, y_block.at[bottom], y_block.at[bottom], me + column)
    y_relay.start()
    y_core = copy(6, y_block, y_block, me + core)
    y_core.start()
    x_relay.wait_recv()
    y_relay.wait_recv()
    d_core = copy(7, diagonal, diagonal, me + core)
    d_core.start()
    here.wait()
    to_core.wait_recv()
    x_core.wait_recv()
    y_core.wait_recv()
    d_core.wait_recv()
    for sent in (to_x, to_y, to_core, x_relay, x_core, y_relay, y_core, d_core):
        sent.wait_send()


def plane_gather(own, number):
    if lax.axis_size("expert") != 8:
        return lax.all_gather(own, "expert", axis=0, tiled=True)
    rows, columns = own.shape
    out = pl.pallas_call(
        gather_kernel,
        out_shape=jax.ShapeDtypeStruct((8, rows, columns), own.dtype),
        in_specs=[pl.BlockSpec(memory_space=pl.ANY)],
        out_specs=pl.BlockSpec(memory_space=pl.ANY),
        scratch_shapes=[
            pltpu.SemaphoreType.DMA((8,)),
            pltpu.SemaphoreType.DMA((8,)),
            pltpu.SemaphoreType.DMA,
        ],
        compiler_params=pltpu.CompilerParams(collective_id=number, has_side_effects=True),
        cost_estimate=pl.CostEstimate(
            flops=0, bytes_accessed=rows * columns * 96, transcendentals=0
        ),
    )(own)
    return out.reshape(8 * rows, columns)


def scatter_kernel(
    parts_ref, out_ref, mine, theirs, x_in, y_in, dx_in, dy_in, send_sem, recv_sem, copy_sem
):
    me = lax.axis_index("expert")
    core, column, line = neighbours(me)
    rows = out_ref.shape[0]
    half = rows // 2
    top, bottom = pl.ds(0, half), pl.ds(half, half)
    greet((me + core, me + column, me + line))

    def copy(at, src, dst, peer):
        return pltpu.make_async_remote_copy(
            src_ref=src,
            dst_ref=dst,
            send_sem=send_sem.at[at],
            recv_sem=recv_sem.at[at],
            device_id={"expert": peer},
            device_id_type=MESH,
        )

    chips = (me + column + line, me + column, me + line, me)
    swaps = [copy(k, parts_ref.at[chips[k] + core], theirs.at[k], me + core) for k in range(4)]
    loads = [
        pltpu.make_async_copy(parts_ref.at[chips[k]], mine.at[k], copy_sem.at[k]) for k in range(4)
    ]
    for k in range(4):
        swaps[k].start()
        loads[k].start()

    def each(first, count, step):
        def body(i, carry):
            step(pl.ds(pl.multiple_of(first + i * 16, 16), 16))
            return carry

        lax.fori_loop(0, count // 16, body, 0)

    def pair_sum(k):
        loads[k].wait()
        swaps[k].wait_recv()

        def step(block):
            total = mine[k, block].astype(f32) + theirs[k, block].astype(f32)
            if k == 3:
                out_ref[block, :] = total
            else:
                mine[k, block] = total.astype(b16)

        each(0, rows, step)

    pair_sum(0)
    d_x = copy(4, mine.at[0, top], dx_in, me + column)
    d_y = copy(5, mine.at[0, bottom], dy_in, me + line)
    d_x.start()
    d_y.start()
    pair_sum(1)
    x_top = copy(6, mine.at[1, top], x_in.at[top], me + column)
    x_top.start()
    pair_sum(2)
    y_bottom = copy(7, mine.at[2, bottom], y_in.at[bottom], me + line)
    y_bottom.start()
    pair_sum(3)

    d_x.wait_recv()

    def add_y(block):
        mine[2, block] = (mine[2, block].astype(f32) + dx_in[block, :].astype(f32)).astype(b16)

    each(0, half, add_y)
    y_top = copy(8, mine.at[2, top], y_in.at[top], me + line)
    y_top.start()
    d_y.wait_recv()

    def add_x(block):
        low = pl.ds(pl.multiple_of(block.start - half, 16), 16)
        mine[1, block] = (mine[1, block].astype(f32) + dy_in[low, :].astype(f32)).astype(b16)

    each(half, half, add_x)
    x_bottom = copy(9, mine.at[1, bottom], x_in.at[bottom], me + column)
    x_bottom.start()
    x_top.wait_recv()
    y_bottom.wait_recv()
    y_top.wait_recv()
    x_bottom.wait_recv()

    def finish(block):
        out_ref[block, :] = (
            out_ref[block, :] + x_in[block, :].astype(f32) + y_in[block, :].astype(f32)
        )

    each(0, rows, finish)
    for sent in swaps + [d_x, d_y, x_top, y_bottom, y_top, x_bottom]:
        sent.wait_send()


def plane_scatter(parts, number):
    if lax.axis_size("expert") != 8:
        return lax.psum_scatter(parts, "expert", scatter_dimension=0, tiled=True).astype(f32)
    rows, columns = parts.shape[0] // 8, parts.shape[1]
    return pl.pallas_call(
        scatter_kernel,
        out_shape=jax.ShapeDtypeStruct((rows, columns), f32),
        in_specs=[pl.BlockSpec(memory_space=pl.ANY)],
        out_specs=pl.BlockSpec(memory_space=pltpu.VMEM),
        scratch_shapes=[
            pltpu.VMEM((4, rows, columns), b16),
            pltpu.VMEM((4, rows, columns), b16),
            pltpu.VMEM((rows, columns), b16),
            pltpu.VMEM((rows, columns), b16),
            pltpu.VMEM((rows // 2, columns), b16),
            pltpu.VMEM((rows // 2, columns), b16),
            pltpu.SemaphoreType.DMA((10,)),
            pltpu.SemaphoreType.DMA((10,)),
            pltpu.SemaphoreType.DMA((4,)),
        ],
        compiler_params=pltpu.CompilerParams(
            collective_id=number, has_side_effects=True, vmem_limit_bytes=32 << 20
        ),
        cost_estimate=pl.CostEstimate(
            flops=0, bytes_accessed=rows * columns * 128, transcendentals=0
        ),
    )(parts.reshape(8, rows, columns))


def rms_scale(value, gain):
    return value * lax.rsqrt(jnp.mean(value * value, axis=-1, keepdims=True) + epsilon) * gain


def rms_back(value, gain, grad):
    scale = lax.rsqrt(jnp.mean(value * value, axis=-1, keepdims=True) + epsilon)
    unit = value * scale
    inward = grad * gain
    back = scale * (inward - unit * jnp.mean(inward * unit, axis=-1, keepdims=True))
    return back, jnp.sum(grad * unit, axis=0)


def dot(a, b):
    return jnp.dot(a, b, preferred_element_type=f32)


def dot_nt(a, b):
    return lax.dot_general(a, b, NT, preferred_element_type=f32)


def dot_tn(a, b):
    return lax.dot_general(a, b, (((0,), (0,)), ((), ())), preferred_element_type=f32)


def silu_parts(value):
    sigma = jax.nn.sigmoid(value)
    return value * sigma, sigma * (1.0 + value * (1.0 - sigma))


def dense_gates(logits, route_ids):
    experts = logits.shape[1]
    ids = jnp.arange(experts, dtype=jnp.int32)
    named = jnp.any(route_ids[:, :, None] == ids, axis=1)
    top = jnp.max(jnp.where(named, logits, -jnp.inf), axis=1, keepdims=True)
    weight = jnp.where(named, jnp.exp(jnp.where(named, logits - top, 0.0)), 0.0)
    return weight / jnp.sum(weight, axis=1, keepdims=True)


def exchange(value, axis, distance):
    size = lax.axis_size(axis)
    return lax.ppermute(value, axis, [(i, i ^ distance) for i in range(size)])


def total_of(value, axes):
    for axis in axes:
        distance = 1
        while distance < lax.axis_size(axis):
            value = value + exchange(value, axis, distance)
            distance *= 2
    return value


class Heads:
    def __init__(self, planes, plane, out_rows, width):
        self.planes, self.plane, self.width = planes, plane, width
        self.each = H // plane
        self.padded = -(-self.each // 2) * 2
        own = 2 * out_rows
        self.owned = own % width == 0 and planes % 2 == 0 and self.padded == self.each
        self.run = own // width if self.owned else self.each

    def group(self, value, size):
        lead = value.shape[:-1]
        if self.owned:
            value = value.reshape(lead + (2, self.planes // 2, self.plane // 2, self.run * size))
            n = len(lead)
            value = jnp.transpose(value, tuple(range(n)) + (n + 2, n, n + 1, n + 3))
        value = value.reshape(lead + (self.plane, self.each * size))
        pad = (self.padded - self.each) * size
        return jnp.pad(value, [(0, 0)] * (len(lead) + 1) + [(0, pad)]) if pad else value

    def ungroup(self, value, size):
        lead = value.shape[:-2]
        value = value[..., : self.each * size]
        if self.owned:
            value = value.reshape(lead + (self.plane // 2, 2, self.planes // 2, self.run * size))
            n = len(lead)
            value = jnp.transpose(value, tuple(range(n)) + (n + 1, n + 2, n, n + 3))
        return value.reshape(lead + (H * size,))


def body(
    block_input,
    out_grad,
    routes,
    norm_in,
    in_proj,
    conv_weight,
    conv_bias,
    step_bias,
    log_rate,
    skip_gain,
    mixer_gain,
    out_proj,
    norm_mid,
    router,
    shared_gate,
    shared_up,
    shared_down,
    expert_gate,
    expert_up,
    expert_down,
):
    both = ("dp", "expert")
    planes, plane = lax.axis_size("dp"), lax.axis_size("expert")
    at = lax.axis_index("expert")
    core = at % 2
    micro, length, width = block_input.shape
    picks = routes.shape[-1]
    local = expert_gate.shape[0]
    experts = local * plane
    capacity = 3 * length * picks // (2 * experts)
    slots = -(-capacity // 8) * 8
    tokens = micro * length
    shard = in_proj.shape[0]
    out_rows = out_proj.shape[0]
    inner = out_rows * planes * plane
    hr = shared_down.shape[0]
    fs = hr * planes
    ehidden = expert_gate.shape[2]
    gather = lambda v, axes: lax.all_gather(v, axes, axis=0, tiled=True)
    scatter = lambda v, axes: lax.psum_scatter(v, axes, scatter_dimension=0, tiled=True)
    heads = Heads(planes, plane, out_rows, inner // H)
    size = heads.width
    wide = heads.padded * size
    states = conv_weight.shape[1] - inner
    main = 2 * wide + states + LANES

    signal = in_proj[:, inner : 2 * inner]
    maps = in_proj[:, 2 * inner : 2 * inner + states]
    steps = in_proj[:, 2 * inner + states :]
    common = jnp.concatenate([norm_in[:, None], norm_mid[:, None], router], axis=1)
    spare = LANES - heads.padded - common.shape[1]
    repeat = lambda v: jnp.broadcast_to(v[:, None, :], (shard, plane, v.shape[1]))
    split = lambda v: v.reshape(shard, planes, plane, hr).transpose(0, 2, 1, 3).reshape(shard, plane, fs)
    sent = jnp.concatenate(
        [
            heads.group(in_proj[:, :inner], size),
            heads.group(signal, size),
            repeat(maps),
            heads.group(steps, 1),
            repeat(common),
            jnp.zeros((shard, plane, spare), b16),
            split(shared_gate),
            split(shared_up),
        ],
        axis=2,
    ).transpose(1, 0, 2)
    came = lax.all_to_all(sent, "expert", split_axis=0, concat_axis=0, tiled=True)
    proj = gather(came.reshape(plane * shard, -1), "dp")
    in_w = proj[:, :main]
    gate_up = proj[:, main:]
    first = 2 * wide + states + heads.padded
    gain_in = proj[:, first].astype(f32)
    gain_mid = proj[:, first + 1].astype(f32)
    route_proj = proj[:, first + 2 : first + 2 + experts]

    own_routes = jnp.pad(routes.reshape(tokens, picks).astype(b16), ((0, 0), (0, LANES - picks)))
    flat_in = block_input.reshape(tokens, width)
    grad_low = out_grad.reshape(tokens, width)
    seen = plane_gather(jnp.concatenate([flat_in, own_routes], axis=1), 0)
    all_grad = plane_gather(grad_low, 1)
    all_in = seen[:, :width].astype(f32)
    all_routes = seen[:, width : width + picks].astype(jnp.int32)
    count = all_in.shape[0]
    seqs = count // LEN

    out_shard = jnp.concatenate(
        [
            jnp.concatenate([out_proj, mixer_gain[:, None]], axis=1),
            jnp.pad(shared_down, ((0, 0), (0, 1))),
        ],
        axis=0,
    )
    out_shard = jnp.pad(out_shard, ((0, 0), (0, LANES - 1)))
    half = planes // 2
    if heads.owned:
        out_all = gather(out_shard, "dp").reshape(planes, out_rows + hr, -1)
        down_w = out_all[:, out_rows:, :width].reshape(fs, width)
        pieces = out_all[:, :out_rows].reshape(2, half, out_rows, -1)
        low = core == 0
        keep = jnp.where(low, pieces[0], pieces[1])
        other = exchange(jnp.where(low, pieces[1], pieces[0]), "expert", 1)
        out_w = jnp.stack([jnp.where(low, keep, other), jnp.where(low, other, keep)], axis=1)
        out_w = out_w.reshape(wide, -1)
    else:
        down_w = gather(shared_down, "dp")
        out_all = gather(out_shard[:out_rows], both)
        out_w = lax.dynamic_slice_in_dim(out_all, at * heads.each * size, heads.each * size, 0)
        out_w = jnp.pad(out_w, ((0, wide - heads.each * size), (0, 0)))
    gain_mix = out_w[:, width]
    out_w = out_w[:, :width]

    pick_own = lambda v: lax.dynamic_index_in_dim(v, at, v.ndim - 2, keepdims=False)
    lane_pad = lambda v: jnp.pad(v.astype(f32), (0, LANES - v.shape[0])).reshape(1, LANES)
    own_lanes = lambda v: jnp.concatenate(
        [pick_own(heads.group(v[:, :inner], size)), v[:, inner:]], axis=1
    ).astype(f32)
    params = (
        own_lanes(conv_weight),
        own_lanes(conv_bias[None]),
        lane_pad(pick_own(heads.group(step_bias, 1))),
        lane_pad(pick_own(heads.group(log_rate, 1))),
        pick_own(heads.group(jnp.repeat(skip_gain, size), size)).astype(f32).reshape(1, -1),
        gain_mix.astype(f32).reshape(1, -1),
    )

    normed = rms_scale(all_in, gain_in).astype(b16)
    merged = dot(normed, in_w)
    mixed, joined, square = mix_forward(merged, params)
    square = jnp.sum(square, axis=1, keepdims=True)
    square_high = square.astype(b16)
    square_low = (square - square_high.astype(f32)).astype(b16)
    lane = jnp.arange(LANES)[None]
    tail = jnp.where(lane == 2 * at, square_high, jnp.where(lane == 2 * at + 1, square_low, 0))
    summed = plane_scatter(
        jnp.concatenate([dot(mixed, out_w).astype(b16), tail.astype(b16)], axis=1), 2
    )
    scale = lax.rsqrt(jnp.sum(summed[:, width:], axis=1, keepdims=True) / inner + epsilon)
    mixer_out = scale * summed[:, :width]
    start = flat_in.astype(f32)
    grad_out = grad_low.astype(f32)
    middle = start + mixer_out
    routed = rms_scale(middle, gain_mid).astype(b16)
    all_routed = plane_gather(routed, 3)

    mine = at * local + jnp.arange(local, dtype=jnp.int32)
    marks = jnp.any(all_routes[:, :, None] == mine, axis=1).reshape(seqs, LEN, local)
    earlier = jnp.arange(LEN)[:, None] > jnp.arange(LEN)[None, :]
    rank = jnp.einsum(
        "ts,nse->net", earlier.astype(b16), marks.astype(b16), preferred_element_type=f32
    ).astype(jnp.int32)
    places = jnp.arange(slots, dtype=jnp.int32)
    chosen = (rank[:, :, None, :] == places[None, None, :, None]) & (
        marks.transpose(0, 2, 1)[:, :, None, :]
    )
    select = chosen.astype(b16).reshape(seqs, local * slots, LEN)
    gates_all = dense_gates(dot(all_routed, route_proj), all_routes)
    gates_mine = lax.dynamic_slice_in_dim(gates_all, at * local, local, axis=1)
    gates_mine = gates_mine.reshape(seqs, LEN, local).transpose(0, 2, 1)
    slot_gates = jnp.sum(jnp.where(chosen, gates_mine[:, :, None, :], 0.0), axis=-1)

    def spread(rows):
        return jnp.einsum(
            "nrt,ntd->nrd", select, rows.reshape(seqs, LEN, -1), preferred_element_type=f32
        ).reshape(seqs, local, slots, -1)

    rows_in = spread(all_routed).astype(b16)
    rows_grad = spread(all_grad)
    outs, backs, dgates, bank_grads = [], [], [], []
    for e in range(local):
        gu_w = gather(jnp.concatenate([expert_gate[e], expert_up[e]], axis=1), "dp")
        e_down = gather(expert_down[e], "dp")
        x = rows_in[:, e].reshape(seqs * slots, -1)
        g = slot_gates[:, e].reshape(seqs * slots, 1)
        dy = rows_grad[:, e].reshape(seqs * slots, -1)
        pre = dot(x, gu_w)
        soft, slope = silu_parts(pre[:, :ehidden])
        lin = pre[:, ehidden:]
        hid = (soft * lin).astype(b16)
        made = dot(hid, e_down).astype(b16).astype(f32)
        dgates.append(jnp.sum(made * dy, axis=1).reshape(seqs, slots))
        outs.append((made * g).astype(b16).reshape(seqs, slots, -1))
        dmade = (dy * g).astype(b16)
        dhid = dot_nt(dmade, e_down)
        dpre = jnp.concatenate([dhid * lin * slope, dhid * soft], axis=1).astype(b16)
        backs.append(dot_nt(dpre, gu_w).astype(b16).reshape(seqs, slots, -1))
        bank_grads.append(
            (
                scatter(dot_tn(x, dpre).astype(b16), "dp").astype(f32),
                scatter(dot_tn(hid, dmade).astype(b16), "dp").astype(f32),
            )
        )
    combine = lambda parts: jnp.einsum(
        "nrt,nrd->ntd", select, jnp.concatenate(parts, axis=1), preferred_element_type=f32
    ).reshape(count, -1)
    dgate_rows = jnp.sum(
        jnp.where(chosen, jnp.stack(dgates, axis=1)[:, :, :, None], 0.0), axis=2
    ).transpose(0, 2, 1)
    dgate_wide = lax.dynamic_update_slice_in_dim(
        jnp.zeros((count, experts), f32), dgate_rows.reshape(count, local), at * local, axis=1
    )
    high = dgate_wide.astype(b16)
    fine = (dgate_wide - high.astype(f32)).astype(b16)
    fill = jnp.zeros((count, -(2 * experts) % LANES), b16)

    pre = dot(all_routed, gate_up)
    soft, slope = silu_parts(pre[:, :fs])
    lin = pre[:, fs:]
    hid = (soft * lin).astype(b16)
    dhid = dot_nt(all_grad, down_w)
    dpre = jnp.concatenate([dhid * lin * slope, dhid * soft], axis=1).astype(b16)
    shared_out = dot(hid, down_w)
    shared_back = dot_nt(dpre, gate_up)

    payload = [(combine(backs) + shared_back).astype(b16), high, fine, fill]
    back = plane_scatter(jnp.concatenate(payload, axis=1), 4)
    out_sum = plane_scatter((combine(outs) + shared_out).astype(b16), 5)

    gates = dense_gates(dot(routed, route_proj), routes.reshape(tokens, picks))
    dgate = back[:, width : width + experts] + back[:, width + experts : width + 2 * experts]
    dlogits = (gates * (dgate - jnp.sum(gates * dgate, axis=1, keepdims=True))).astype(b16)
    droute = back[:, :width] + dot_nt(dlogits, route_proj)
    dmid_part, mid_gain_grad = rms_back(middle, gain_mid, droute)
    dmid = grad_out + dmid_part

    scaled = (dmid * scale).astype(b16)
    inward = scale * jnp.sum(scaled.astype(f32) * mixer_out, axis=1, keepdims=True) / inner
    inward_high = inward.astype(b16)
    inward_low = (inward - inward_high.astype(f32)).astype(b16)
    tail = jnp.where(lane == 0, inward_high, jnp.where(lane == 1, inward_low, 0)).astype(b16)
    spread_mid = plane_gather(jnp.concatenate([scaled, tail], axis=1), 6)
    all_mid = spread_mid[:, :width]
    all_inward = spread_mid[:, width : width + 1].astype(f32) + spread_mid[
        :, width + 1 : width + 2
    ].astype(f32)
    dmerged, weight_grad, bias_grad, skip_grad, head_grad = mix_backward(
        merged, joined, dot_nt(all_mid, out_w), all_inward, params
    )
    dnormed = plane_scatter(dot_nt(dmerged, in_w).astype(b16), 7)
    dstart, unused = rms_back(start, gain_in, dnormed)

    def owners(grad):
        grad = scatter(grad.astype(b16), "dp")
        grad = grad.reshape(plane, shard, -1)
        return lax.all_to_all(grad, "expert", split_axis=0, concat_axis=0, tiled=True).astype(f32)

    shared_grad = owners(dot_tn(all_routed, dpre))
    unsplit = lambda v: (
        v.reshape(plane, shard, planes, hr).transpose(1, 2, 0, 3).reshape(shard, planes * plane * hr)
    )
    out_w_grad = dot_tn(mixed, all_mid).astype(b16)
    down_grad = dot_tn(hid, all_grad).astype(b16)
    if heads.owned:
        parts = out_w_grad.reshape(half, 2, out_rows, width)
        keep = jnp.where(low, parts[:, 0], parts[:, 1])
        other = exchange(jnp.where(low, parts[:, 1], parts[:, 0]), "expert", 1)
        out_parts = jnp.concatenate([jnp.where(low, keep, other), jnp.where(low, other, keep)])
        rows = jnp.concatenate([out_parts, down_grad.reshape(planes, hr, width)], axis=1)
        rows = scatter(rows.reshape(planes * (out_rows + hr), width), "dp").astype(f32)
        out_w_grad, down_grad = rows[:out_rows], rows[out_rows:]
    else:
        rows = lax.dynamic_update_slice_in_dim(
            jnp.zeros((inner, width), b16), out_w_grad[: heads.each * size], at * heads.each * size, 0
        )
        out_w_grad = scatter(rows, both).astype(f32)
        down_grad = scatter(down_grad, "dp").astype(f32)

    extra = jnp.concatenate(
        [
            jnp.zeros((width, heads.padded + 1), f32),
            mid_gain_grad[:, None],
            dot_tn(routed, dlogits),
            jnp.zeros((width, spare), f32),
        ],
        axis=1,
    )
    in_w_grad = dot_tn(normed, dmerged)
    in_w_grad = jnp.concatenate([in_w_grad[:, :-LANES], in_w_grad[:, -LANES:] + extra], axis=1)
    in_w_grad = owners(in_w_grad)
    by_row = in_w_grad.transpose(1, 0, 2)
    step_part = 2 * wide + states
    in_grad = jnp.concatenate(
        [
            heads.ungroup(by_row[:, :, :wide], size),
            heads.ungroup(by_row[:, :, wide : 2 * wide], size),
            jnp.sum(by_row[:, :, 2 * wide : step_part], axis=1),
            heads.ungroup(by_row[:, :, step_part : step_part + heads.padded], 1),
        ],
        axis=1,
    )
    shared_common = jnp.sum(by_row[:, :, first:], axis=1)
    gain_in_grad = jnp.sum(in_proj.astype(f32) * in_grad, axis=1) / norm_in.astype(f32)
    gain_mix_grad = jnp.sum(out_proj.astype(f32) * out_w_grad, axis=1) / mixer_gain.astype(f32)

    place = lambda v, size: heads.ungroup(
        lax.dynamic_update_slice_in_dim(
            jnp.zeros(v.shape[:-1] + (plane, v.shape[-1]), f32), v[..., None, :], at, v.ndim - 1
        ),
        size,
    )
    taps = jnp.concatenate([weight_grad, bias_grad], axis=0)
    taps = jnp.concatenate([place(taps[:, :wide], size), taps[:, wide:]], axis=1)
    skip_grad = jnp.sum(skip_grad.reshape(heads.padded, size), axis=1)
    head_rows = jnp.concatenate([head_grad[:2, : heads.padded], skip_grad[None]], axis=0)
    head_rows = place(head_rows, 1).reshape(1, -1)
    head_rows = jnp.pad(head_rows, ((0, 0), (0, taps.shape[1] - head_rows.shape[1])))
    small = total_of(jnp.concatenate([taps, head_rows], axis=0), ("dp", "expert"))

    shape = block_input.shape
    return (
        (middle + out_sum).astype(b16).reshape(shape),
        (dmid + dstart).reshape(shape),
        gain_in_grad,
        in_grad,
        small[:4],
        small[4],
        small[5, :H],
        small[5, H : 2 * H],
        small[5, 2 * H : 3 * H],
        gain_mix_grad,
        out_w_grad,
        shared_common[:, 1],
        shared_common[:, 2 : 2 + experts],
        unsplit(shared_grad[:, :, :fs].transpose(0, 1, 2)),
        unsplit(shared_grad[:, :, fs:]),
        down_grad,
        jnp.stack([a[:, :ehidden] for a, _ in bank_grads]),
        jnp.stack([a[:, ehidden:] for a, _ in bank_grads]),
        jnp.stack([b for _, b in bank_grads]),
    )


def solution(mesh):
    both = ("dp", "expert")
    rows, matrix, bank = P(both), P(both, None), P("expert", "dp", None)
    token = P(None, both, None)
    in_specs = (token, token, token, rows, matrix, P(), P(), P(), P(), P(), rows, matrix, rows)
    in_specs = in_specs + (matrix, matrix, matrix, matrix, bank, bank, bank)
    out_specs = (token, token, rows, matrix, P(), P(), P(), P(), P(), rows, matrix, rows)
    out_specs = out_specs + (matrix, matrix, matrix, matrix, bank, bank, bank)
    return jax.shard_map(body, mesh=mesh, in_specs=in_specs, out_specs=out_specs, check_vma=False)
```

```python
from functools import partial

import jax
import jax.numpy as jnp
from jax import lax
from jax.experimental import pallas as pl
from jax.experimental.pallas import tpu as pltpu
from jax.sharding import PartitionSpec as P

H = 48
LEN = 128
LANES = 128
epsilon = 1e-05
f32 = jnp.float32
b16 = jnp.bfloat16
highest = lax.Precision.HIGHEST
NT = (((1,), (1,)), ((), ()))


def sigmoid(value):
    return 0.5 * jnp.tanh(0.5 * value) + 0.5


def grids():
    row = lax.broadcasted_iota(jnp.int32, (LEN, LANES), 0)
    lane = lax.broadcasted_iota(jnp.int32, (LEN, LANES), 1)
    return row, lane


def shifted(signal, row):
    return [signal] + [jnp.where(row >= k, pltpu.roll(signal, k, 0), 0.0) for k in (1, 2, 3)]


def convolved(parts, weight_ref, bias_ref, block):
    weight = weight_ref[:, block]
    total = bias_ref[:, block] + weight[3:4] * parts[0]
    for k in (1, 2, 3):
        total = total + weight[3 - k : 4 - k] * parts[k]
    return total


def pick(value, lane):
    low = lane < LANES // 2
    return jnp.concatenate([jnp.where(low, value, 0.0), jnp.where(low, 0.0, value)], axis=0)


def step_terms(merged_ref, step_ref, rate_ref, tail):
    raw = merged_ref[:, tail] + step_ref[...]
    step = jnp.maximum(raw, 0.0) + jnp.log1p(jnp.exp(-jnp.abs(raw)))
    decay = -jnp.exp(rate_ref[...]) * step
    row, lane = grids()
    cumul = jnp.dot(
        (row >= lane).astype(f32), decay, precision=highest, preferred_element_type=f32
    )
    return raw, step, decay, cumul


def forward_kernel(
    pairs,
    merged_ref,
    weight_ref,
    bias_ref,
    step_ref,
    rate_ref,
    skip_ref,
    gain_ref,
    mixed_ref,
    joined_ref,
    square_ref,
    cross_ref,
):
    row, lane = grids()
    tail = pl.ds((2 * pairs + 2) * LANES, LANES)
    raw, step, decay, cumul = step_terms(merged_ref, step_ref, rate_ref, tail)
    cross_ref[...] = cumul.T
    maps = []
    for at in (0, 1):
        signal = merged_ref[:, pl.ds((2 * pairs + at) * LANES, LANES)]
        block = pl.ds((pairs + at) * LANES, LANES)
        conv = convolved(shifted(signal, row), weight_ref, bias_ref, block)
        maps.append((conv * sigmoid(conv)).astype(b16))
    inner = lax.dot_general(maps[1], maps[0], NT, preferred_element_type=f32)
    square = jnp.zeros((LEN, LANES), f32)
    for pair in range(pairs):
        block = pl.ds(pair * LANES, LANES)
        signal = merged_ref[:, pl.ds((pairs + pair) * LANES, LANES)]
        conv = convolved(shifted(signal, row), weight_ref, bias_ref, block)
        values = conv * sigmoid(conv)
        steps, parts = [], []
        for head in (2 * pair, 2 * pair + 1):
            steps.append(step[:, head : head + 1])
            spread = cumul[:, head : head + 1] - cross_ref[head : head + 1, :]
            parts.append(inner * jnp.exp(jnp.where(row >= lane, spread, -1e30)))
        scaled = values * jnp.where(lane < LANES // 2, steps[0], steps[1])
        scanned = jnp.dot(
            jnp.concatenate(parts, axis=1).astype(b16),
            pick(scaled, lane).astype(b16),
            preferred_element_type=f32,
        )
        joined = scanned + skip_ref[:, block] * values
        joined_ref[:, block] = joined
        gate = merged_ref[:, block]
        gated = joined * (gate * sigmoid(gate))
        mixed_ref[:, block] = (gated * gain_ref[:, block]).astype(b16)
        square = square + gated * gated
    square_ref[...] = square


def backward_kernel(
    pairs,
    merged_ref,
    joined_ref,
    grad_ref,
    inward_ref,
    weight_ref,
    bias_ref,
    step_ref,
    rate_ref,
    skip_ref,
    gain_ref,
    out_ref,
    weight_out,
    bias_out,
    skip_out,
    head_out,
    cross_ref,
):
    row, lane = grids()
    low = lane < LANES // 2

    @pl.when(pl.program_id(0) == 0)
    def _():
        weight_out[...] = jnp.zeros_like(weight_out)
        bias_out[...] = jnp.zeros_like(bias_out)
        skip_out[...] = jnp.zeros_like(skip_out)
        head_out[...] = jnp.zeros_like(head_out)

    inward = inward_ref[...]
    tail = pl.ds((2 * pairs + 2) * LANES, LANES)
    raw, step, decay, cumul = step_terms(merged_ref, step_ref, rate_ref, tail)
    cross_ref[...] = cumul.T
    convs, slopes, shifts, maps = [], [], [], []
    for at in (0, 1):
        signal = merged_ref[:, pl.ds((2 * pairs + at) * LANES, LANES)]
        parts = shifted(signal, row)
        conv = convolved(parts, weight_ref, bias_ref, pl.ds((pairs + at) * LANES, LANES))
        sigma = sigmoid(conv)
        shifts.append(parts)
        slopes.append(sigma * (1.0 + conv * (1.0 - sigma)))
        maps.append((conv * sigma).astype(b16))
    flipped = lax.dot_general(maps[0], maps[1], NT, preferred_element_type=f32)
    dinner = jnp.zeros((LEN, LEN), f32)
    dstep = jnp.zeros((LEN, LANES), f32)
    dcum = jnp.zeros((LEN, LANES), f32)

    def back_conv(grad, parts, block, out_block):
        bias_out[:, block] += jnp.sum(grad, axis=0, keepdims=True)
        weight = weight_ref[:, block]
        total = weight[3:4] * grad
        taps = [jnp.sum(grad * parts[3 - k], axis=0, keepdims=True) for k in range(4)]
        weight_out[:, block] += jnp.concatenate(taps, axis=0)
        for k in (1, 2, 3):
            later = jnp.where(row < LEN - k, pltpu.roll(grad, LEN - k, 0), 0.0)
            total = total + weight[3 - k : 4 - k] * later
        out_ref[:, out_block] = total.astype(b16)

    for pair in range(pairs):
        block = pl.ds(pair * LANES, LANES)
        other = pl.ds((pairs + pair) * LANES, LANES)
        gate = merged_ref[:, block]
        joined = joined_ref[:, block]
        sigma = sigmoid(gate)
        soft = gate * sigma
        dgated = grad_ref[:, block] * gain_ref[:, block] - joined * soft * inward
        djoined = dgated * soft
        out_ref[:, block] = (dgated * joined * (sigma + soft * (1.0 - sigma))).astype(b16)

        parts = shifted(merged_ref[:, other], row)
        conv = convolved(parts, weight_ref, bias_ref, block)
        csig = sigmoid(conv)
        values = conv * csig
        skip = skip_ref[:, block]
        skip_out[:, block] += jnp.sum(djoined * values, axis=0, keepdims=True)
        scanned = joined - skip * values
        steps, blends, spreads = [], [], []
        for head in (2 * pair, 2 * pair + 1):
            steps.append(step[:, head : head + 1])
            spread = cumul[:, head : head + 1] - cross_ref[head : head + 1, :]
            spreads.append(jnp.exp(jnp.where(row >= lane, spread, -1e30)))
            blends.append(flipped * jnp.exp(jnp.where(row <= lane, -spread, -1e30)))
        widened = jnp.where(low, steps[0], steps[1])
        scaled = (values * widened).astype(b16)
        dlow = djoined.astype(b16)
        both = pick(djoined, lane).astype(b16)
        dweights = lax.dot_general(both, scaled, NT, preferred_element_type=f32)
        dinner = dinner + dweights[:LEN] * spreads[0] + dweights[LEN:] * spreads[1]
        dscaled = jnp.dot(
            jnp.concatenate(blends, axis=1).astype(b16), both, preferred_element_type=f32
        )
        dvalues = skip * djoined + dscaled * widened
        first = dscaled * values
        second = dlow.astype(f32) * scanned - scaled.astype(f32) * dscaled
        for at in (0, 1):
            mine = low if at == 0 else jnp.logical_not(low)
            here = lane == 2 * pair + at
            total = jnp.sum(jnp.where(mine, first, 0.0), axis=1, keepdims=True)
            dstep = jnp.where(here, total, dstep)
            total = jnp.sum(jnp.where(mine, second, 0.0), axis=1, keepdims=True)
            dcum = jnp.where(here, total, dcum)
        back_conv(dvalues * (csig * (1.0 + conv * (1.0 - csig))), parts, block, other)
    dmaps = (
        jnp.dot(dinner.T.astype(b16), maps[1], preferred_element_type=f32),
        jnp.dot(dinner.astype(b16), maps[0], preferred_element_type=f32),
    )
    for at in (0, 1):
        back_conv(
            dmaps[at] * slopes[at],
            shifts[at],
            pl.ds((pairs + at) * LANES, LANES),
            pl.ds((2 * pairs + at) * LANES, LANES),
        )
    ddecay = jnp.dot(
        (row <= lane).astype(f32), dcum, precision=highest, preferred_element_type=f32
    )
    dstep = dstep - ddecay * jnp.exp(rate_ref[...])
    draw = jnp.where(lane < 2 * pairs, dstep * sigmoid(raw), 0.0)
    out_ref[:, tail] = draw.astype(b16)
    head_out[0:1, :] += jnp.sum(draw, axis=0, keepdims=True)
    head_out[1:2, :] += jnp.sum(ddecay * decay, axis=0, keepdims=True)


def rows_of(columns):
    return pl.BlockSpec((LEN, columns), lambda s: (s, 0))


def fixed(rows, columns):
    return pl.BlockSpec((rows, columns), lambda s: (0, 0))


def mix_forward(merged, params):
    tokens, columns = merged.shape
    width = params[-1].shape[1]
    return pl.pallas_call(
        partial(forward_kernel, width // LANES),
        grid=(tokens // LEN,),
        in_specs=[rows_of(columns)] + [fixed(*p.shape) for p in params],
        out_specs=[rows_of(width), rows_of(width), rows_of(LANES)],
        out_shape=[
            jax.ShapeDtypeStruct((tokens, width), b16),
            jax.ShapeDtypeStruct((tokens, width), f32),
            jax.ShapeDtypeStruct((tokens, LANES), f32),
        ],
        scratch_shapes=[pltpu.VMEM((LANES, LEN), f32)],
        compiler_params=pltpu.CompilerParams(vmem_limit_bytes=32 << 20),
        cost_estimate=pl.CostEstimate(flops=0, bytes_accessed=1024, transcendentals=0),
    )(merged, *params)


def mix_backward(merged, joined, grad, inward, params):
    tokens, columns = merged.shape
    width = params[-1].shape[1]
    conv = params[0].shape[1]
    return pl.pallas_call(
        partial(backward_kernel, width // LANES),
        grid=(tokens // LEN,),
        in_specs=[rows_of(columns), rows_of(width), rows_of(width), rows_of(1)]
        + [fixed(*p.shape) for p in params],
        out_specs=[
            rows_of(columns),
            fixed(4, conv),
            fixed(1, conv),
            fixed(1, width),
            fixed(8, LANES),
        ],
        out_shape=[
            jax.ShapeDtypeStruct((tokens, columns), b16),
            jax.ShapeDtypeStruct((4, conv), f32),
            jax.ShapeDtypeStruct((1, conv), f32),
            jax.ShapeDtypeStruct((1, width), f32),
            jax.ShapeDtypeStruct((8, LANES), f32),
        ],
        scratch_shapes=[pltpu.VMEM((LANES, LEN), f32)],
        compiler_params=pltpu.CompilerParams(vmem_limit_bytes=32 << 20),
        cost_estimate=pl.CostEstimate(flops=0, bytes_accessed=1024, transcendentals=0),
    )(merged, joined, grad, inward, *params)


MESH = pl.DeviceIdType.MESH


def neighbours(me):
    core, column, line = me % 2, (me // 2) % 2, me // 4
    return 1 - 2 * core, 2 - 4 * column, 4 - 8 * line


def other_plane(me):
    place = lax.axis_index("dp")
    return {"dp": place + 1 - 2 * (place % 2), "expert": me}


def greet(peers):
    barrier = pltpu.get_barrier_semaphore()
    for peer in peers:
        pl.semaphore_signal(barrier, inc=1, device_id=peer, device_id_type=MESH)
    pl.semaphore_wait(barrier, len(peers))


def far_plane(me):
    place = lax.axis_index("dp")
    return {"dp": place + 2 - 4 * (place // 2), "expert": me}


def peers_of(me, across, along=0):
    core, column, line = neighbours(me)
    peers = [{"expert": me + core}, {"expert": me + column}, {"expert": me + line}]
    peers = peers + ([other_plane(me)] if across else [])
    return peers + ([far_plane(me)] if along else [])


def begin_swaps(refs, swaps, first, send_sem, recv_sem, peer):
    found = []
    for i in range(swaps):
        found.append(remote(send_sem, recv_sem, first + i, refs[i], refs[swaps + i], peer[0]))
        found[-1].start()
    return found


def remote(send_sem, recv_sem, at, src, dst, peer):
    return pltpu.make_async_remote_copy(
        src_ref=src,
        dst_ref=dst,
        send_sem=send_sem.at[at],
        recv_sem=recv_sem.at[at],
        device_id=peer,
        device_id_type=MESH,
    )


def gather_kernel(sets, count, swaps, lines, waits, *refs):
    total = count + swaps + lines
    owns, give, block = refs[:count], refs[count : count + swaps], refs[count + swaps : total]
    refs = refs[total + waits :]
    outs, take, line_out = refs[:count], refs[count : count + swaps], refs[count + swaps : total]
    send_sem, recv_sem, copy_sem = refs[total:]
    me = lax.axis_index("expert")
    core, column, line = neighbours(me)
    half = owns[0].shape[0] // 2
    top, bottom = pl.ds(0, half), pl.ds(half, half)
    peers = peers_of(me, max(sets) == 2 or swaps or lines, lines)
    greet(peers)
    copy = partial(remote, send_sem, recv_sem)
    arrays = range(count)
    place = lax.axis_index("dp")
    distant = place + 2 - 4 * (place // 2)
    along = []
    for i in range(lines):
        base = 17 * count + swaps + 3 * i
        own, out = block[i], line_out[i]
        along.append(
            (
                pltpu.make_async_copy(own, out.at[place], copy_sem.at[count + i]),
                copy(base, own, out.at[place], peers[4]),
                copy(base + 1, own, out.at[place], peers[3]),
                copy(base + 2, out.at[distant], out.at[distant], peers[3]),
            )
        )
    steps = []
    here, across = [], []
    for i in arrays:
        here.append(pltpu.make_async_copy(owns[i], outs[i].at[me], copy_sem.at[i]))
        if sets[i] == 2:
            across.append(copy(17 * i + 16, owns[i], outs[i].at[8 + me], peers[3]))
    for g in range(2):
        for i in arrays:
            if sets[i] <= g:
                continue
            out = lambda at: outs[i].at[8 * g + at]
            own = owns[i] if g == 0 else out(me)
            at_x, at_y, at_d = out(me + column), out(me + line), out(me + column + line)
            base = 17 * i + 8 * g
            steps.append(
                (
                    copy(base, own, out(me), peers[1]),
                    copy(base + 1, own, out(me), peers[2]),
                    copy(base + 2, own, out(me), peers[0]),
                    copy(base + 3, at_x.at[top], at_x.at[top], peers[2]),
                    copy(base + 4, at_y.at[bottom], at_y.at[bottom], peers[1]),
                    copy(base + 5, at_x, at_x, peers[0]),
                    copy(base + 6, at_y, at_y, peers[0]),
                    copy(base + 7, at_d, at_d, peers[0]),
                )
            )

    def begin(group):
        for to_x, to_y, to_core, *unused in group:
            to_x.start()
            to_y.start()
            to_core.start()

    def relay(group):
        for to_x, to_y, to_core, x_relay, y_relay, x_core, y_core, d_core in group:
            to_x.wait_recv()
            x_relay.start()
            x_core.start()
            to_y.wait_recv()
            y_relay.start()
            y_core.start()

    def close(group):
        for to_x, to_y, to_core, x_relay, y_relay, x_core, y_core, d_core in group:
            x_relay.wait_recv()
            y_relay.wait_recv()
            d_core.start()

    first, second = steps[:count], steps[count:]
    for here_block, to_far, to_near, relayed in along:
        to_far.start()
        to_near.start()
        here_block.start()
    for copied in across:
        copied.start()
    begin(first)
    swapped = begin_swaps(give + take, swaps, 17 * count, send_sem, recv_sem, peers[3:4])
    for here_block, to_far, to_near, relayed in along:
        to_far.wait_recv()
        relayed.start()
    for copied in here:
        copied.start()
    for copied in across:
        copied.wait_recv()
    begin(second)
    relay(first)
    close(first)
    relay(second)
    close(second)
    for copied in here:
        copied.wait()
    for copied in across:
        copied.wait_send()
    for copied in swapped:
        copied.wait()
    for here_block, to_far, to_near, relayed in along:
        here_block.wait()
        to_near.wait_recv()
        relayed.wait_recv()
        for copied in (to_far, to_near, relayed):
            copied.wait_send()
    for group in steps:
        for at in (2, 5, 6, 7):
            group[at].wait_recv()
        for sent in group:
            sent.wait_send()


def plane_gather(number, *owns, sets=1, swaps=(), lines=(), after=()):
    if lax.axis_size("expert") != 8 or (lines and lax.axis_size("dp") != 4):
        return [lax.all_gather(own, "expert", axis=0, tiled=True) for own in owns] + [
            lax.all_gather(line, "dp", axis=0, tiled=True) for line in lines
        ]
    count = len(owns)
    sets = (sets,) * count if isinstance(sets, int) else sets
    total = count + len(swaps) + len(lines)
    anywhere = pl.BlockSpec(memory_space=pl.ANY)
    outs = pl.pallas_call(
        partial(gather_kernel, sets, count, len(swaps), len(lines), len(after)),
        out_shape=[
            jax.ShapeDtypeStruct((8 * n,) + own.shape, own.dtype) for n, own in zip(sets, owns)
        ]
        + [jax.ShapeDtypeStruct(v.shape, v.dtype) for v in swaps]
        + [jax.ShapeDtypeStruct((4,) + v.shape, v.dtype) for v in lines],
        in_specs=[anywhere] * (total + len(after)),
        out_specs=[anywhere] * total,
        scratch_shapes=[
            pltpu.SemaphoreType.DMA((17 * count + len(swaps) + 3 * len(lines),)),
            pltpu.SemaphoreType.DMA((17 * count + len(swaps) + 3 * len(lines),)),
            pltpu.SemaphoreType.DMA((count + len(lines),)),
        ],
        compiler_params=pltpu.CompilerParams(collective_id=number, has_side_effects=True),
        cost_estimate=pl.CostEstimate(flops=0, bytes_accessed=1024, transcendentals=0),
    )(*owns, *swaps, *lines, *after)
    gathered = [out.reshape(-1, out.shape[2]) for out in outs[:count]]
    spread = [out.reshape(4 * out.shape[1], out.shape[2]) for out in outs[total - len(lines) :]]
    return gathered + list(outs[count : total - len(lines)]) + spread


def scatter_kernel(sets, count, extra, gathers, lines, waits, *refs):
    parts, give = refs[:count], refs[count : count + extra]
    refs = refs[count + extra :]
    owns, blocks = refs[:gathers], refs[gathers : gathers + lines]
    refs = refs[gathers + lines + waits :]
    outs, take = refs[:count], refs[count : count + extra]
    refs = refs[count + extra :]
    gathered, line_outs = refs[:gathers], refs[gathers : gathers + lines]
    refs = refs[gathers + lines :]
    per = 6 * sets + (3 if sets == 2 else 0)
    held = [refs[per * i : per * (i + 1)] for i in range(count)]
    send_sem, recv_sem, copy_sem = refs[per * count :]
    me = lax.axis_index("expert")
    core, column, line = neighbours(me)
    rows = outs[0].shape[0]
    half = rows // 2
    top, bottom = pl.ds(0, half), pl.ds(half, half)
    peers = peers_of(me, sets == 2 or extra or lines, lines)
    greet(peers)
    copy = partial(remote, send_sem, recv_sem)
    arrays = range(count)
    chips = (me + column + line, me + column, me + line, me)
    order = range(sets - 1, -1, -1)
    keep = lambda g, i, at: held[i][6 * g + at]
    total_ref = lambda g, i: outs[i] if g == 0 else held[i][12]
    swaps, loads = {}, {}
    for g in order:
        for k in range(4):
            for i in arrays:
                base = 21 * i + 10 * g + k
                swaps[g, i, k] = copy(
                    base, parts[i].at[8 * g + chips[k] + core], keep(g, i, 1).at[k], peers[0]
                )
                loads[g, i, k] = pltpu.make_async_copy(
                    parts[i].at[8 * g + chips[k]],
                    keep(g, i, 0).at[k],
                    copy_sem.at[8 * i + 4 * g + k],
                )
                swaps[g, i, k].start()
                loads[g, i, k].start()

    swapped = begin_swaps(give + take, extra, 21 * count, send_sem, recv_sem, peers[3:4])
    base = 21 * count + extra
    place = lax.axis_index("dp")
    distant = place + 2 - 4 * (place // 2)
    here, small, along = [], [], []
    for i in range(gathers):
        own, out = owns[i], lambda at: gathered[i].at[at]
        at_x, at_y, at_d = out(me + column), out(me + line), out(me + column + line)
        low, high = pl.ds(0, own.shape[0] // 2), pl.ds(own.shape[0] // 2, own.shape[0] // 2)
        here.append(pltpu.make_async_copy(own, out(me), copy_sem.at[8 * count + i]))
        small.append(
            (
                copy(base, own, out(me), peers[1]),
                copy(base + 1, own, out(me), peers[2]),
                copy(base + 2, own, out(me), peers[0]),
                copy(base + 3, at_x.at[low], at_x.at[low], peers[2]),
                copy(base + 4, at_y.at[high], at_y.at[high], peers[1]),
                copy(base + 5, at_x, at_x, peers[0]),
                copy(base + 6, at_y, at_y, peers[0]),
                copy(base + 7, at_d, at_d, peers[0]),
            )
        )
        base += 8
        for begun in [here[-1]] + list(small[-1][:3]):
            begun.start()
    for i in range(lines):
        own, out = blocks[i], line_outs[i]
        here.append(pltpu.make_async_copy(own, out.at[place], copy_sem.at[8 * count + gathers + i]))
        along.append(
            (
                copy(base, own, out.at[place], peers[4]),
                copy(base + 1, own, out.at[place], peers[3]),
                copy(base + 2, out.at[distant], out.at[distant], peers[3]),
            )
        )
        base += 3
        for begun in [here[-1]] + list(along[-1][:2]):
            begun.start()

    def each(first, amount, step):
        def body(at, carry):
            step(pl.ds(pl.multiple_of(first + at * 16, 16), 16))
            return carry

        lax.fori_loop(0, amount // 16, body, 0)

    def pair_sum(g, k):
        for i in arrays:
            loads[g, i, k].wait()
            swaps[g, i, k].wait_recv()

        def step(block):
            for i in arrays:
                mine, theirs = keep(g, i, 0), keep(g, i, 1)
                total = mine[k, block].astype(f32) + theirs[k, block].astype(f32)
                if k == 3:
                    total_ref(g, i)[block, :] = total
                else:
                    mine[k, block] = total.astype(b16)

        each(0, rows, step)

    sent = []

    def sends(g, at, k, area, into, peer):
        found = []
        for i in arrays:
            target = keep(g, i, into)
            target = target if into > 3 else target.at[area]
            source = keep(g, i, 0).at[k, area]
            found.append(copy(21 * i + 10 * g + at, source, target, peer))
            found[-1].start()
        sent.extend(found)
        return found

    legs = {}
    for g in order:
        pair_sum(g, 0)
        d_x = sends(g, 4, 0, top, 4, peers[1])
        d_y = sends(g, 5, 0, bottom, 5, peers[2])
        pair_sum(g, 1)
        x_top = sends(g, 6, 1, top, 2, peers[1])
        pair_sum(g, 2)
        y_bottom = sends(g, 7, 2, bottom, 3, peers[2])
        pair_sum(g, 3)
        legs[g] = [d_x, d_y, x_top, y_bottom]

    for to_x, to_y, to_core, x_relay, y_relay, x_core, y_core, d_core in small:
        to_x.wait_recv()
        x_relay.start()
        x_core.start()
        to_y.wait_recv()
        y_relay.start()
        y_core.start()
    for to_far, to_near, relayed in along:
        to_far.wait_recv()
        relayed.start()

    for g in order:
        d_x, d_y, x_top, y_bottom = legs[g]
        for i in arrays:
            d_x[i].wait_recv()

        def add_y(block):
            for i in arrays:
                mine, extra = keep(g, i, 0), keep(g, i, 4)
                mine[2, block] = (
                    mine[2, block].astype(f32) + extra[block, :].astype(f32)
                ).astype(b16)

        each(0, half, add_y)
        y_top = sends(g, 8, 2, top, 3, peers[2])
        for i in arrays:
            d_y[i].wait_recv()

        def add_x(block):
            low = pl.ds(pl.multiple_of(block.start - half, 16), 16)
            for i in arrays:
                mine, extra = keep(g, i, 0), keep(g, i, 5)
                mine[1, block] = (
                    mine[1, block].astype(f32) + extra[low, :].astype(f32)
                ).astype(b16)

        each(half, half, add_x)
        x_bottom = sends(g, 9, 1, bottom, 2, peers[1])
        legs[g] = [x_top, y_bottom, y_top, x_bottom]

    for to_x, to_y, to_core, x_relay, y_relay, x_core, y_core, d_core in small:
        x_relay.wait_recv()
        y_relay.wait_recv()
        d_core.start()
    across = []
    for g in order:
        for i in arrays:
            for came in legs[g]:
                came[i].wait_recv()

        def finish(block):
            for i in arrays:
                total = (
                    total_ref(g, i)[block, :]
                    + keep(g, i, 2)[block, :].astype(f32)
                    + keep(g, i, 3)[block, :].astype(f32)
                )
                if g == 0:
                    outs[i][block, :] = total
                else:
                    held[i][13][block, :] = total.astype(b16)

        each(0, rows, finish)
        if g == 1:
            for i in arrays:
                across.append(copy(21 * i + 20, held[i][13], held[i][14], peers[3]))
                across[-1].start()
    if sets == 2:
        for i in arrays:
            across[i].wait_recv()

        def add_z(block):
            for i in arrays:
                outs[i][block, :] = outs[i][block, :] + held[i][14][block, :].astype(f32)

        each(0, rows, add_z)
    for done in list(swaps.values()) + sent + across:
        done.wait_send()
    for copied in swapped + here:
        copied.wait()
    for group in small:
        for at in (2, 5, 6, 7):
            group[at].wait_recv()
        for copied in group:
            copied.wait_send()
    for to_far, to_near, relayed in along:
        to_near.wait_recv()
        relayed.wait_recv()
        for copied in (to_far, to_near, relayed):
            copied.wait_send()


def plane_scatter(number, *parts, sets=1, swaps=(), gathers=(), lines=(), after=()):
    if lax.axis_size("expert") != 8:
        return [
            lax.psum_scatter(part, "expert", scatter_dimension=0, tiled=True).astype(f32)
            for part in parts
        ] + [lax.all_gather(v, "expert", axis=0) for v in gathers] + [
            lax.all_gather(v, "dp", axis=0) for v in lines
        ]
    count = len(parts)
    others = list(swaps) + list(gathers) + list(lines) + list(after)
    moved = len(others) - len(after)
    sems = 21 * count + len(swaps) + 8 * len(gathers) + 3 * len(lines)
    rows = parts[0].shape[0] // (8 * sets)
    scratch = []
    for part in parts:
        columns = part.shape[1]
        for g in range(sets):
            scratch += [pltpu.VMEM((4, rows, columns), b16)] * 2
            scratch += [pltpu.VMEM((rows, columns), b16)] * 2
            scratch += [pltpu.VMEM((rows // 2, columns), b16)] * 2
        if sets == 2:
            scratch += [pltpu.VMEM((rows, columns), f32)]
            scratch += [pltpu.VMEM((rows, columns), b16)] * 2
    return pl.pallas_call(
        partial(
            scatter_kernel, sets, count, len(swaps), len(gathers), len(lines), len(after)
        ),
        out_shape=[jax.ShapeDtypeStruct((rows, part.shape[1]), f32) for part in parts]
        + [jax.ShapeDtypeStruct(v.shape, v.dtype) for v in swaps]
        + [jax.ShapeDtypeStruct((8,) + v.shape, v.dtype) for v in gathers]
        + [jax.ShapeDtypeStruct((4,) + v.shape, v.dtype) for v in lines],
        in_specs=[pl.BlockSpec(memory_space=pl.ANY)] * (count + len(others)),
        out_specs=[pl.BlockSpec(memory_space=pltpu.VMEM)] * count
        + [pl.BlockSpec(memory_space=pl.ANY)] * moved,
        scratch_shapes=scratch
        + [
            pltpu.SemaphoreType.DMA((sems,)),
            pltpu.SemaphoreType.DMA((sems,)),
            pltpu.SemaphoreType.DMA((8 * count + len(gathers) + len(lines),)),
        ],
        compiler_params=pltpu.CompilerParams(
            collective_id=number, has_side_effects=True, vmem_limit_bytes=(16 + 24 * sets) << 20
        ),
        cost_estimate=pl.CostEstimate(flops=0, bytes_accessed=1024, transcendentals=0),
    )(*[part.reshape(8 * sets, rows, part.shape[1]) for part in parts], *others)


def rms_scale(value, gain):
    return value * lax.rsqrt(jnp.mean(value * value, axis=-1, keepdims=True) + epsilon) * gain


def rms_back(value, gain, grad):
    scale = lax.rsqrt(jnp.mean(value * value, axis=-1, keepdims=True) + epsilon)
    unit = value * scale
    inward = grad * gain
    back = scale * (inward - unit * jnp.mean(inward * unit, axis=-1, keepdims=True))
    return back, jnp.sum(grad * unit, axis=0)


def dot(a, b):
    return jnp.dot(a, b, preferred_element_type=f32)


def dot_nt(a, b):
    return lax.dot_general(a, b, NT, preferred_element_type=f32)


def dot_tn(a, b):
    return lax.dot_general(a, b, (((0,), (0,)), ((), ())), preferred_element_type=f32)


def silu_parts(value):
    sigma = jax.nn.sigmoid(value)
    return value * sigma, sigma * (1.0 + value * (1.0 - sigma))


def dense_gates(logits, route_ids):
    experts = logits.shape[1]
    ids = jnp.arange(experts, dtype=jnp.int32)
    named = jnp.any(route_ids[:, :, None] == ids, axis=1)
    top = jnp.max(jnp.where(named, logits, -jnp.inf), axis=1, keepdims=True)
    weight = jnp.where(named, jnp.exp(jnp.where(named, logits - top, 0.0)), 0.0)
    return weight / jnp.sum(weight, axis=1, keepdims=True)


def tie(*values):
    return lax.optimization_barrier(values)


def exchange(value, axis, distance):
    size = lax.axis_size(axis)
    return lax.ppermute(value, axis, [(i, i ^ distance) for i in range(size)])


def total_of(value, axes):
    for axis in axes:
        distance = 1
        while distance < lax.axis_size(axis):
            value = value + exchange(value, axis, distance)
            distance *= 2
    return value


def merge_kernel(near, parts, select_ref, *refs):
    rows_refs, (small_ref, weight_ref), out_ref = refs[:parts], refs[parts : parts + 2], refs[-1]
    slots = select_ref.shape[1] // parts
    total = None
    for k in range(parts):
        term = lax.dot_general(
            select_ref[0, k * slots : (k + 1) * slots, :],
            rows_refs[k][0],
            (((0,), (0,)), ((), ())),
            preferred_element_type=f32,
        )
        total = term if total is None else total + term
    first = pl.program_id(0) < near

    @pl.when(first)
    def _():
        out_ref[...] = (total + dot(small_ref[...], weight_ref[...])).astype(b16)

    @pl.when(jnp.logical_not(first))
    def _():
        out_ref[...] = total.astype(b16)


def merge(select, parts, small, weight, after=()):
    seqs, slots, unused = select.shape
    slots = slots // len(parts)
    width = weight.shape[1]
    near = small.shape[0] // LEN
    return pl.pallas_call(
        partial(merge_kernel, near, len(parts)),
        grid=(seqs,),
        in_specs=[pl.BlockSpec((1,) + select.shape[1:], lambda s: (s, 0, 0))]
        + [pl.BlockSpec((1, slots, width), lambda s: (s, 0, 0))] * len(parts)
        + [
            pl.BlockSpec((LEN, small.shape[1]), lambda s: (jnp.minimum(s, near - 1), 0)),
            fixed(*weight.shape),
        ]
        + [pl.BlockSpec(memory_space=pl.ANY)] * len(after),
        out_specs=rows_of(width),
        out_shape=jax.ShapeDtypeStruct((seqs * LEN, width), b16),
        compiler_params=pltpu.CompilerParams(vmem_limit_bytes=32 << 20),
        cost_estimate=pl.CostEstimate(flops=0, bytes_accessed=1024, transcendentals=0),
    )(select, *[v.reshape(seqs, slots, width) for v in parts], small, weight, *after)


def spread_kernel(parts, select_ref, rows_ref, *out_refs):
    slots = select_ref.shape[1] // parts
    rows = dot(select_ref[0], rows_ref[...]).astype(b16)
    for k in range(parts):
        out_refs[k][0] = rows[k * slots : (k + 1) * slots]


def spread(select, rows, parts):
    seqs, slots, unused = select.shape
    slots = slots // parts
    width = rows.shape[1]
    outs = pl.pallas_call(
        partial(spread_kernel, parts),
        grid=(seqs,),
        in_specs=[
            pl.BlockSpec((1,) + select.shape[1:], lambda s: (s, 0, 0)),
            rows_of(width),
        ],
        out_specs=[pl.BlockSpec((1, slots, width), lambda s: (s, 0, 0))] * parts,
        out_shape=[jax.ShapeDtypeStruct((seqs, slots, width), b16)] * parts,
        compiler_params=pltpu.CompilerParams(vmem_limit_bytes=32 << 20),
        cost_estimate=pl.CostEstimate(flops=0, bytes_accessed=1024, transcendentals=0),
    )(select, rows)
    return [v.reshape(seqs * slots, width) for v in outs]


def bank_kernel(parity_ref, gate_ref, up_ref, down_ref, out_ref):
    columns = gate_ref.shape[2]
    rows = down_ref.shape[1]
    out_ref[0, 0, :, :columns] = gate_ref[0]
    out_ref[0, 0, :, columns : 2 * columns] = up_ref[0]
    for k in range(3):
        out_ref[0, 0, k * rows : (k + 1) * rows, 2 * columns :] = down_ref[
            0, :, k * columns : (k + 1) * columns
        ]


def bank_rows(parity, gate, up, down):
    local, rows, columns = gate.shape
    half = local // 2
    which = lambda side, e, p: ((p[0] + side) % 2 * half + e, 0, 0)
    block = lambda v: pl.BlockSpec((1,) + v.shape[1:], which)
    return pl.pallas_call(
        bank_kernel,
        grid_spec=pltpu.PrefetchScalarGridSpec(
            num_scalar_prefetch=1,
            grid=(2, half),
            in_specs=[block(gate), block(up), block(down)],
            out_specs=pl.BlockSpec(
                (1, 1, rows, 3 * columns), lambda side, e, p: (side, e, 0, 0)
            ),
        ),
        out_shape=jax.ShapeDtypeStruct((2, half, rows, 3 * columns), b16),
        cost_estimate=pl.CostEstimate(flops=0, bytes_accessed=1024, transcendentals=0),
    )(parity.reshape(1), gate, up, down)


class Heads:
    def __init__(self, planes, plane, out_rows, width):
        self.planes, self.plane, self.width = planes, plane, width
        self.each = H // plane
        self.padded = -(-self.each // 2) * 2
        own = 2 * out_rows
        self.owned = own % width == 0 and planes % 2 == 0 and self.padded == self.each
        self.run = own // width if self.owned else self.each

    def group(self, value, size):
        lead = value.shape[:-1]
        if self.owned:
            value = value.reshape(lead + (2, self.planes // 2, self.plane // 2, self.run * size))
            n = len(lead)
            value = jnp.transpose(value, tuple(range(n)) + (n + 2, n, n + 1, n + 3))
        value = value.reshape(lead + (self.plane, self.each * size))
        pad = (self.padded - self.each) * size
        return jnp.pad(value, [(0, 0)] * (len(lead) + 1) + [(0, pad)]) if pad else value

    def ungroup(self, value, size):
        lead = value.shape[:-2]
        value = value[..., : self.each * size]
        if self.owned:
            value = value.reshape(lead + (self.plane // 2, 2, self.planes // 2, self.run * size))
            n = len(lead)
            value = jnp.transpose(value, tuple(range(n)) + (n + 1, n + 2, n, n + 3))
        return value.reshape(lead + (H * size,))


def body(
    block_input,
    out_grad,
    routes,
    norm_in,
    in_proj,
    conv_weight,
    conv_bias,
    step_bias,
    log_rate,
    skip_gain,
    mixer_gain,
    out_proj,
    norm_mid,
    router,
    shared_gate,
    shared_up,
    shared_down,
    expert_gate,
    expert_up,
    expert_down,
):
    both = ("dp", "expert")
    planes, plane = lax.axis_size("dp"), lax.axis_size("expert")
    at = lax.axis_index("expert")
    core = at % 2
    micro, length, width = block_input.shape
    picks = routes.shape[-1]
    local = expert_gate.shape[0]
    experts = local * plane
    sets = 2 if planes == 4 and plane == 8 else 1
    place = lax.axis_index("dp")
    odd = place % 2 == 1
    taken = local // sets
    capacity = 3 * length * picks // (2 * experts)
    slots = -(-capacity // 8) * 8
    tokens = micro * length
    shard = in_proj.shape[0]
    out_rows = out_proj.shape[0]
    inner = out_rows * planes * plane
    hr = shared_down.shape[0]
    fs = hr * planes
    ehidden = expert_gate.shape[2]
    gather = lambda v, axes: lax.all_gather(v, axes, axis=0, tiled=True)
    scatter = lambda v, axes: lax.psum_scatter(v, axes, scatter_dimension=0, tiled=True)
    heads = Heads(planes, plane, out_rows, inner // H)
    size = heads.width
    wide = heads.padded * size
    states = conv_weight.shape[1] - inner
    main = 2 * wide + states + LANES

    signal = in_proj[:, inner : 2 * inner]
    maps = in_proj[:, 2 * inner : 2 * inner + states]
    steps = in_proj[:, 2 * inner + states :]
    common = jnp.concatenate([norm_in[:, None], norm_mid[:, None], router], axis=1)
    spare = LANES - heads.padded - common.shape[1]
    repeat = lambda v: jnp.broadcast_to(v[:, None, :], (shard, plane, v.shape[1]))
    split = lambda v: v.reshape(shard, planes, plane, hr).transpose(0, 2, 1, 3).reshape(shard, plane, fs)
    sent = jnp.concatenate(
        [
            heads.group(in_proj[:, :inner], size),
            heads.group(signal, size),
            repeat(maps),
            heads.group(steps, 1),
            repeat(common),
            jnp.zeros((shard, plane, spare), b16),
            split(shared_gate),
            split(shared_up),
        ],
        axis=2,
    ).transpose(1, 0, 2)
    came = lax.all_to_all(sent, "expert", split_axis=0, concat_axis=0, tiled=True)

    third = width // 3
    part = expert_down.shape[1]
    stacked = lambda v: jnp.concatenate([v[:, k * third : (k + 1) * third] for k in range(3)], axis=0)
    ends, gives = None, []
    if sets == 2:
        ends = [[0, 2], [1, 3]]
        sides = bank_rows((place % 2).astype(jnp.int32), expert_gate, expert_up, expert_down)
        banks = [sides[0, e] for e in range(taken)]
        gives = [sides[1, e] for e in range(taken)]
    else:
        banks = [
            jnp.concatenate([expert_gate[e], expert_up[e], stacked(expert_down[e])], axis=1)
            for e in range(local)
        ]

    def settle(e, came):
        rows = came.shape[0]
        both = jnp.zeros((2 * rows, came.shape[1]), b16)
        both = lax.dynamic_update_slice_in_dim(both, banks[e], place % 2 * rows, 0)
        banks[e] = lax.dynamic_update_slice_in_dim(both, came, (1 - place % 2) * rows, 0)

    own_routes = jnp.pad(routes.reshape(tokens, picks).astype(b16), ((0, 0), (0, LANES - picks)))
    flat_in = block_input.reshape(tokens, width)
    grad_low = out_grad.reshape(tokens, width)
    flat_in, came = tie(flat_in, came)
    all_in, all_grad, all_routes, *swapped = plane_gather(
        0, flat_in, grad_low, own_routes, sets=(1, sets, sets), swaps=gives
    )
    for e, other in enumerate(swapped):
        settle(e, other)
    proj = gather(came.reshape(plane * shard, -1), "dp")
    in_w = proj[:, :main]
    gate_up = proj[:, main:]
    first = 2 * wide + states + heads.padded
    gain_in = proj[:, first].astype(f32)
    gain_mid = proj[:, first + 1].astype(f32)
    route_proj = proj[:, first + 2 : first + 2 + experts]
    all_routes = all_routes[:, :picks].astype(jnp.int32)
    near = all_in.shape[0]
    count = all_grad.shape[0]
    seqs = count // LEN

    out_shard = jnp.concatenate(
        [
            jnp.concatenate([out_proj, mixer_gain[:, None]], axis=1),
            jnp.pad(shared_down, ((0, 0), (0, 1))),
        ],
        axis=0,
    )
    out_shard = jnp.pad(out_shard, ((0, 0), (0, LANES - 1)))
    half = planes // 2
    if heads.owned:
        out_all = gather(out_shard, "dp").reshape(planes, out_rows + hr, -1)
        down_w = out_all[:, out_rows:, :width].reshape(fs, width)
        pieces = out_all[:, :out_rows].reshape(2, half, out_rows, -1)
        low = core == 0
        keep = jnp.where(low, pieces[0], pieces[1])
        other = exchange(jnp.where(low, pieces[1], pieces[0]), "expert", 1)
        out_w = jnp.stack([jnp.where(low, keep, other), jnp.where(low, other, keep)], axis=1)
        out_w = out_w.reshape(wide, -1)
    else:
        down_w = gather(shared_down, "dp")
        out_all = gather(out_shard[:out_rows], both)
        out_w = lax.dynamic_slice_in_dim(out_all, at * heads.each * size, heads.each * size, 0)
        out_w = jnp.pad(out_w, ((0, wide - heads.each * size), (0, 0)))
    gain_mix = out_w[:, width]
    out_w = out_w[:, :width]

    pick_own = lambda v: lax.dynamic_index_in_dim(v, at, v.ndim - 2, keepdims=False)
    lane_pad = lambda v: jnp.pad(v.astype(f32), (0, LANES - v.shape[0])).reshape(1, LANES)
    own_lanes = lambda v: jnp.concatenate(
        [pick_own(heads.group(v[:, :inner], size)), v[:, inner:]], axis=1
    ).astype(f32)
    params = (
        own_lanes(conv_weight),
        own_lanes(conv_bias[None]),
        lane_pad(pick_own(heads.group(step_bias, 1))),
        lane_pad(pick_own(heads.group(log_rate, 1))),
        pick_own(heads.group(jnp.repeat(skip_gain, size), size)).astype(f32).reshape(1, -1),
        gain_mix.astype(f32).reshape(1, -1),
    )

    normed = rms_scale(all_in.astype(f32), gain_in).astype(b16)
    merged = dot(normed, in_w)
    mixed, joined, square = mix_forward(merged, params)
    square = jnp.sum(square, axis=1, keepdims=True)
    square_high = square.astype(b16)
    square_low = (square - square_high.astype(f32)).astype(b16)
    lane = jnp.arange(LANES)[None]
    tail = jnp.where(lane == 2 * at, square_high, jnp.where(lane == 2 * at + 1, square_low, 0))
    summed, squares = plane_scatter(2, dot(mixed, out_w).astype(b16), tail.astype(b16))
    scale = lax.rsqrt(jnp.sum(squares, axis=1, keepdims=True) / inner + epsilon)
    mixer_out = scale * summed
    start = flat_in.astype(f32)
    grad_out = grad_low.astype(f32)
    middle = start + mixer_out
    routed = rms_scale(middle, gain_mid).astype(b16)
    whole = [
        lax.all_gather(banks[e], "dp", axis=0, tiled=True, axis_index_groups=ends)
        for e in range(taken)
    ]
    if sets == 2:
        routed, whole[0] = tie(routed, whole[0])
    (all_routed,) = plane_gather(3, routed, sets=sets)

    lowest = at * local + (place % sets) * taken
    mine = lowest + jnp.arange(taken, dtype=jnp.int32)
    marks = jnp.any(all_routes[:, :, None] == mine, axis=1).reshape(seqs, LEN, taken)
    earlier = jnp.arange(LEN)[:, None] > jnp.arange(LEN)[None, :]
    rank = jnp.einsum(
        "ts,nse->net", earlier.astype(b16), marks.astype(b16), preferred_element_type=f32
    ).astype(jnp.int32)
    places = jnp.arange(slots, dtype=jnp.int32)
    chosen = (rank[:, :, None, :] == places[None, None, :, None]) & (
        marks.transpose(0, 2, 1)[:, :, None, :]
    )
    select = chosen.astype(b16)
    gates_all = dense_gates(dot(all_routed, route_proj), all_routes)
    gates_mine = lax.dynamic_slice_in_dim(gates_all, lowest, taken, axis=1)
    gates_mine = gates_mine.reshape(seqs, LEN, taken).transpose(0, 2, 1)
    slot_gates = jnp.sum(jnp.where(chosen, gates_mine[:, :, None, :], 0.0), axis=-1)

    select = select.reshape(seqs, taken * slots, LEN)
    rows_in = spread(select, all_routed, taken)
    rows_grad = spread(select, all_grad, taken)
    outs, backs, dgates, sums = [], [], [], []
    tied = []
    made_grads = []

    def weight_grads(x, depre, ehid, dmade):
        made_grads[:] = [dot_tn(x, depre).astype(b16), dot_tn(ehid, dmade).astype(b16)]
        sums.append(
            [
                lax.psum_scatter(
                    v, "dp", scatter_dimension=0, tiled=True, axis_index_groups=ends
                )
                for v in made_grads
            ]
        )

    for e in range(taken):
        bank = whole[e]
        x, dy = rows_in[e], rows_grad[e]
        x, bank, *tied = tie(x, bank, *tied)
        gu_w = bank[:, : 2 * ehidden]
        e_down = bank[:, 2 * ehidden :].reshape(planes, 3, part, third)
        e_down = e_down.transpose(0, 2, 1, 3).reshape(ehidden, width)
        g = slot_gates[:, e].reshape(seqs * slots, 1)
        epre = dot(x, gu_w)
        esoft, eslope = silu_parts(epre[:, :ehidden])
        elin = epre[:, ehidden:]
        ehid = (esoft * elin).astype(b16)
        made = dot(ehid, e_down).astype(b16).astype(f32)
        dy = dy.astype(f32)
        dgates.append(jnp.sum(made * dy, axis=1).reshape(seqs, slots))
        outs.append((made * g).astype(b16))
        dmade = (dy * g).astype(b16)
        dehid = dot_nt(dmade, e_down)
        depre = jnp.concatenate([dehid * elin * eslope, dehid * esoft], axis=1).astype(b16)
        backs.append(dot_nt(depre, gu_w).astype(b16))
        weight_grads(x, depre, ehid, dmade)
        tied = tied + made_grads
        if e == 0:
            tied = list(tie(all_routed, *tied))
            near_routed, near_grad = tied[0][:near], all_grad[:near]
            pre = dot(near_routed, gate_up)
            soft, slope = silu_parts(pre[:, :fs])
            lin = pre[:, fs:]
            hid = (soft * lin).astype(b16)
            dhid = dot_nt(near_grad, down_w)
            dpre = jnp.concatenate([dhid * lin * slope, dhid * soft], axis=1).astype(b16)
            shared_grad = dot_tn(near_routed, dpre).astype(b16)
            down_grad = dot_tn(hid, near_grad).astype(b16)
            tied = [shared_grad, down_grad, hid, dpre] + tied[1:]
    shared_grad, down_grad, hid, dpre = tied[:4]
    dgate_rows = jnp.sum(
        jnp.where(chosen, jnp.stack(dgates, axis=1)[:, :, :, None], 0.0), axis=2
    ).transpose(0, 2, 1)
    dgate_wide = lax.dynamic_update_slice_in_dim(
        jnp.zeros((count, experts), f32), dgate_rows.reshape(count, taken), lowest, axis=1
    )
    high = dgate_wide.astype(b16)
    fine = (dgate_wide - high.astype(f32)).astype(b16)
    fill = jnp.zeros((count, -(2 * experts) % LANES), b16)
    back_part = merge(select, backs, dpre, gate_up.T)
    back, back_gates = plane_scatter(
        4, back_part, jnp.concatenate([high, fine, fill], axis=1), sets=sets, after=made_grads
    )

    gates = dense_gates(dot(routed, route_proj), routes.reshape(tokens, picks))
    dgate = back_gates[:, :experts] + back_gates[:, experts : 2 * experts]
    dlogits = (gates * (dgate - jnp.sum(gates * dgate, axis=1, keepdims=True))).astype(b16)
    droute = back + dot_nt(dlogits, route_proj)
    dmid_part, mid_gain_grad = rms_back(middle, gain_mid, droute)
    dmid = grad_out + dmid_part

    def small_rows(weight_grad, bias_grad, skip_grad, head_grad):
        spot = lambda v, size: heads.ungroup(
            lax.dynamic_update_slice_in_dim(
                jnp.zeros(v.shape[:-1] + (plane, v.shape[-1]), f32), v[..., None, :], at, v.ndim - 1
            ),
            size,
        )
        taps = jnp.concatenate([weight_grad, bias_grad], axis=0)
        taps = jnp.concatenate([spot(taps[:, :wide], size), taps[:, wide:]], axis=1)
        skip_grad = jnp.sum(skip_grad.reshape(heads.padded, size), axis=1)
        head_rows = jnp.concatenate([head_grad[:2, : heads.padded], skip_grad[None]], axis=0)
        head_rows = spot(head_rows, 1).reshape(1, -1)
        head_rows = jnp.pad(head_rows, ((0, 0), (0, taps.shape[1] - head_rows.shape[1])))
        rows = jnp.concatenate([taps, head_rows], axis=0)
        return jnp.pad(rows, ((0, 16 - rows.shape[0]), (0, 0)))

    def owners(grad):
        grad = scatter(grad.astype(b16), "dp").reshape(plane, shard, -1)
        return lax.all_to_all(grad, "expert", split_axis=0, concat_axis=0, tiled=True).astype(f32)

    scaled = (dmid * scale).astype(b16)
    inward = scale * jnp.sum(scaled.astype(f32) * mixer_out, axis=1, keepdims=True) / inner
    inward_high = inward.astype(b16)
    inward_low = (inward - inward_high.astype(f32)).astype(b16)
    tail = jnp.where(lane == 0, inward_high, jnp.where(lane == 1, inward_low, 0)).astype(b16)
    shared_rows = owners(shared_grad)
    all_mid, all_inward = plane_gather(6, scaled, tail, after=sums[0])
    kept, sent = [], []
    if sets == 2:
        for group in sums:
            for v in group:
                rows = v.shape[0] // 2
                kept.append(jnp.where(odd, v[rows:], v[:rows]))
                sent.append(jnp.where(odd, v[:rows], v[rows:]))
    swapped = [exchange(v, "dp", 1) for v in sent]
    all_inward = all_inward[:, :1].astype(f32) + all_inward[:, 1:2].astype(f32)
    dmerged, weight_grad, bias_grad, skip_grad, head_grad = mix_backward(
        merged, joined, dot_nt(all_mid, out_w), all_inward, params
    )
    taps_of = small_rows(weight_grad, bias_grad, skip_grad, head_grad)
    dnormed, taps_of = plane_scatter(
        7,
        dot_nt(dmerged, in_w).astype(b16),
        gathers=[taps_of],
        after=[shared_rows] + swapped,
    )
    taps_of = jnp.sum(taps_of, axis=0)
    out_part = merge(select, outs, hid, down_w, after=[dmerged])
    out_part, dnormed = tie(out_part, dnormed)
    out_sum, small = plane_scatter(5, out_part, sets=sets, lines=[taps_of])
    small = jnp.sum(small, axis=0)

    shared_grad = shared_rows
    unsplit = lambda v: (
        v.reshape(plane, shard, planes, hr).transpose(1, 2, 0, 3).reshape(shard, planes * plane * hr)
    )
    out_w_grad = dot_tn(mixed, all_mid).astype(b16)
    if heads.owned:
        parts = out_w_grad.reshape(half, 2, out_rows, width)
        keep = jnp.where(low, parts[:, 0], parts[:, 1])
        other = exchange(jnp.where(low, parts[:, 1], parts[:, 0]), "expert", 1)
        out_parts = jnp.concatenate([jnp.where(low, keep, other), jnp.where(low, other, keep)])
        rows = jnp.concatenate([out_parts, down_grad.reshape(planes, hr, width)], axis=1)
        rows = scatter(rows.reshape(planes * (out_rows + hr), width), "dp").astype(f32)
        out_w_grad, down_grad = rows[:out_rows], rows[out_rows:]
    else:
        rows = lax.dynamic_update_slice_in_dim(
            jnp.zeros((inner, width), b16), out_w_grad[: heads.each * size], at * heads.each * size, 0
        )
        out_w_grad = scatter(rows, both).astype(f32)
        down_grad = scatter(down_grad, "dp").astype(f32)

    extra = jnp.concatenate(
        [
            jnp.zeros((width, heads.padded + 1), f32),
            mid_gain_grad[:, None],
            dot_tn(routed, dlogits),
            jnp.zeros((width, spare), f32),
        ],
        axis=1,
    )
    in_w_grad = dot_tn(normed, dmerged)
    in_w_grad = jnp.concatenate([in_w_grad[:, :-LANES], in_w_grad[:, -LANES:] + extra], axis=1)
    in_w_grad = owners(in_w_grad)
    by_row = in_w_grad.transpose(1, 0, 2)
    step_part = 2 * wide + states
    in_grad = jnp.concatenate(
        [
            heads.ungroup(by_row[:, :, :wide], size),
            heads.ungroup(by_row[:, :, wide : 2 * wide], size),
            jnp.sum(by_row[:, :, 2 * wide : step_part], axis=1),
            heads.ungroup(by_row[:, :, step_part : step_part + heads.padded], 1),
        ],
        axis=1,
    )
    shared_common = jnp.sum(by_row[:, :, first:], axis=1)
    gain_in_grad = jnp.sum(in_proj.astype(f32) * in_grad, axis=1) / norm_in.astype(f32)
    gain_mix_grad = jnp.sum(out_proj.astype(f32) * out_w_grad, axis=1) / mixer_gain.astype(f32)

    bank_grads = []
    for e in range(taken):
        if sets == 1:
            bank_grads.append([v.astype(f32) for v in sums[e]])
            continue
        pair = [
            (jnp.where(odd, came, keep), jnp.where(odd, keep, came))
            for keep, came in zip(kept[2 * e : 2 * e + 2], swapped[2 * e : 2 * e + 2])
        ]
        bank_grads.append([v.astype(f32) for v, _ in pair])
        bank_grads.append([v.astype(f32) for _, v in pair])
    bank_grads = bank_grads[::2] + bank_grads[1::2] if sets == 2 else bank_grads
    dstart, unused = rms_back(start, gain_in, dnormed)
    shape = block_input.shape
    return (
        (middle + out_sum).astype(b16).reshape(shape),
        (dmid + dstart).reshape(shape),
        gain_in_grad,
        in_grad,
        small[:4],
        small[4],
        small[5, :H],
        small[5, H : 2 * H],
        small[5, 2 * H : 3 * H],
        gain_mix_grad,
        out_w_grad,
        shared_common[:, 1],
        shared_common[:, 2 : 2 + experts],
        unsplit(shared_grad[:, :, :fs].transpose(0, 1, 2)),
        unsplit(shared_grad[:, :, fs:]),
        down_grad,
        jnp.stack([v[:, :ehidden] for v, _ in bank_grads]),
        jnp.stack([v[:, ehidden:] for v, _ in bank_grads]),
        jnp.stack([v for _, v in bank_grads]),
    )


def solution(mesh):
    both = ("dp", "expert")
    rows, matrix, bank = P(both), P(both, None), P("expert", "dp", None)
    token = P(None, both, None)
    in_specs = (token, token, token, rows, matrix, P(), P(), P(), P(), P(), rows, matrix, rows)
    in_specs = in_specs + (matrix, matrix, matrix, matrix, bank, bank, bank)
    out_specs = (token, token, rows, matrix, P(), P(), P(), P(), P(), rows, matrix, rows)
    out_specs = out_specs + (matrix, matrix, matrix, matrix, bank, bank, bank)
    return jax.shard_map(body, mesh=mesh, in_specs=in_specs, out_specs=out_specs, check_vma=False)
```

```python
from functools import partial

import jax
import jax.numpy as jnp
from jax import lax
from jax.experimental import pallas as pl
from jax.experimental.pallas import tpu as pltpu
from jax.sharding import PartitionSpec as P

H = 48
LEN = 128
LANES = 128
epsilon = 1e-05
f32 = jnp.float32
b16 = jnp.bfloat16
highest = lax.Precision.HIGHEST
NT = (((1,), (1,)), ((), ()))


def sigmoid(value):
    return 0.5 * jnp.tanh(0.5 * value) + 0.5


def grids():
    row = lax.broadcasted_iota(jnp.int32, (LEN, LANES), 0)
    lane = lax.broadcasted_iota(jnp.int32, (LEN, LANES), 1)
    return row, lane


def shifted(signal, row):
    return [signal] + [jnp.where(row >= k, pltpu.roll(signal, k, 0), 0.0) for k in (1, 2, 3)]


def convolved(parts, weight_ref, bias_ref, block):
    weight = weight_ref[:, block]
    total = bias_ref[:, block] + weight[3:4] * parts[0]
    for k in (1, 2, 3):
        total = total + weight[3 - k : 4 - k] * parts[k]
    return total


def pick(value, lane):
    low = lane < LANES // 2
    return jnp.concatenate([jnp.where(low, value, 0.0), jnp.where(low, 0.0, value)], axis=0)


def step_terms(merged_ref, step_ref, rate_ref, tail):
    raw = merged_ref[:, tail] + step_ref[...]
    step = jnp.maximum(raw, 0.0) + jnp.log1p(jnp.exp(-jnp.abs(raw)))
    decay = -jnp.exp(rate_ref[...]) * step
    row, lane = grids()
    cumul = jnp.dot(
        (row >= lane).astype(f32), decay, precision=highest, preferred_element_type=f32
    )
    return raw, step, decay, cumul


def forward_kernel(
    pairs,
    merged_ref,
    weight_ref,
    bias_ref,
    step_ref,
    rate_ref,
    skip_ref,
    gain_ref,
    mixed_ref,
    joined_ref,
    square_ref,
    cross_ref,
):
    row, lane = grids()
    tail = pl.ds((2 * pairs + 2) * LANES, LANES)
    raw, step, decay, cumul = step_terms(merged_ref, step_ref, rate_ref, tail)
    cross_ref[...] = cumul.T
    maps = []
    for at in (0, 1):
        signal = merged_ref[:, pl.ds((2 * pairs + at) * LANES, LANES)]
        block = pl.ds((pairs + at) * LANES, LANES)
        conv = convolved(shifted(signal, row), weight_ref, bias_ref, block)
        maps.append((conv * sigmoid(conv)).astype(b16))
    inner = lax.dot_general(maps[1], maps[0], NT, preferred_element_type=f32)
    square = jnp.zeros((LEN, LANES), f32)
    for pair in range(pairs):
        block = pl.ds(pair * LANES, LANES)
        signal = merged_ref[:, pl.ds((pairs + pair) * LANES, LANES)]
        conv = convolved(shifted(signal, row), weight_ref, bias_ref, block)
        values = conv * sigmoid(conv)
        steps, parts = [], []
        for head in (2 * pair, 2 * pair + 1):
            steps.append(step[:, head : head + 1])
            spread = cumul[:, head : head + 1] - cross_ref[head : head + 1, :]
            parts.append(inner * jnp.exp(jnp.where(row >= lane, spread, -1e30)))
        scaled = values * jnp.where(lane < LANES // 2, steps[0], steps[1])
        scanned = jnp.dot(
            jnp.concatenate(parts, axis=1).astype(b16),
            pick(scaled, lane).astype(b16),
            preferred_element_type=f32,
        )
        joined = scanned + skip_ref[:, block] * values
        joined_ref[:, block] = joined
        gate = merged_ref[:, block]
        gated = joined * (gate * sigmoid(gate))
        mixed_ref[:, block] = (gated * gain_ref[:, block]).astype(b16)
        square = square + gated * gated
    square_ref[...] = square


def backward_kernel(
    pairs,
    merged_ref,
    joined_ref,
    grad_ref,
    inward_ref,
    weight_ref,
    bias_ref,
    step_ref,
    rate_ref,
    skip_ref,
    gain_ref,
    out_ref,
    weight_out,
    bias_out,
    skip_out,
    head_out,
    cross_ref,
):
    row, lane = grids()
    low = lane < LANES // 2

    @pl.when(pl.program_id(0) == 0)
    def _():
        weight_out[...] = jnp.zeros_like(weight_out)
        bias_out[...] = jnp.zeros_like(bias_out)
        skip_out[...] = jnp.zeros_like(skip_out)
        head_out[...] = jnp.zeros_like(head_out)

    inward = inward_ref[...]
    tail = pl.ds((2 * pairs + 2) * LANES, LANES)
    raw, step, decay, cumul = step_terms(merged_ref, step_ref, rate_ref, tail)
    cross_ref[...] = cumul.T
    convs, slopes, shifts, maps = [], [], [], []
    for at in (0, 1):
        signal = merged_ref[:, pl.ds((2 * pairs + at) * LANES, LANES)]
        parts = shifted(signal, row)
        conv = convolved(parts, weight_ref, bias_ref, pl.ds((pairs + at) * LANES, LANES))
        sigma = sigmoid(conv)
        shifts.append(parts)
        slopes.append(sigma * (1.0 + conv * (1.0 - sigma)))
        maps.append((conv * sigma).astype(b16))
    flipped = lax.dot_general(maps[0], maps[1], NT, preferred_element_type=f32)
    dinner = jnp.zeros((LEN, LEN), f32)
    dstep = jnp.zeros((LEN, LANES), f32)
    dcum = jnp.zeros((LEN, LANES), f32)

    def back_conv(grad, parts, block, out_block):
        bias_out[:, block] += jnp.sum(grad, axis=0, keepdims=True)
        weight = weight_ref[:, block]
        total = weight[3:4] * grad
        taps = [jnp.sum(grad * parts[3 - k], axis=0, keepdims=True) for k in range(4)]
        weight_out[:, block] += jnp.concatenate(taps, axis=0)
        for k in (1, 2, 3):
            later = jnp.where(row < LEN - k, pltpu.roll(grad, LEN - k, 0), 0.0)
            total = total + weight[3 - k : 4 - k] * later
        out_ref[:, out_block] = total.astype(b16)

    for pair in range(pairs):
        block = pl.ds(pair * LANES, LANES)
        other = pl.ds((pairs + pair) * LANES, LANES)
        gate = merged_ref[:, block]
        joined = joined_ref[:, block]
        sigma = sigmoid(gate)
        soft = gate * sigma
        dgated = grad_ref[:, block] * gain_ref[:, block] - joined * soft * inward
        djoined = dgated * soft
        out_ref[:, block] = (dgated * joined * (sigma + soft * (1.0 - sigma))).astype(b16)

        parts = shifted(merged_ref[:, other], row)
        conv = convolved(parts, weight_ref, bias_ref, block)
        csig = sigmoid(conv)
        values = conv * csig
        skip = skip_ref[:, block]
        skip_out[:, block] += jnp.sum(djoined * values, axis=0, keepdims=True)
        scanned = joined - skip * values
        steps, blends, spreads = [], [], []
        for head in (2 * pair, 2 * pair + 1):
            steps.append(step[:, head : head + 1])
            spread = cumul[:, head : head + 1] - cross_ref[head : head + 1, :]
            spreads.append(jnp.exp(jnp.where(row >= lane, spread, -1e30)))
            blends.append(flipped * jnp.exp(jnp.where(row <= lane, -spread, -1e30)))
        widened = jnp.where(low, steps[0], steps[1])
        scaled = (values * widened).astype(b16)
        dlow = djoined.astype(b16)
        both = pick(djoined, lane).astype(b16)
        dweights = lax.dot_general(both, scaled, NT, preferred_element_type=f32)
        dinner = dinner + dweights[:LEN] * spreads[0] + dweights[LEN:] * spreads[1]
        dscaled = jnp.dot(
            jnp.concatenate(blends, axis=1).astype(b16), both, preferred_element_type=f32
        )
        dvalues = skip * djoined + dscaled * widened
        first = dscaled * values
        second = dlow.astype(f32) * scanned - scaled.astype(f32) * dscaled
        for at in (0, 1):
            mine = low if at == 0 else jnp.logical_not(low)
            here = lane == 2 * pair + at
            total = jnp.sum(jnp.where(mine, first, 0.0), axis=1, keepdims=True)
            dstep = jnp.where(here, total, dstep)
            total = jnp.sum(jnp.where(mine, second, 0.0), axis=1, keepdims=True)
            dcum = jnp.where(here, total, dcum)
        back_conv(dvalues * (csig * (1.0 + conv * (1.0 - csig))), parts, block, other)
    dmaps = (
        jnp.dot(dinner.T.astype(b16), maps[1], preferred_element_type=f32),
        jnp.dot(dinner.astype(b16), maps[0], preferred_element_type=f32),
    )
    for at in (0, 1):
        back_conv(
            dmaps[at] * slopes[at],
            shifts[at],
            pl.ds((pairs + at) * LANES, LANES),
            pl.ds((2 * pairs + at) * LANES, LANES),
        )
    ddecay = jnp.dot(
        (row <= lane).astype(f32), dcum, precision=highest, preferred_element_type=f32
    )
    dstep = dstep - ddecay * jnp.exp(rate_ref[...])
    draw = jnp.where(lane < 2 * pairs, dstep * sigmoid(raw), 0.0)
    out_ref[:, tail] = draw.astype(b16)
    head_out[0:1, :] += jnp.sum(draw, axis=0, keepdims=True)
    head_out[1:2, :] += jnp.sum(ddecay * decay, axis=0, keepdims=True)


def rows_of(columns):
    return pl.BlockSpec((LEN, columns), lambda s: (s, 0))


def fixed(rows, columns):
    return pl.BlockSpec((rows, columns), lambda s: (0, 0))


def mix_forward(merged, params):
    tokens, columns = merged.shape
    width = params[-1].shape[1]
    return pl.pallas_call(
        partial(forward_kernel, width // LANES),
        grid=(tokens // LEN,),
        in_specs=[rows_of(columns)] + [fixed(*p.shape) for p in params],
        out_specs=[rows_of(width), rows_of(width), rows_of(LANES)],
        out_shape=[
            jax.ShapeDtypeStruct((tokens, width), b16),
            jax.ShapeDtypeStruct((tokens, width), f32),
            jax.ShapeDtypeStruct((tokens, LANES), f32),
        ],
        scratch_shapes=[pltpu.VMEM((LANES, LEN), f32)],
        compiler_params=pltpu.CompilerParams(vmem_limit_bytes=32 << 20),
        cost_estimate=pl.CostEstimate(flops=0, bytes_accessed=1024, transcendentals=0),
    )(merged, *params)


def mix_backward(merged, joined, grad, inward, params):
    tokens, columns = merged.shape
    width = params[-1].shape[1]
    conv = params[0].shape[1]
    return pl.pallas_call(
        partial(backward_kernel, width // LANES),
        grid=(tokens // LEN,),
        in_specs=[rows_of(columns), rows_of(width), rows_of(width), rows_of(1)]
        + [fixed(*p.shape) for p in params],
        out_specs=[
            rows_of(columns),
            fixed(4, conv),
            fixed(1, conv),
            fixed(1, width),
            fixed(8, LANES),
        ],
        out_shape=[
            jax.ShapeDtypeStruct((tokens, columns), b16),
            jax.ShapeDtypeStruct((4, conv), f32),
            jax.ShapeDtypeStruct((1, conv), f32),
            jax.ShapeDtypeStruct((1, width), f32),
            jax.ShapeDtypeStruct((8, LANES), f32),
        ],
        scratch_shapes=[pltpu.VMEM((LANES, LEN), f32)],
        compiler_params=pltpu.CompilerParams(vmem_limit_bytes=32 << 20),
        cost_estimate=pl.CostEstimate(flops=0, bytes_accessed=1024, transcendentals=0),
    )(merged, joined, grad, inward, *params)


MESH = pl.DeviceIdType.MESH


def neighbours(me):
    core, column, line = me % 2, (me // 2) % 2, me // 4
    return 1 - 2 * core, 2 - 4 * column, 4 - 8 * line


def other_plane(me):
    place = lax.axis_index("dp")
    return {"dp": place + 1 - 2 * (place % 2), "expert": me}


def greet(peers):
    barrier = pltpu.get_barrier_semaphore()
    for peer in peers:
        pl.semaphore_signal(barrier, inc=1, device_id=peer, device_id_type=MESH)
    pl.semaphore_wait(barrier, len(peers))


def far_plane(me):
    place = lax.axis_index("dp")
    return {"dp": place + 2 - 4 * (place // 2), "expert": me}


def peers_of(me, across, along=0):
    core, column, line = neighbours(me)
    peers = [{"expert": me + core}, {"expert": me + column}, {"expert": me + line}]
    peers = peers + ([other_plane(me)] if across else [])
    return peers + ([far_plane(me)] if along else [])


def begin_swaps(refs, swaps, first, send_sem, recv_sem, peer):
    found = []
    for i in range(swaps):
        found.append(remote(send_sem, recv_sem, first + i, refs[i], refs[swaps + i], peer[0]))
        found[-1].start()
    return found


def remote(send_sem, recv_sem, at, src, dst, peer):
    return pltpu.make_async_remote_copy(
        src_ref=src,
        dst_ref=dst,
        send_sem=send_sem.at[at],
        recv_sem=recv_sem.at[at],
        device_id=peer,
        device_id_type=MESH,
    )


def gather_kernel(sets, count, swaps, lines, waits, *refs):
    owns, sides, block = refs[:count], refs[count : count + swaps], refs[count + swaps :][:lines]
    refs = refs[count + swaps + lines + waits :]
    shares = swaps * (sides[0].shape[1] if swaps else 0)
    total = count + shares + lines
    outs, take, line_out = refs[:count], refs[count : count + shares], refs[count + shares : total]
    send_sem, recv_sem, copy_sem = refs[total:]
    me = lax.axis_index("expert")
    core, column, line = neighbours(me)
    half = owns[0].shape[0] // 2
    top, bottom = pl.ds(0, half), pl.ds(half, half)
    peers = peers_of(me, max(sets) == 2 or swaps or lines, lines)
    greet(peers)
    copy = partial(remote, send_sem, recv_sem)
    arrays = range(count)
    place = lax.axis_index("dp")
    distant = place + 2 - 4 * (place // 2)
    along = []
    for i in range(lines):
        base = 17 * count + shares + 3 * i
        own, out = block[i], line_out[i]
        along.append(
            (
                pltpu.make_async_copy(own, out.at[place], copy_sem.at[count + i]),
                copy(base, own, out.at[place], peers[4]),
                copy(base + 1, own, out.at[place], peers[3]),
                copy(base + 2, out.at[distant], out.at[distant], peers[3]),
            )
        )
    steps = []
    here, across = [], []
    for i in arrays:
        here.append(pltpu.make_async_copy(owns[i], outs[i].at[me], copy_sem.at[i]))
        if sets[i] == 2:
            across.append(copy(17 * i + 16, owns[i], outs[i].at[8 + me], peers[3]))
    for g in range(2):
        for i in arrays:
            if sets[i] <= g:
                continue
            out = lambda at: outs[i].at[8 * g + at]
            own = owns[i] if g == 0 else out(me)
            at_x, at_y, at_d = out(me + column), out(me + line), out(me + column + line)
            base = 17 * i + 8 * g
            steps.append(
                (
                    copy(base, own, out(me), peers[1]),
                    copy(base + 1, own, out(me), peers[2]),
                    copy(base + 2, own, out(me), peers[0]),
                    copy(base + 3, at_x.at[top], at_x.at[top], peers[2]),
                    copy(base + 4, at_y.at[bottom], at_y.at[bottom], peers[1]),
                    copy(base + 5, at_x, at_x, peers[0]),
                    copy(base + 6, at_y, at_y, peers[0]),
                    copy(base + 7, at_d, at_d, peers[0]),
                )
            )

    def begin(group):
        for to_x, to_y, to_core, *unused in group:
            to_x.start()
            to_y.start()
            to_core.start()

    def relay(group):
        for to_x, to_y, to_core, x_relay, y_relay, x_core, y_core, d_core in group:
            to_x.wait_recv()
            x_relay.start()
            x_core.start()
            to_y.wait_recv()
            y_relay.start()
            y_core.start()

    def close(group):
        for to_x, to_y, to_core, x_relay, y_relay, x_core, y_core, d_core in group:
            x_relay.wait_recv()
            y_relay.wait_recv()
            d_core.start()

    first, second = steps[:count], steps[count:]
    for here_block, to_far, to_near, relayed in along:
        to_far.start()
        to_near.start()
        here_block.start()
    for copied in across:
        copied.start()
    begin(first)
    swapped = []
    for i in range(shares):
        mine = take[i].at[place % 2]
        here.append(pltpu.make_async_copy(sides[0].at[0, i], mine, copy_sem.at[count + lines + i]))
        swapped.append(copy(17 * count + i, sides[0].at[1, i], mine, peers[3]))
        swapped[-1].start()
    for here_block, to_far, to_near, relayed in along:
        to_far.wait_recv()
        relayed.start()
    for copied in here:
        copied.start()
    for copied in across:
        copied.wait_recv()
    begin(second)
    relay(first)
    close(first)
    relay(second)
    close(second)
    for copied in here:
        copied.wait()
    for copied in across:
        copied.wait_send()
    for copied in swapped:
        copied.wait()
    for here_block, to_far, to_near, relayed in along:
        here_block.wait()
        to_near.wait_recv()
        relayed.wait_recv()
        for copied in (to_far, to_near, relayed):
            copied.wait_send()
    for group in steps:
        for at in (2, 5, 6, 7):
            group[at].wait_recv()
        for sent in group:
            sent.wait_send()


def plane_gather(number, *owns, sets=1, swaps=(), lines=(), after=()):
    if lax.axis_size("expert") != 8 or (lines and lax.axis_size("dp") != 4):
        return [lax.all_gather(own, "expert", axis=0, tiled=True) for own in owns] + [
            lax.all_gather(line, "dp", axis=0, tiled=True) for line in lines
        ]
    count = len(owns)
    sets = (sets,) * count if isinstance(sets, int) else sets
    shares = [v for side in swaps for v in [side.shape[2:]] * side.shape[1]]
    total = count + len(shares) + len(lines)
    sems = 17 * count + len(shares) + 3 * len(lines)
    anywhere = pl.BlockSpec(memory_space=pl.ANY)
    outs = pl.pallas_call(
        partial(gather_kernel, sets, count, len(swaps), len(lines), len(after)),
        out_shape=[
            jax.ShapeDtypeStruct((8 * n,) + own.shape, own.dtype) for n, own in zip(sets, owns)
        ]
        + [jax.ShapeDtypeStruct((2,) + v, b16) for v in shares]
        + [jax.ShapeDtypeStruct((4,) + v.shape, v.dtype) for v in lines],
        in_specs=[anywhere] * (count + len(swaps) + len(lines) + len(after)),
        out_specs=[anywhere] * total,
        scratch_shapes=[
            pltpu.SemaphoreType.DMA((sems,)),
            pltpu.SemaphoreType.DMA((sems,)),
            pltpu.SemaphoreType.DMA((count + len(lines) + len(shares),)),
        ],
        compiler_params=pltpu.CompilerParams(collective_id=number, has_side_effects=True),
        cost_estimate=pl.CostEstimate(flops=0, bytes_accessed=1024, transcendentals=0),
    )(*owns, *swaps, *lines, *after)
    gathered = [out.reshape(-1, out.shape[2]) for out in outs[:count]]
    spread = [out.reshape(4 * out.shape[1], out.shape[2]) for out in outs[total - len(lines) :]]
    return gathered + list(outs[count : total - len(lines)]) + spread


def scatter_kernel(sets, count, extra, gathers, lines, waits, *refs):
    parts, give = refs[:count], refs[count : count + extra]
    refs = refs[count + extra :]
    owns, blocks = refs[:gathers], refs[gathers : gathers + lines]
    refs = refs[gathers + lines + waits :]
    outs, take = refs[:count], refs[count : count + extra]
    refs = refs[count + extra :]
    gathered, line_outs = refs[:gathers], refs[gathers : gathers + lines]
    refs = refs[gathers + lines :]
    per = 6 * sets + (3 if sets == 2 else 0)
    held = [refs[per * i : per * (i + 1)] for i in range(count)]
    send_sem, recv_sem, copy_sem = refs[per * count :]
    me = lax.axis_index("expert")
    core, column, line = neighbours(me)
    rows = outs[0].shape[0]
    half = rows // 2
    top, bottom = pl.ds(0, half), pl.ds(half, half)
    peers = peers_of(me, sets == 2 or extra or lines, lines)
    greet(peers)
    copy = partial(remote, send_sem, recv_sem)
    arrays = range(count)
    chips = (me + column + line, me + column, me + line, me)
    order = range(sets - 1, -1, -1)
    keep = lambda g, i, at: held[i][6 * g + at]
    total_ref = lambda g, i: outs[i] if g == 0 else held[i][12]
    swaps, loads = {}, {}
    for g in order:
        for k in range(4):
            for i in arrays:
                base = 21 * i + 10 * g + k
                swaps[g, i, k] = copy(
                    base, parts[i].at[8 * g + chips[k] + core], keep(g, i, 1).at[k], peers[0]
                )
                loads[g, i, k] = pltpu.make_async_copy(
                    parts[i].at[8 * g + chips[k]],
                    keep(g, i, 0).at[k],
                    copy_sem.at[8 * i + 4 * g + k],
                )
                swaps[g, i, k].start()
                loads[g, i, k].start()

    swapped = begin_swaps(give + take, extra, 21 * count, send_sem, recv_sem, peers[3:4])
    base = 21 * count + extra
    place = lax.axis_index("dp")
    distant = place + 2 - 4 * (place // 2)
    here, small, along = [], [], []
    for i in range(gathers):
        own, out = owns[i], lambda at: gathered[i].at[at]
        at_x, at_y, at_d = out(me + column), out(me + line), out(me + column + line)
        low, high = pl.ds(0, own.shape[0] // 2), pl.ds(own.shape[0] // 2, own.shape[0] // 2)
        here.append(pltpu.make_async_copy(own, out(me), copy_sem.at[8 * count + i]))
        small.append(
            (
                copy(base, own, out(me), peers[1]),
                copy(base + 1, own, out(me), peers[2]),
                copy(base + 2, own, out(me), peers[0]),
                copy(base + 3, at_x.at[low], at_x.at[low], peers[2]),
                copy(base + 4, at_y.at[high], at_y.at[high], peers[1]),
                copy(base + 5, at_x, at_x, peers[0]),
                copy(base + 6, at_y, at_y, peers[0]),
                copy(base + 7, at_d, at_d, peers[0]),
            )
        )
        base += 8
        for begun in [here[-1]] + list(small[-1][:3]):
            begun.start()
    for i in range(lines):
        own, out = blocks[i], line_outs[i]
        here.append(pltpu.make_async_copy(own, out.at[place], copy_sem.at[8 * count + gathers + i]))
        along.append(
            (
                copy(base, own, out.at[place], peers[4]),
                copy(base + 1, own, out.at[place], peers[3]),
                copy(base + 2, out.at[distant], out.at[distant], peers[3]),
            )
        )
        base += 3
        for begun in [here[-1]] + list(along[-1][:2]):
            begun.start()

    def each(first, amount, step):
        def body(at, carry):
            step(pl.ds(pl.multiple_of(first + at * 16, 16), 16))
            return carry

        lax.fori_loop(0, amount // 16, body, 0)

    def pair_sum(g, k):
        for i in arrays:
            loads[g, i, k].wait()
            swaps[g, i, k].wait_recv()

        def step(block):
            for i in arrays:
                mine, theirs = keep(g, i, 0), keep(g, i, 1)
                total = mine[k, block].astype(f32) + theirs[k, block].astype(f32)
                if k == 3:
                    total_ref(g, i)[block, :] = total
                else:
                    mine[k, block] = total.astype(b16)

        each(0, rows, step)

    sent = []

    def sends(g, at, k, area, into, peer):
        found = []
        for i in arrays:
            target = keep(g, i, into)
            target = target if into > 3 else target.at[area]
            source = keep(g, i, 0).at[k, area]
            found.append(copy(21 * i + 10 * g + at, source, target, peer))
            found[-1].start()
        sent.extend(found)
        return found

    legs = {}

    def begin_legs(g, summed):
        for k in range(4):
            if not summed:
                pair_sum(g, k)
            if k == 0:
                legs[g] = [
                    sends(g, 4, 0, top, 4, peers[1]),
                    sends(g, 5, 0, bottom, 5, peers[2]),
                ]
            elif k == 1:
                legs[g].append(sends(g, 6, 1, top, 2, peers[1]))
            elif k == 2:
                legs[g].append(sends(g, 7, 2, bottom, 3, peers[2]))

    def second_legs(g):
        d_x, d_y, x_top, y_bottom = legs[g]
        for i in arrays:
            d_x[i].wait_recv()

        def add_y(block):
            for i in arrays:
                mine, extra = keep(g, i, 0), keep(g, i, 4)
                mine[2, block] = (
                    mine[2, block].astype(f32) + extra[block, :].astype(f32)
                ).astype(b16)

        each(0, half, add_y)
        y_top = sends(g, 8, 2, top, 3, peers[2])
        for i in arrays:
            d_y[i].wait_recv()

        def add_x(block):
            low = pl.ds(pl.multiple_of(block.start - half, 16), 16)
            for i in arrays:
                mine, extra = keep(g, i, 0), keep(g, i, 5)
                mine[1, block] = (
                    mine[1, block].astype(f32) + extra[low, :].astype(f32)
                ).astype(b16)

        each(half, half, add_x)
        x_bottom = sends(g, 9, 1, bottom, 2, peers[1])
        legs[g] = [x_top, y_bottom, y_top, x_bottom]

    begin_legs(sets - 1, False)
    if sets == 2:
        for k in range(4):
            pair_sum(0, k)
    for to_x, to_y, to_core, x_relay, y_relay, x_core, y_core, d_core in small:
        to_x.wait_recv()
        x_relay.start()
        x_core.start()
        to_y.wait_recv()
        y_relay.start()
        y_core.start()
    for to_far, to_near, relayed in along:
        to_far.wait_recv()
        relayed.start()
    second_legs(sets - 1)
    if sets == 2:
        begin_legs(0, True)
    for to_x, to_y, to_core, x_relay, y_relay, x_core, y_core, d_core in small:
        x_relay.wait_recv()
        y_relay.wait_recv()
        d_core.start()
    across = []
    for g in order:
        if g == 0 and sets == 2:
            second_legs(0)
        for i in arrays:
            for came in legs[g]:
                came[i].wait_recv()

        def finish(block):
            for i in arrays:
                total = (
                    total_ref(g, i)[block, :]
                    + keep(g, i, 2)[block, :].astype(f32)
                    + keep(g, i, 3)[block, :].astype(f32)
                )
                if g == 0:
                    outs[i][block, :] = total
                else:
                    held[i][13][block, :] = total.astype(b16)

        each(0, rows, finish)
        if g == 1:
            for i in arrays:
                across.append(copy(21 * i + 20, held[i][13], held[i][14], peers[3]))
                across[-1].start()
    if sets == 2:
        for i in arrays:
            across[i].wait_recv()

        def add_z(block):
            for i in arrays:
                outs[i][block, :] = outs[i][block, :] + held[i][14][block, :].astype(f32)

        each(0, rows, add_z)
    for done in list(swaps.values()) + sent + across:
        done.wait_send()
    for copied in swapped + here:
        copied.wait()
    for group in small:
        for at in (2, 5, 6, 7):
            group[at].wait_recv()
        for copied in group:
            copied.wait_send()
    for to_far, to_near, relayed in along:
        to_near.wait_recv()
        relayed.wait_recv()
        for copied in (to_far, to_near, relayed):
            copied.wait_send()


def plane_scatter(number, *parts, sets=1, swaps=(), gathers=(), lines=(), after=()):
    if lax.axis_size("expert") != 8:
        return [
            lax.psum_scatter(part, "expert", scatter_dimension=0, tiled=True).astype(f32)
            for part in parts
        ] + [lax.all_gather(v, "expert", axis=0) for v in gathers] + [
            lax.all_gather(v, "dp", axis=0) for v in lines
        ]
    count = len(parts)
    others = list(swaps) + list(gathers) + list(lines) + list(after)
    moved = len(others) - len(after)
    sems = 21 * count + len(swaps) + 8 * len(gathers) + 3 * len(lines)
    rows = parts[0].shape[0] // (8 * sets)
    scratch = []
    for part in parts:
        columns = part.shape[1]
        for g in range(sets):
            scratch += [pltpu.VMEM((4, rows, columns), b16)] * 2
            scratch += [pltpu.VMEM((rows, columns), b16)] * 2
            scratch += [pltpu.VMEM((rows // 2, columns), b16)] * 2
        if sets == 2:
            scratch += [pltpu.VMEM((rows, columns), f32)]
            scratch += [pltpu.VMEM((rows, columns), b16)] * 2
    return pl.pallas_call(
        partial(
            scatter_kernel, sets, count, len(swaps), len(gathers), len(lines), len(after)
        ),
        out_shape=[jax.ShapeDtypeStruct((rows, part.shape[1]), f32) for part in parts]
        + [jax.ShapeDtypeStruct(v.shape, v.dtype) for v in swaps]
        + [jax.ShapeDtypeStruct((8,) + v.shape, v.dtype) for v in gathers]
        + [jax.ShapeDtypeStruct((4,) + v.shape, v.dtype) for v in lines],
        in_specs=[pl.BlockSpec(memory_space=pl.ANY)] * (count + len(others)),
        out_specs=[pl.BlockSpec(memory_space=pltpu.VMEM)] * count
        + [pl.BlockSpec(memory_space=pl.ANY)] * moved,
        scratch_shapes=scratch
        + [
            pltpu.SemaphoreType.DMA((sems,)),
            pltpu.SemaphoreType.DMA((sems,)),
            pltpu.SemaphoreType.DMA((8 * count + len(gathers) + len(lines),)),
        ],
        compiler_params=pltpu.CompilerParams(collective_id=number, has_side_effects=True),
        cost_estimate=pl.CostEstimate(flops=0, bytes_accessed=1024, transcendentals=0),
    )(*[part.reshape(8 * sets, rows, part.shape[1]) for part in parts], *others)


def rms_scale(value, gain):
    return value * lax.rsqrt(jnp.mean(value * value, axis=-1, keepdims=True) + epsilon) * gain


def rms_back(value, gain, grad):
    scale = lax.rsqrt(jnp.mean(value * value, axis=-1, keepdims=True) + epsilon)
    unit = value * scale
    inward = grad * gain
    back = scale * (inward - unit * jnp.mean(inward * unit, axis=-1, keepdims=True))
    return back, jnp.sum(grad * unit, axis=0)


def dot(a, b):
    return jnp.dot(a, b, preferred_element_type=f32)


def dot_nt(a, b):
    return lax.dot_general(a, b, NT, preferred_element_type=f32)


def dot_tn(a, b):
    return lax.dot_general(a, b, (((0,), (0,)), ((), ())), preferred_element_type=f32)


def silu_parts(value):
    sigma = jax.nn.sigmoid(value)
    return value * sigma, sigma * (1.0 + value * (1.0 - sigma))


def dense_gates(logits, route_ids):
    experts = logits.shape[1]
    ids = jnp.arange(experts, dtype=jnp.int32)
    named = jnp.any(route_ids[:, :, None] == ids, axis=1)
    top = jnp.max(jnp.where(named, logits, -jnp.inf), axis=1, keepdims=True)
    weight = jnp.where(named, jnp.exp(jnp.where(named, logits - top, 0.0)), 0.0)
    return weight / jnp.sum(weight, axis=1, keepdims=True)


def tie(*values):
    return lax.optimization_barrier(values)


def exchange(value, axis, distance):
    size = lax.axis_size(axis)
    return lax.ppermute(value, axis, [(i, i ^ distance) for i in range(size)])


def total_of(value, axes):
    for axis in axes:
        distance = 1
        while distance < lax.axis_size(axis):
            value = value + exchange(value, axis, distance)
            distance *= 2
    return value


def merge_kernel(near, parts, select_ref, *refs):
    rows_refs, (small_ref, weight_ref), out_ref = refs[:parts], refs[parts : parts + 2], refs[-1]
    slots = select_ref.shape[1] // parts
    total = None
    for k in range(parts):
        term = lax.dot_general(
            select_ref[0, k * slots : (k + 1) * slots, :],
            rows_refs[k][0],
            (((0,), (0,)), ((), ())),
            preferred_element_type=f32,
        )
        total = term if total is None else total + term
    first = pl.program_id(0) < near

    @pl.when(first)
    def _():
        out_ref[...] = (total + dot(small_ref[...], weight_ref[...])).astype(b16)

    @pl.when(jnp.logical_not(first))
    def _():
        out_ref[...] = total.astype(b16)


def merge(select, parts, small, weight, after=()):
    seqs, slots, unused = select.shape
    slots = slots // len(parts)
    width = weight.shape[1]
    near = small.shape[0] // LEN
    return pl.pallas_call(
        partial(merge_kernel, near, len(parts)),
        grid=(seqs,),
        in_specs=[pl.BlockSpec((1,) + select.shape[1:], lambda s: (s, 0, 0))]
        + [pl.BlockSpec((1, slots, width), lambda s: (s, 0, 0))] * len(parts)
        + [
            pl.BlockSpec((LEN, small.shape[1]), lambda s: (jnp.minimum(s, near - 1), 0)),
            fixed(*weight.shape),
        ]
        + [pl.BlockSpec(memory_space=pl.ANY)] * len(after),
        out_specs=rows_of(width),
        out_shape=jax.ShapeDtypeStruct((seqs * LEN, width), b16),
        compiler_params=pltpu.CompilerParams(vmem_limit_bytes=32 << 20),
        cost_estimate=pl.CostEstimate(flops=0, bytes_accessed=1024, transcendentals=0),
    )(select, *[v.reshape(seqs, slots, width) for v in parts], small, weight, *after)


def spread_kernel(parts, select_ref, rows_ref, *out_refs):
    slots = select_ref.shape[1] // parts
    rows = dot(select_ref[0], rows_ref[...]).astype(b16)
    for k in range(parts):
        out_refs[k][0] = rows[k * slots : (k + 1) * slots]


def spread(select, rows, parts):
    seqs, slots, unused = select.shape
    slots = slots // parts
    width = rows.shape[1]
    outs = pl.pallas_call(
        partial(spread_kernel, parts),
        grid=(seqs,),
        in_specs=[
            pl.BlockSpec((1,) + select.shape[1:], lambda s: (s, 0, 0)),
            rows_of(width),
        ],
        out_specs=[pl.BlockSpec((1, slots, width), lambda s: (s, 0, 0))] * parts,
        out_shape=[jax.ShapeDtypeStruct((seqs, slots, width), b16)] * parts,
        compiler_params=pltpu.CompilerParams(vmem_limit_bytes=32 << 20),
        cost_estimate=pl.CostEstimate(flops=0, bytes_accessed=1024, transcendentals=0),
    )(select, rows)
    return [v.reshape(seqs * slots, width) for v in outs]


def expert_kernel(
    x_ref,
    dy_ref,
    gate_ref,
    bank_ref,
    out_ref,
    back_ref,
    dgate_ref,
    wide_ref,
    tall_ref,
    down_ref,
    wide_sum,
    tall_sum,
):
    hidden = tall_ref.shape[0]
    third = x_ref.shape[1] // 3
    part = hidden // 4

    @pl.when(pl.program_id(0) == 0)
    def _():
        for i in range(4):
            for k in range(3):
                down_ref[i * part : (i + 1) * part, k * third : (k + 1) * third] = bank_ref[
                    (3 * i + k) * part : (3 * i + k + 1) * part, 2 * hidden :
                ]
        wide_sum[...] = jnp.zeros_like(wide_sum)
        tall_sum[...] = jnp.zeros_like(tall_sum)

    x, gate = x_ref[...], gate_ref[...]
    pre = dot(x, bank_ref[:, : 2 * hidden])
    lin = pre[:, hidden:]
    sigma = sigmoid(pre[:, :hidden])
    soft = pre[:, :hidden] * sigma
    slope = sigma * (1.0 + pre[:, :hidden] * (1.0 - sigma))
    hid = (soft * lin).astype(b16)
    made = dot(hid, down_ref[...]).astype(b16).astype(f32)
    dy = dy_ref[...].astype(f32)
    dgate_ref[...] = jnp.sum(made * dy, axis=1, keepdims=True)
    out_ref[...] = (made * gate).astype(b16)
    dmade = (dy * gate).astype(b16)
    dhid = dot_nt(dmade, down_ref[...])
    dpre = jnp.concatenate([dhid * lin * slope, dhid * soft], axis=1).astype(b16)
    back_ref[...] = dot_nt(dpre, bank_ref[:, : 2 * hidden]).astype(b16)
    wide_sum[...] += dot_tn(x, dpre)
    tall_sum[...] += dot_tn(hid, dmade)

    @pl.when(pl.program_id(0) == pl.num_programs(0) - 1)
    def _():
        wide_ref[...] = wide_sum[...].astype(b16)
        tall_ref[...] = tall_sum[...].astype(b16)


def expert(x, dy, gate, bank, hidden, after=()):
    rows, width = x.shape
    block = 256
    per = pl.BlockSpec((block, width), lambda s: (s, 0))
    one = pl.BlockSpec((block, 1), lambda s: (s, 0))

    def kernel(*refs):
        expert_kernel(*refs[:4], *refs[4 + len(after) :])

    return pl.pallas_call(
        kernel,
        grid=(rows // block,),
        in_specs=[
            per,
            per,
            one,
            pl.BlockSpec(bank.shape, lambda s: (0, 0), pipeline_mode=pl.Buffered(1)),
        ]
        + [pl.BlockSpec(memory_space=pl.ANY)] * len(after),
        out_specs=[per, per, one, fixed(width, 2 * hidden), fixed(hidden, width)],
        out_shape=[
            jax.ShapeDtypeStruct((rows, width), b16),
            jax.ShapeDtypeStruct((rows, width), b16),
            jax.ShapeDtypeStruct((rows, 1), f32),
            jax.ShapeDtypeStruct((width, 2 * hidden), b16),
            jax.ShapeDtypeStruct((hidden, width), b16),
        ],
        scratch_shapes=[
            pltpu.VMEM((hidden, width), b16),
            pltpu.VMEM((width, 2 * hidden), f32),
            pltpu.VMEM((hidden, width), f32),
        ],
        compiler_params=pltpu.CompilerParams(vmem_limit_bytes=48 << 20),
        cost_estimate=pl.CostEstimate(flops=0, bytes_accessed=1024, transcendentals=0),
    )(x, dy, gate, bank, *after)


def shared_kernel(
    x_ref, dy_ref, wide_ref, tall_ref, hid_ref, dpre_ref, wide_out, tall_out, wide_sum, tall_sum
):
    hidden = tall_ref.shape[0]

    @pl.when(pl.program_id(0) == 0)
    def _():
        wide_sum[...] = jnp.zeros_like(wide_sum)
        tall_sum[...] = jnp.zeros_like(tall_sum)

    x, dy = x_ref[...], dy_ref[...]
    pre = dot(x, wide_ref[...])
    lin = pre[:, hidden:]
    sigma = sigmoid(pre[:, :hidden])
    soft = pre[:, :hidden] * sigma
    slope = sigma * (1.0 + pre[:, :hidden] * (1.0 - sigma))
    hid = (soft * lin).astype(b16)
    dhid = dot_nt(dy, tall_ref[...])
    dpre = jnp.concatenate([dhid * lin * slope, dhid * soft], axis=1).astype(b16)
    hid_ref[...] = hid
    dpre_ref[...] = dpre
    wide_sum[...] += dot_tn(x, dpre)
    tall_sum[...] += dot_tn(hid, dy)

    @pl.when(pl.program_id(0) == pl.num_programs(0) - 1)
    def _():
        wide_out[...] = wide_sum[...].astype(b16)
        tall_out[...] = tall_sum[...].astype(b16)


def shared_expert(x, dy, wide, tall, rows, after=()):
    width, hidden = x.shape[1], tall.shape[0]
    block = 256
    per = lambda n: pl.BlockSpec((block, n), lambda s: (s, 0))

    def kernel(*refs):
        shared_kernel(*refs[:4], *refs[4 + len(after) :])

    return pl.pallas_call(
        kernel,
        grid=(rows // block,),
        in_specs=[per(width), per(width), fixed(*wide.shape), fixed(*tall.shape)]
        + [pl.BlockSpec(memory_space=pl.ANY)] * len(after),
        out_specs=[per(hidden), per(2 * hidden), fixed(*wide.shape), fixed(*tall.shape)],
        out_shape=[
            jax.ShapeDtypeStruct((rows, hidden), b16),
            jax.ShapeDtypeStruct((rows, 2 * hidden), b16),
            jax.ShapeDtypeStruct(wide.shape, b16),
            jax.ShapeDtypeStruct(tall.shape, b16),
        ],
        scratch_shapes=[pltpu.VMEM(wide.shape, f32), pltpu.VMEM(tall.shape, f32)],
        compiler_params=pltpu.CompilerParams(vmem_limit_bytes=32 << 20),
        cost_estimate=pl.CostEstimate(flops=0, bytes_accessed=1024, transcendentals=0),
    )(x, dy, wide, tall, *after)


def bank_kernel(parity_ref, gate_ref, up_ref, down_ref, out_ref):
    columns = gate_ref.shape[2]
    rows = down_ref.shape[1]
    out_ref[0, 0, :, :columns] = gate_ref[0]
    out_ref[0, 0, :, columns : 2 * columns] = up_ref[0]
    for k in range(3):
        out_ref[0, 0, k * rows : (k + 1) * rows, 2 * columns :] = down_ref[
            0, :, k * columns : (k + 1) * columns
        ]


def bank_rows(parity, gate, up, down):
    local, rows, columns = gate.shape
    half = local // 2
    which = lambda side, e, p: ((p[0] + side) % 2 * half + e, 0, 0)
    block = lambda v: pl.BlockSpec((1,) + v.shape[1:], which)
    return pl.pallas_call(
        bank_kernel,
        grid_spec=pltpu.PrefetchScalarGridSpec(
            num_scalar_prefetch=1,
            grid=(2, half),
            in_specs=[block(gate), block(up), block(down)],
            out_specs=pl.BlockSpec(
                (1, 1, rows, 3 * columns), lambda side, e, p: (side, e, 0, 0)
            ),
        ),
        out_shape=jax.ShapeDtypeStruct((2, half, rows, 3 * columns), b16),
        cost_estimate=pl.CostEstimate(flops=0, bytes_accessed=1024, transcendentals=0),
    )(parity.reshape(1), gate, up, down)


def plain_expert(x, dy, gate, bank, planes):
    width = x.shape[1]
    hidden = bank.shape[1] // 3
    gate_up = bank[:, : 2 * hidden]
    down = bank[:, 2 * hidden :].reshape(planes, 3, hidden // planes, width // 3)
    down = down.transpose(0, 2, 1, 3).reshape(hidden, width)
    pre = dot(x, gate_up)
    soft, slope = silu_parts(pre[:, :hidden])
    lin = pre[:, hidden:]
    hid = (soft * lin).astype(b16)
    made = dot(hid, down).astype(b16).astype(f32)
    dy = dy.astype(f32)
    dmade = (dy * gate).astype(b16)
    dhid = dot_nt(dmade, down)
    dpre = jnp.concatenate([dhid * lin * slope, dhid * soft], axis=1).astype(b16)
    return (
        (made * gate).astype(b16),
        dot_nt(dpre, gate_up).astype(b16),
        jnp.sum(made * dy, axis=1, keepdims=True),
        dot_tn(x, dpre).astype(b16),
        dot_tn(hid, dmade).astype(b16),
    )


class Heads:
    def __init__(self, planes, plane, out_rows, width):
        self.planes, self.plane, self.width = planes, plane, width
        self.each = H // plane
        self.padded = -(-self.each // 2) * 2
        own = 2 * out_rows
        self.owned = own % width == 0 and planes % 2 == 0 and self.padded == self.each
        self.run = own // width if self.owned else self.each

    def group(self, value, size):
        lead = value.shape[:-1]
        if self.owned:
            value = value.reshape(lead + (2, self.planes // 2, self.plane // 2, self.run * size))
            n = len(lead)
            value = jnp.transpose(value, tuple(range(n)) + (n + 2, n, n + 1, n + 3))
        value = value.reshape(lead + (self.plane, self.each * size))
        pad = (self.padded - self.each) * size
        return jnp.pad(value, [(0, 0)] * (len(lead) + 1) + [(0, pad)]) if pad else value

    def ungroup(self, value, size):
        lead = value.shape[:-2]
        value = value[..., : self.each * size]
        if self.owned:
            value = value.reshape(lead + (self.plane // 2, 2, self.planes // 2, self.run * size))
            n = len(lead)
            value = jnp.transpose(value, tuple(range(n)) + (n + 1, n + 2, n, n + 3))
        return value.reshape(lead + (H * size,))


def body(
    block_input,
    out_grad,
    routes,
    norm_in,
    in_proj,
    conv_weight,
    conv_bias,
    step_bias,
    log_rate,
    skip_gain,
    mixer_gain,
    out_proj,
    norm_mid,
    router,
    shared_gate,
    shared_up,
    shared_down,
    expert_gate,
    expert_up,
    expert_down,
):
    both = ("dp", "expert")
    planes, plane = lax.axis_size("dp"), lax.axis_size("expert")
    at = lax.axis_index("expert")
    core = at % 2
    micro, length, width = block_input.shape
    picks = routes.shape[-1]
    local = expert_gate.shape[0]
    experts = local * plane
    sets = 2 if planes == 4 and plane == 8 else 1
    place = lax.axis_index("dp")
    odd = place % 2 == 1
    taken = local // sets
    capacity = 3 * length * picks // (2 * experts)
    slots = -(-capacity // 8) * 8
    tokens = micro * length
    shard = in_proj.shape[0]
    out_rows = out_proj.shape[0]
    inner = out_rows * planes * plane
    hr = shared_down.shape[0]
    fs = hr * planes
    ehidden = expert_gate.shape[2]
    gather = lambda v, axes: lax.all_gather(v, axes, axis=0, tiled=True)
    scatter = lambda v, axes: lax.psum_scatter(v, axes, scatter_dimension=0, tiled=True)
    heads = Heads(planes, plane, out_rows, inner // H)
    size = heads.width
    wide = heads.padded * size
    states = conv_weight.shape[1] - inner
    main = 2 * wide + states + LANES

    signal = in_proj[:, inner : 2 * inner]
    maps = in_proj[:, 2 * inner : 2 * inner + states]
    steps = in_proj[:, 2 * inner + states :]
    common = jnp.concatenate([norm_in[:, None], norm_mid[:, None], router], axis=1)
    spare = LANES - heads.padded - common.shape[1]
    repeat = lambda v: jnp.broadcast_to(v[:, None, :], (shard, plane, v.shape[1]))
    split = lambda v: v.reshape(shard, planes, plane, hr).transpose(0, 2, 1, 3).reshape(shard, plane, fs)
    sent = jnp.concatenate(
        [
            heads.group(in_proj[:, :inner], size),
            heads.group(signal, size),
            repeat(maps),
            heads.group(steps, 1),
            repeat(common),
            jnp.zeros((shard, plane, spare), b16),
            split(shared_gate),
            split(shared_up),
        ],
        axis=2,
    ).transpose(1, 0, 2)
    came = lax.all_to_all(sent, "expert", split_axis=0, concat_axis=0, tiled=True)

    third = width // 3
    part = expert_down.shape[1]
    stacked = lambda v: jnp.concatenate([v[:, k * third : (k + 1) * third] for k in range(3)], axis=0)
    ends, gives = None, []
    if sets == 2:
        ends = [[0, 2], [1, 3]]
        sides = bank_rows((place % 2).astype(jnp.int32), expert_gate, expert_up, expert_down)
        gives = [sides]
    else:
        banks = [
            jnp.concatenate([expert_gate[e], expert_up[e], stacked(expert_down[e])], axis=1)
            for e in range(local)
        ]

    own_routes = jnp.pad(routes.reshape(tokens, picks).astype(b16), ((0, 0), (0, LANES - picks)))
    flat_in = block_input.reshape(tokens, width)
    grad_low = out_grad.reshape(tokens, width)
    flat_in, came = tie(flat_in, came)
    all_in, all_grad, all_routes, *swapped = plane_gather(
        0, flat_in, grad_low, own_routes, sets=(1, sets, sets), swaps=gives
    )
    if sets == 2:
        banks = [v.reshape(-1, v.shape[2]) for v in swapped]
    proj = gather(came.reshape(plane * shard, -1), "dp")
    in_w = proj[:, :main]
    gate_up = proj[:, main:]
    first = 2 * wide + states + heads.padded
    gain_in = proj[:, first].astype(f32)
    gain_mid = proj[:, first + 1].astype(f32)
    route_proj = proj[:, first + 2 : first + 2 + experts]
    all_routes = all_routes[:, :picks].astype(jnp.int32)
    near = all_in.shape[0]
    count = all_grad.shape[0]
    seqs = count // LEN

    out_shard = jnp.concatenate(
        [
            jnp.concatenate([out_proj, mixer_gain[:, None]], axis=1),
            jnp.pad(shared_down, ((0, 0), (0, 1))),
        ],
        axis=0,
    )
    out_shard = jnp.pad(out_shard, ((0, 0), (0, LANES - 1)))
    half = planes // 2
    if heads.owned:
        out_all = gather(out_shard, "dp").reshape(planes, out_rows + hr, -1)
        down_w = out_all[:, out_rows:, :width].reshape(fs, width)
        pieces = out_all[:, :out_rows].reshape(2, half, out_rows, -1)
        low = core == 0
        keep = jnp.where(low, pieces[0], pieces[1])
        other = exchange(jnp.where(low, pieces[1], pieces[0]), "expert", 1)
        out_w = jnp.stack([jnp.where(low, keep, other), jnp.where(low, other, keep)], axis=1)
        out_w = out_w.reshape(wide, -1)
    else:
        down_w = gather(shared_down, "dp")
        out_all = gather(out_shard[:out_rows], both)
        out_w = lax.dynamic_slice_in_dim(out_all, at * heads.each * size, heads.each * size, 0)
        out_w = jnp.pad(out_w, ((0, wide - heads.each * size), (0, 0)))
    gain_mix = out_w[:, width]
    out_w = out_w[:, :width]

    pick_own = lambda v: lax.dynamic_index_in_dim(v, at, v.ndim - 2, keepdims=False)
    lane_pad = lambda v: jnp.pad(v.astype(f32), (0, LANES - v.shape[0])).reshape(1, LANES)
    own_lanes = lambda v: jnp.concatenate(
        [pick_own(heads.group(v[:, :inner], size)), v[:, inner:]], axis=1
    ).astype(f32)
    params = (
        own_lanes(conv_weight),
        own_lanes(conv_bias[None]),
        lane_pad(pick_own(heads.group(step_bias, 1))),
        lane_pad(pick_own(heads.group(log_rate, 1))),
        pick_own(heads.group(jnp.repeat(skip_gain, size), size)).astype(f32).reshape(1, -1),
        gain_mix.astype(f32).reshape(1, -1),
    )

    normed = rms_scale(all_in.astype(f32), gain_in).astype(b16)
    merged = dot(normed, in_w)
    mixed, joined, square = mix_forward(merged, params)
    square = jnp.sum(square, axis=1, keepdims=True)
    square_high = square.astype(b16)
    square_low = (square - square_high.astype(f32)).astype(b16)
    lane = jnp.arange(LANES)[None]
    tail = jnp.where(lane == 2 * at, square_high, jnp.where(lane == 2 * at + 1, square_low, 0))
    summed, squares = plane_scatter(2, dot(mixed, out_w).astype(b16), tail.astype(b16))
    scale = lax.rsqrt(jnp.sum(squares, axis=1, keepdims=True) / inner + epsilon)
    mixer_out = scale * summed
    start = flat_in.astype(f32)
    grad_out = grad_low.astype(f32)
    middle = start + mixer_out
    routed = rms_scale(middle, gain_mid).astype(b16)
    whole = [
        lax.all_gather(banks[e], "dp", axis=0, tiled=True, axis_index_groups=ends)
        for e in range(taken)
    ]
    if sets == 2:
        routed, whole[0] = tie(routed, whole[0])
    (all_routed,) = plane_gather(3, routed, sets=sets)

    lowest = at * local + (place % sets) * taken
    mine = lowest + jnp.arange(taken, dtype=jnp.int32)
    marks = jnp.any(all_routes[:, :, None] == mine, axis=1).reshape(seqs, LEN, taken)
    earlier = jnp.arange(LEN)[:, None] > jnp.arange(LEN)[None, :]
    rank = jnp.einsum(
        "ts,nse->net", earlier.astype(b16), marks.astype(b16), preferred_element_type=f32
    ).astype(jnp.int32)
    places = jnp.arange(slots, dtype=jnp.int32)
    chosen = (rank[:, :, None, :] == places[None, None, :, None]) & (
        marks.transpose(0, 2, 1)[:, :, None, :]
    )
    select = chosen.astype(b16)
    gates_all = dense_gates(dot(all_routed, route_proj), all_routes)
    gates_mine = lax.dynamic_slice_in_dim(gates_all, lowest, taken, axis=1)
    gates_mine = gates_mine.reshape(seqs, LEN, taken).transpose(0, 2, 1)
    slot_gates = jnp.sum(jnp.where(chosen, gates_mine[:, :, None, :], 0.0), axis=-1)

    select = select.reshape(seqs, taken * slots, LEN)
    rows_in = spread(select, all_routed, taken)
    rows_grad = spread(select, all_grad, taken)
    outs, backs, dgates, sums = [], [], [], []
    tied = []
    for e in range(taken):
        gate = slot_gates[:, e].reshape(seqs * slots, 1)
        if sets == 2:
            out, grad, dgate, *made_grads = expert(
                rows_in[e], rows_grad[e], gate, whole[e], ehidden, after=tied
            )
        else:
            out, grad, dgate, *made_grads = plain_expert(
                rows_in[e], rows_grad[e], gate, whole[e], planes
            )
        outs.append(out)
        backs.append(grad)
        dgates.append(dgate.reshape(seqs, slots))
        sums.append(
            [
                lax.psum_scatter(
                    v, "dp", scatter_dimension=0, tiled=True, axis_index_groups=ends
                )
                for v in made_grads
            ]
        )
        if e == 0:
            hid, dpre, shared_grad, down_grad = shared_expert(
                all_routed, all_grad, gate_up, down_w, near, after=made_grads
            )
            tied = [hid, dpre, shared_grad, down_grad]
    dgate_rows = jnp.sum(
        jnp.where(chosen, jnp.stack(dgates, axis=1)[:, :, :, None], 0.0), axis=2
    ).transpose(0, 2, 1)
    dgate_wide = lax.dynamic_update_slice_in_dim(
        jnp.zeros((count, experts), f32), dgate_rows.reshape(count, taken), lowest, axis=1
    )
    high = dgate_wide.astype(b16)
    fine = (dgate_wide - high.astype(f32)).astype(b16)
    fill = jnp.zeros((count, -(2 * experts) % LANES), b16)
    back_part = merge(select, backs, dpre, gate_up.T)
    back, back_gates = plane_scatter(
        4, back_part, jnp.concatenate([high, fine, fill], axis=1), sets=sets, after=made_grads
    )

    gates = dense_gates(dot(routed, route_proj), routes.reshape(tokens, picks))
    dgate = back_gates[:, :experts] + back_gates[:, experts : 2 * experts]
    dlogits = (gates * (dgate - jnp.sum(gates * dgate, axis=1, keepdims=True))).astype(b16)
    droute = back + dot_nt(dlogits, route_proj)
    dmid_part, mid_gain_grad = rms_back(middle, gain_mid, droute)
    dmid = grad_out + dmid_part

    def small_rows(weight_grad, bias_grad, skip_grad, head_grad):
        spot = lambda v, size: heads.ungroup(
            lax.dynamic_update_slice_in_dim(
                jnp.zeros(v.shape[:-1] + (plane, v.shape[-1]), f32), v[..., None, :], at, v.ndim - 1
            ),
            size,
        )
        taps = jnp.concatenate([weight_grad, bias_grad], axis=0)
        taps = jnp.concatenate([spot(taps[:, :wide], size), taps[:, wide:]], axis=1)
        skip_grad = jnp.sum(skip_grad.reshape(heads.padded, size), axis=1)
        head_rows = jnp.concatenate([head_grad[:2, : heads.padded], skip_grad[None]], axis=0)
        head_rows = spot(head_rows, 1).reshape(1, -1)
        head_rows = jnp.pad(head_rows, ((0, 0), (0, taps.shape[1] - head_rows.shape[1])))
        rows = jnp.concatenate([taps, head_rows], axis=0)
        return jnp.pad(rows, ((0, 16 - rows.shape[0]), (0, 0)))

    def owners(grad):
        grad = scatter(grad.astype(b16), "dp").reshape(plane, shard, -1)
        return lax.all_to_all(grad, "expert", split_axis=0, concat_axis=0, tiled=True).astype(f32)

    scaled = (dmid * scale).astype(b16)
    inward = scale * jnp.sum(scaled.astype(f32) * mixer_out, axis=1, keepdims=True) / inner
    inward_high = inward.astype(b16)
    inward_low = (inward - inward_high.astype(f32)).astype(b16)
    tail = jnp.where(lane == 0, inward_high, jnp.where(lane == 1, inward_low, 0)).astype(b16)
    shared_rows = owners(shared_grad)
    all_mid, all_inward = plane_gather(6, scaled, tail, after=sums[0])
    kept, sent = [], []
    if sets == 2:
        for group in sums:
            for v in group:
                rows = v.shape[0] // 2
                kept.append(jnp.where(odd, v[rows:], v[:rows]))
                sent.append(jnp.where(odd, v[:rows], v[rows:]))
    swapped = [exchange(v, "dp", 1) for v in sent]
    all_inward = all_inward[:, :1].astype(f32) + all_inward[:, 1:2].astype(f32)
    dmerged, weight_grad, bias_grad, skip_grad, head_grad = mix_backward(
        merged, joined, dot_nt(all_mid, out_w), all_inward, params
    )
    taps_of = small_rows(weight_grad, bias_grad, skip_grad, head_grad)
    dnormed, taps_of = plane_scatter(
        7,
        dot_nt(dmerged, in_w).astype(b16),
        gathers=[taps_of],
        after=[shared_rows],
    )
    taps_of = jnp.sum(taps_of, axis=0)
    out_part = merge(select, outs, hid, down_w, after=[dnormed])
    out_part, dnormed = tie(out_part, dnormed)
    out_sum, small = plane_scatter(5, out_part, sets=sets, lines=[taps_of], after=swapped)
    small = jnp.sum(small, axis=0)

    shared_grad = shared_rows
    unsplit = lambda v: (
        v.reshape(plane, shard, planes, hr).transpose(1, 2, 0, 3).reshape(shard, planes * plane * hr)
    )
    out_w_grad = dot_tn(mixed, all_mid).astype(b16)
    if heads.owned:
        parts = out_w_grad.reshape(half, 2, out_rows, width)
        keep = jnp.where(low, parts[:, 0], parts[:, 1])
        other = exchange(jnp.where(low, parts[:, 1], parts[:, 0]), "expert", 1)
        out_parts = jnp.concatenate([jnp.where(low, keep, other), jnp.where(low, other, keep)])
        rows = jnp.concatenate([out_parts, down_grad.reshape(planes, hr, width)], axis=1)
        rows = scatter(rows.reshape(planes * (out_rows + hr), width), "dp").astype(f32)
        out_w_grad, down_grad = rows[:out_rows], rows[out_rows:]
    else:
        rows = lax.dynamic_update_slice_in_dim(
            jnp.zeros((inner, width), b16), out_w_grad[: heads.each * size], at * heads.each * size, 0
        )
        out_w_grad = scatter(rows, both).astype(f32)
        down_grad = scatter(down_grad, "dp").astype(f32)

    extra = jnp.concatenate(
        [
            jnp.zeros((width, heads.padded + 1), f32),
            mid_gain_grad[:, None],
            dot_tn(routed, dlogits),
            jnp.zeros((width, spare), f32),
        ],
        axis=1,
    )
    in_w_grad = dot_tn(normed, dmerged)
    in_w_grad = jnp.concatenate([in_w_grad[:, :-LANES], in_w_grad[:, -LANES:] + extra], axis=1)
    in_w_grad = owners(in_w_grad)
    by_row = in_w_grad.transpose(1, 0, 2)
    step_part = 2 * wide + states
    in_grad = jnp.concatenate(
        [
            heads.ungroup(by_row[:, :, :wide], size),
            heads.ungroup(by_row[:, :, wide : 2 * wide], size),
            jnp.sum(by_row[:, :, 2 * wide : step_part], axis=1),
            heads.ungroup(by_row[:, :, step_part : step_part + heads.padded], 1),
        ],
        axis=1,
    )
    shared_common = jnp.sum(by_row[:, :, first:], axis=1)
    gain_in_grad = jnp.sum(in_proj.astype(f32) * in_grad, axis=1) / norm_in.astype(f32)
    gain_mix_grad = jnp.sum(out_proj.astype(f32) * out_w_grad, axis=1) / mixer_gain.astype(f32)

    bank_grads = []
    for e in range(taken):
        if sets == 1:
            bank_grads.append([v.astype(f32) for v in sums[e]])
            continue
        pair = [
            (jnp.where(odd, came, keep), jnp.where(odd, keep, came))
            for keep, came in zip(kept[2 * e : 2 * e + 2], swapped[2 * e : 2 * e + 2])
        ]
        bank_grads.append([v.astype(f32) for v, _ in pair])
        bank_grads.append([v.astype(f32) for _, v in pair])
    bank_grads = bank_grads[::2] + bank_grads[1::2] if sets == 2 else bank_grads
    dstart, unused = rms_back(start, gain_in, dnormed)
    shape = block_input.shape
    return (
        (middle + out_sum).astype(b16).reshape(shape),
        (dmid + dstart).reshape(shape),
        gain_in_grad,
        in_grad,
        small[:4],
        small[4],
        small[5, :H],
        small[5, H : 2 * H],
        small[5, 2 * H : 3 * H],
        gain_mix_grad,
        out_w_grad,
        shared_common[:, 1],
        shared_common[:, 2 : 2 + experts],
        unsplit(shared_grad[:, :, :fs].transpose(0, 1, 2)),
        unsplit(shared_grad[:, :, fs:]),
        down_grad,
        jnp.stack([v[:, :ehidden] for v, _ in bank_grads]),
        jnp.stack([v[:, ehidden:] for v, _ in bank_grads]),
        jnp.stack([v for _, v in bank_grads]),
    )


def solution(mesh):
    both = ("dp", "expert")
    rows, matrix, bank = P(both), P(both, None), P("expert", "dp", None)
    token = P(None, both, None)
    in_specs = (token, token, token, rows, matrix, P(), P(), P(), P(), P(), rows, matrix, rows)
    in_specs = in_specs + (matrix, matrix, matrix, matrix, bank, bank, bank)
    out_specs = (token, token, rows, matrix, P(), P(), P(), P(), P(), rows, matrix, rows)
    out_specs = out_specs + (matrix, matrix, matrix, matrix, bank, bank, bank)
    return jax.shard_map(body, mesh=mesh, in_specs=in_specs, out_specs=out_specs, check_vma=False)
```

```python
from functools import partial

import jax
import jax.numpy as jnp
from jax import lax
from jax.experimental import pallas as pl
from jax.experimental.pallas import tpu as pltpu
from jax.sharding import PartitionSpec as P

H = 48
LEN = 128
LANES = 128
epsilon = 1e-05
f32 = jnp.float32
b16 = jnp.bfloat16
highest = lax.Precision.HIGHEST
NT = (((1,), (1,)), ((), ()))


def sigmoid(value):
    return 0.5 * jnp.tanh(0.5 * value) + 0.5


def grids():
    row = lax.broadcasted_iota(jnp.int32, (LEN, LANES), 0)
    lane = lax.broadcasted_iota(jnp.int32, (LEN, LANES), 1)
    return row, lane


def shifted(signal, row):
    return [signal] + [jnp.where(row >= k, pltpu.roll(signal, k, 0), 0.0) for k in (1, 2, 3)]


def convolved(parts, weight_ref, bias_ref, block):
    weight = weight_ref[:, block]
    total = bias_ref[:, block] + weight[3:4] * parts[0]
    for k in (1, 2, 3):
        total = total + weight[3 - k : 4 - k] * parts[k]
    return total


def pick(value, lane):
    low = lane < LANES // 2
    return jnp.concatenate([jnp.where(low, value, 0.0), jnp.where(low, 0.0, value)], axis=0)


def step_terms(merged_ref, step_ref, rate_ref, tail):
    raw = merged_ref[:, tail] + step_ref[...]
    step = jnp.maximum(raw, 0.0) + jnp.log1p(jnp.exp(-jnp.abs(raw)))
    decay = -jnp.exp(rate_ref[...]) * step
    row, lane = grids()
    cumul = jnp.dot(
        (row >= lane).astype(f32), decay, precision=highest, preferred_element_type=f32
    )
    return raw, step, decay, cumul


def forward_kernel(
    pairs,
    merged_ref,
    weight_ref,
    bias_ref,
    step_ref,
    rate_ref,
    skip_ref,
    gain_ref,
    mixed_ref,
    joined_ref,
    square_ref,
    cross_ref,
):
    row, lane = grids()
    tail = pl.ds((2 * pairs + 2) * LANES, LANES)
    raw, step, decay, cumul = step_terms(merged_ref, step_ref, rate_ref, tail)
    cross_ref[...] = cumul.T
    maps = []
    for at in (0, 1):
        signal = merged_ref[:, pl.ds((2 * pairs + at) * LANES, LANES)]
        block = pl.ds((pairs + at) * LANES, LANES)
        conv = convolved(shifted(signal, row), weight_ref, bias_ref, block)
        maps.append((conv * sigmoid(conv)).astype(b16))
    inner = lax.dot_general(maps[1], maps[0], NT, preferred_element_type=f32)
    square = jnp.zeros((LEN, LANES), f32)
    for pair in range(pairs):
        block = pl.ds(pair * LANES, LANES)
        signal = merged_ref[:, pl.ds((pairs + pair) * LANES, LANES)]
        conv = convolved(shifted(signal, row), weight_ref, bias_ref, block)
        values = conv * sigmoid(conv)
        steps, parts = [], []
        for head in (2 * pair, 2 * pair + 1):
            steps.append(step[:, head : head + 1])
            spread = cumul[:, head : head + 1] - cross_ref[head : head + 1, :]
            parts.append(inner * jnp.exp(jnp.where(row >= lane, spread, -1e30)))
        scaled = values * jnp.where(lane < LANES // 2, steps[0], steps[1])
        scanned = jnp.dot(
            jnp.concatenate(parts, axis=1).astype(b16),
            pick(scaled, lane).astype(b16),
            preferred_element_type=f32,
        )
        joined = scanned + skip_ref[:, block] * values
        joined_ref[:, block] = joined
        gate = merged_ref[:, block]
        gated = joined * (gate * sigmoid(gate))
        mixed_ref[:, block] = (gated * gain_ref[:, block]).astype(b16)
        square = square + gated * gated
    square_ref[...] = square


def backward_kernel(
    pairs,
    merged_ref,
    joined_ref,
    grad_ref,
    inward_ref,
    weight_ref,
    bias_ref,
    step_ref,
    rate_ref,
    skip_ref,
    gain_ref,
    out_ref,
    weight_out,
    bias_out,
    skip_out,
    head_out,
    cross_ref,
):
    row, lane = grids()
    low = lane < LANES // 2

    @pl.when(pl.program_id(0) == 0)
    def _():
        weight_out[...] = jnp.zeros_like(weight_out)
        bias_out[...] = jnp.zeros_like(bias_out)
        skip_out[...] = jnp.zeros_like(skip_out)
        head_out[...] = jnp.zeros_like(head_out)

    inward = inward_ref[...]
    tail = pl.ds((2 * pairs + 2) * LANES, LANES)
    raw, step, decay, cumul = step_terms(merged_ref, step_ref, rate_ref, tail)
    cross_ref[...] = cumul.T
    convs, slopes, shifts, maps = [], [], [], []
    for at in (0, 1):
        signal = merged_ref[:, pl.ds((2 * pairs + at) * LANES, LANES)]
        parts = shifted(signal, row)
        conv = convolved(parts, weight_ref, bias_ref, pl.ds((pairs + at) * LANES, LANES))
        sigma = sigmoid(conv)
        shifts.append(parts)
        slopes.append(sigma * (1.0 + conv * (1.0 - sigma)))
        maps.append((conv * sigma).astype(b16))
    flipped = lax.dot_general(maps[0], maps[1], NT, preferred_element_type=f32)
    dinner = jnp.zeros((LEN, LEN), f32)
    dstep = jnp.zeros((LEN, LANES), f32)
    dcum = jnp.zeros((LEN, LANES), f32)

    def back_conv(grad, parts, block, out_block):
        bias_out[:, block] += jnp.sum(grad, axis=0, keepdims=True)
        weight = weight_ref[:, block]
        total = weight[3:4] * grad
        taps = [jnp.sum(grad * parts[3 - k], axis=0, keepdims=True) for k in range(4)]
        weight_out[:, block] += jnp.concatenate(taps, axis=0)
        for k in (1, 2, 3):
            later = jnp.where(row < LEN - k, pltpu.roll(grad, LEN - k, 0), 0.0)
            total = total + weight[3 - k : 4 - k] * later
        out_ref[:, out_block] = total.astype(b16)

    for pair in range(pairs):
        block = pl.ds(pair * LANES, LANES)
        other = pl.ds((pairs + pair) * LANES, LANES)
        gate = merged_ref[:, block]
        joined = joined_ref[:, block]
        sigma = sigmoid(gate)
        soft = gate * sigma
        dgated = grad_ref[:, block] * gain_ref[:, block] - joined * soft * inward
        djoined = dgated * soft
        out_ref[:, block] = (dgated * joined * (sigma + soft * (1.0 - sigma))).astype(b16)

        parts = shifted(merged_ref[:, other], row)
        conv = convolved(parts, weight_ref, bias_ref, block)
        csig = sigmoid(conv)
        values = conv * csig
        skip = skip_ref[:, block]
        skip_out[:, block] += jnp.sum(djoined * values, axis=0, keepdims=True)
        scanned = joined - skip * values
        steps, blends, spreads = [], [], []
        for head in (2 * pair, 2 * pair + 1):
            steps.append(step[:, head : head + 1])
            spread = cumul[:, head : head + 1] - cross_ref[head : head + 1, :]
            spreads.append(jnp.exp(jnp.where(row >= lane, spread, -1e30)))
            blends.append(flipped * jnp.exp(jnp.where(row <= lane, -spread, -1e30)))
        widened = jnp.where(low, steps[0], steps[1])
        scaled = (values * widened).astype(b16)
        dlow = djoined.astype(b16)
        both = pick(djoined, lane).astype(b16)
        dweights = lax.dot_general(both, scaled, NT, preferred_element_type=f32)
        dinner = dinner + dweights[:LEN] * spreads[0] + dweights[LEN:] * spreads[1]
        dscaled = jnp.dot(
            jnp.concatenate(blends, axis=1).astype(b16), both, preferred_element_type=f32
        )
        dvalues = skip * djoined + dscaled * widened
        first = dscaled * values
        second = dlow.astype(f32) * scanned - scaled.astype(f32) * dscaled
        for at in (0, 1):
            mine = low if at == 0 else jnp.logical_not(low)
            here = lane == 2 * pair + at
            total = jnp.sum(jnp.where(mine, first, 0.0), axis=1, keepdims=True)
            dstep = jnp.where(here, total, dstep)
            total = jnp.sum(jnp.where(mine, second, 0.0), axis=1, keepdims=True)
            dcum = jnp.where(here, total, dcum)
        back_conv(dvalues * (csig * (1.0 + conv * (1.0 - csig))), parts, block, other)
    dmaps = (
        jnp.dot(dinner.T.astype(b16), maps[1], preferred_element_type=f32),
        jnp.dot(dinner.astype(b16), maps[0], preferred_element_type=f32),
    )
    for at in (0, 1):
        back_conv(
            dmaps[at] * slopes[at],
            shifts[at],
            pl.ds((pairs + at) * LANES, LANES),
            pl.ds((2 * pairs + at) * LANES, LANES),
        )
    ddecay = jnp.dot(
        (row <= lane).astype(f32), dcum, precision=highest, preferred_element_type=f32
    )
    dstep = dstep - ddecay * jnp.exp(rate_ref[...])
    draw = jnp.where(lane < 2 * pairs, dstep * sigmoid(raw), 0.0)
    out_ref[:, tail] = draw.astype(b16)
    head_out[0:1, :] += jnp.sum(draw, axis=0, keepdims=True)
    head_out[1:2, :] += jnp.sum(ddecay * decay, axis=0, keepdims=True)


def rows_of(columns):
    return pl.BlockSpec((LEN, columns), lambda s: (s, 0))


def fixed(rows, columns):
    return pl.BlockSpec((rows, columns), lambda s: (0, 0))


def mix_forward(merged, params):
    tokens, columns = merged.shape
    width = params[-1].shape[1]
    return pl.pallas_call(
        partial(forward_kernel, width // LANES),
        grid=(tokens // LEN,),
        in_specs=[rows_of(columns)] + [fixed(*p.shape) for p in params],
        out_specs=[rows_of(width), rows_of(width), rows_of(LANES)],
        out_shape=[
            jax.ShapeDtypeStruct((tokens, width), b16),
            jax.ShapeDtypeStruct((tokens, width), f32),
            jax.ShapeDtypeStruct((tokens, LANES), f32),
        ],
        scratch_shapes=[pltpu.VMEM((LANES, LEN), f32)],
        compiler_params=pltpu.CompilerParams(vmem_limit_bytes=32 << 20),
        cost_estimate=pl.CostEstimate(flops=0, bytes_accessed=1024, transcendentals=0),
    )(merged, *params)


def mix_backward(merged, joined, grad, inward, params):
    tokens, columns = merged.shape
    width = params[-1].shape[1]
    conv = params[0].shape[1]
    return pl.pallas_call(
        partial(backward_kernel, width // LANES),
        grid=(tokens // LEN,),
        in_specs=[rows_of(columns), rows_of(width), rows_of(width), rows_of(1)]
        + [fixed(*p.shape) for p in params],
        out_specs=[
            rows_of(columns),
            fixed(4, conv),
            fixed(1, conv),
            fixed(1, width),
            fixed(8, LANES),
        ],
        out_shape=[
            jax.ShapeDtypeStruct((tokens, columns), b16),
            jax.ShapeDtypeStruct((4, conv), f32),
            jax.ShapeDtypeStruct((1, conv), f32),
            jax.ShapeDtypeStruct((1, width), f32),
            jax.ShapeDtypeStruct((8, LANES), f32),
        ],
        scratch_shapes=[pltpu.VMEM((LANES, LEN), f32)],
        compiler_params=pltpu.CompilerParams(vmem_limit_bytes=32 << 20),
        cost_estimate=pl.CostEstimate(flops=0, bytes_accessed=1024, transcendentals=0),
    )(merged, joined, grad, inward, *params)


MESH = pl.DeviceIdType.MESH


def neighbours(me):
    core, column, line = me % 2, (me // 2) % 2, me // 4
    return 1 - 2 * core, 2 - 4 * column, 4 - 8 * line


def other_plane(me):
    place = lax.axis_index("dp")
    return {"dp": place + 1 - 2 * (place % 2), "expert": me}


def greet(peers):
    barrier = pltpu.get_barrier_semaphore()
    for peer in peers:
        pl.semaphore_signal(barrier, inc=1, device_id=peer, device_id_type=MESH)
    pl.semaphore_wait(barrier, len(peers))


def far_plane(me):
    place = lax.axis_index("dp")
    return {"dp": place + 2 - 4 * (place // 2), "expert": me}


def peers_of(me, across, along=0):
    core, column, line = neighbours(me)
    peers = [{"expert": me + core}, {"expert": me + column}, {"expert": me + line}]
    peers = peers + ([other_plane(me)] if across else [])
    return peers + ([far_plane(me)] if along else [])


def begin_swaps(refs, swaps, first, send_sem, recv_sem, peer):
    found = []
    for i in range(swaps):
        found.append(remote(send_sem, recv_sem, first + i, refs[i], refs[swaps + i], peer[0]))
        found[-1].start()
    return found


def remote(send_sem, recv_sem, at, src, dst, peer):
    return pltpu.make_async_remote_copy(
        src_ref=src,
        dst_ref=dst,
        send_sem=send_sem.at[at],
        recv_sem=recv_sem.at[at],
        device_id=peer,
        device_id_type=MESH,
    )


def gather_kernel(sets, count, swaps, lines, waits, *refs):
    owns, sides, block = refs[:count], refs[count : count + swaps], refs[count + swaps :][:lines]
    refs = refs[count + swaps + lines + waits :]
    shares = swaps * (sides[0].shape[1] if swaps else 0)
    total = count + shares + lines
    outs, take, line_out = refs[:count], refs[count : count + shares], refs[count + shares : total]
    send_sem, recv_sem, copy_sem = refs[total:]
    me = lax.axis_index("expert")
    core, column, line = neighbours(me)
    half = owns[0].shape[0] // 2
    top, bottom = pl.ds(0, half), pl.ds(half, half)
    peers = peers_of(me, max(sets) == 2 or swaps or lines, lines)
    greet(peers)
    copy = partial(remote, send_sem, recv_sem)
    arrays = range(count)
    place = lax.axis_index("dp")
    distant = place + 2 - 4 * (place // 2)
    along = []
    for i in range(lines):
        base = 17 * count + shares + 3 * i
        own, out = block[i], line_out[i]
        along.append(
            (
                pltpu.make_async_copy(own, out.at[place], copy_sem.at[count + i]),
                copy(base, own, out.at[place], peers[4]),
                copy(base + 1, own, out.at[place], peers[3]),
                copy(base + 2, out.at[distant], out.at[distant], peers[3]),
            )
        )
    steps = []
    here, across = [], []
    for i in arrays:
        here.append(pltpu.make_async_copy(owns[i], outs[i].at[me], copy_sem.at[i]))
        if sets[i] == 2:
            across.append(copy(17 * i + 16, owns[i], outs[i].at[8 + me], peers[3]))
    for g in range(2):
        for i in arrays:
            if sets[i] <= g:
                continue
            out = lambda at: outs[i].at[8 * g + at]
            own = owns[i] if g == 0 else out(me)
            at_x, at_y, at_d = out(me + column), out(me + line), out(me + column + line)
            base = 17 * i + 8 * g
            steps.append(
                (
                    copy(base, own, out(me), peers[1]),
                    copy(base + 1, own, out(me), peers[2]),
                    copy(base + 2, own, out(me), peers[0]),
                    copy(base + 3, at_x.at[top], at_x.at[top], peers[2]),
                    copy(base + 4, at_y.at[bottom], at_y.at[bottom], peers[1]),
                    copy(base + 5, at_x, at_x, peers[0]),
                    copy(base + 6, at_y, at_y, peers[0]),
                    copy(base + 7, at_d, at_d, peers[0]),
                )
            )

    def begin(group):
        for to_x, to_y, to_core, *unused in group:
            to_x.start()
            to_y.start()
            to_core.start()

    def relay(group):
        for to_x, to_y, to_core, x_relay, y_relay, x_core, y_core, d_core in group:
            to_x.wait_recv()
            x_relay.start()
            x_core.start()
            to_y.wait_recv()
            y_relay.start()
            y_core.start()

    def close(group):
        for to_x, to_y, to_core, x_relay, y_relay, x_core, y_core, d_core in group:
            x_relay.wait_recv()
            y_relay.wait_recv()
            d_core.start()

    first, second = steps[:count], steps[count:]
    for here_block, to_far, to_near, relayed in along:
        to_far.start()
        to_near.start()
        here_block.start()
    for copied in across:
        copied.start()
    begin(first)
    swapped = []
    for i in range(shares):
        mine = take[i].at[place % 2]
        here.append(pltpu.make_async_copy(sides[0].at[0, i], mine, copy_sem.at[count + lines + i]))
        swapped.append(copy(17 * count + i, sides[0].at[1, i], mine, peers[3]))
        swapped[-1].start()
    for here_block, to_far, to_near, relayed in along:
        to_far.wait_recv()
        relayed.start()
    for copied in here:
        copied.start()
    for copied in across:
        copied.wait_recv()
    begin(second)
    relay(first)
    close(first)
    relay(second)
    close(second)
    for copied in here:
        copied.wait()
    for copied in across:
        copied.wait_send()
    for copied in swapped:
        copied.wait()
    for here_block, to_far, to_near, relayed in along:
        here_block.wait()
        to_near.wait_recv()
        relayed.wait_recv()
        for copied in (to_far, to_near, relayed):
            copied.wait_send()
    for group in steps:
        for at in (2, 5, 6, 7):
            group[at].wait_recv()
        for sent in group:
            sent.wait_send()


def plane_gather(number, *owns, sets=1, swaps=(), lines=(), after=()):
    if lax.axis_size("expert") != 8 or (lines and lax.axis_size("dp") != 4):
        return [lax.all_gather(own, "expert", axis=0, tiled=True) for own in owns] + [
            lax.all_gather(line, "dp", axis=0, tiled=True) for line in lines
        ]
    count = len(owns)
    sets = (sets,) * count if isinstance(sets, int) else sets
    shares = [v for side in swaps for v in [side.shape[2:]] * side.shape[1]]
    total = count + len(shares) + len(lines)
    sems = 17 * count + len(shares) + 3 * len(lines)
    anywhere = pl.BlockSpec(memory_space=pl.ANY)
    outs = pl.pallas_call(
        partial(gather_kernel, sets, count, len(swaps), len(lines), len(after)),
        out_shape=[
            jax.ShapeDtypeStruct((8 * n,) + own.shape, own.dtype) for n, own in zip(sets, owns)
        ]
        + [jax.ShapeDtypeStruct((2,) + v, b16) for v in shares]
        + [jax.ShapeDtypeStruct((4,) + v.shape, v.dtype) for v in lines],
        in_specs=[anywhere] * (count + len(swaps) + len(lines) + len(after)),
        out_specs=[anywhere] * total,
        scratch_shapes=[
            pltpu.SemaphoreType.DMA((sems,)),
            pltpu.SemaphoreType.DMA((sems,)),
            pltpu.SemaphoreType.DMA((count + len(lines) + len(shares),)),
        ],
        compiler_params=pltpu.CompilerParams(collective_id=number, has_side_effects=True),
        cost_estimate=pl.CostEstimate(flops=0, bytes_accessed=1024, transcendentals=0),
    )(*owns, *swaps, *lines, *after)
    gathered = [out.reshape(-1, out.shape[2]) for out in outs[:count]]
    spread = [out.reshape(4 * out.shape[1], out.shape[2]) for out in outs[total - len(lines) :]]
    return gathered + list(outs[count : total - len(lines)]) + spread


def scatter_kernel(sets, count, extra, gathers, lines, waits, *refs):
    parts, give = refs[:count], refs[count : count + extra]
    refs = refs[count + extra :]
    owns, blocks = refs[:gathers], refs[gathers : gathers + lines]
    refs = refs[gathers + lines + waits :]
    outs, take = refs[:count], refs[count : count + extra]
    refs = refs[count + extra :]
    gathered, line_outs = refs[:gathers], refs[gathers : gathers + lines]
    refs = refs[gathers + lines :]
    per = 6 * sets + (3 if sets == 2 else 0)
    held = [refs[per * i : per * (i + 1)] for i in range(count)]
    send_sem, recv_sem, copy_sem = refs[per * count :]
    me = lax.axis_index("expert")
    core, column, line = neighbours(me)
    rows = outs[0].shape[0]
    half = rows // 2
    top, bottom = pl.ds(0, half), pl.ds(half, half)
    peers = peers_of(me, sets == 2 or extra or lines, lines)
    greet(peers)
    copy = partial(remote, send_sem, recv_sem)
    arrays = range(count)
    chips = (me + column + line, me + column, me + line, me)
    order = range(sets - 1, -1, -1)
    keep = lambda g, i, at: held[i][6 * g + at]
    total_ref = lambda g, i: outs[i] if g == 0 else held[i][12]
    swaps, loads = {}, {}
    for g in order:
        for k in range(4):
            for i in arrays:
                base = 21 * i + 10 * g + k
                swaps[g, i, k] = copy(
                    base, parts[i].at[8 * g + chips[k] + core], keep(g, i, 1).at[k], peers[0]
                )
                loads[g, i, k] = pltpu.make_async_copy(
                    parts[i].at[8 * g + chips[k]],
                    keep(g, i, 0).at[k],
                    copy_sem.at[8 * i + 4 * g + k],
                )
                swaps[g, i, k].start()
                loads[g, i, k].start()

    swapped = begin_swaps(give + take, extra, 21 * count, send_sem, recv_sem, peers[3:4])
    base = 21 * count + extra
    place = lax.axis_index("dp")
    distant = place + 2 - 4 * (place // 2)
    here, small, along = [], [], []
    for i in range(gathers):
        own, out = owns[i], lambda at: gathered[i].at[at]
        at_x, at_y, at_d = out(me + column), out(me + line), out(me + column + line)
        low, high = pl.ds(0, own.shape[0] // 2), pl.ds(own.shape[0] // 2, own.shape[0] // 2)
        here.append(pltpu.make_async_copy(own, out(me), copy_sem.at[8 * count + i]))
        small.append(
            (
                copy(base, own, out(me), peers[1]),
                copy(base + 1, own, out(me), peers[2]),
                copy(base + 2, own, out(me), peers[0]),
                copy(base + 3, at_x.at[low], at_x.at[low], peers[2]),
                copy(base + 4, at_y.at[high], at_y.at[high], peers[1]),
                copy(base + 5, at_x, at_x, peers[0]),
                copy(base + 6, at_y, at_y, peers[0]),
                copy(base + 7, at_d, at_d, peers[0]),
            )
        )
        base += 8
        for begun in [here[-1]] + list(small[-1][:3]):
            begun.start()
    for i in range(lines):
        own, out = blocks[i], line_outs[i]
        here.append(pltpu.make_async_copy(own, out.at[place], copy_sem.at[8 * count + gathers + i]))
        along.append(
            (
                copy(base, own, out.at[place], peers[4]),
                copy(base + 1, own, out.at[place], peers[3]),
                copy(base + 2, out.at[distant], out.at[distant], peers[3]),
            )
        )
        base += 3
        for begun in [here[-1]] + list(along[-1][:2]):
            begun.start()

    def each(first, amount, step):
        def body(at, carry):
            step(pl.ds(pl.multiple_of(first + at * 16, 16), 16))
            return carry

        lax.fori_loop(0, amount // 16, body, 0)

    def pair_sum(g, k):
        for i in arrays:
            loads[g, i, k].wait()
            swaps[g, i, k].wait_recv()

        def step(block):
            for i in arrays:
                mine, theirs = keep(g, i, 0), keep(g, i, 1)
                total = mine[k, block].astype(f32) + theirs[k, block].astype(f32)
                if k == 3:
                    total_ref(g, i)[block, :] = total
                else:
                    mine[k, block] = total.astype(b16)

        each(0, rows, step)

    sent = []

    def sends(g, at, k, area, into, peer):
        found = []
        for i in arrays:
            target = keep(g, i, into)
            target = target if into > 3 else target.at[area]
            source = keep(g, i, 0).at[k, area]
            found.append(copy(21 * i + 10 * g + at, source, target, peer))
            found[-1].start()
        sent.extend(found)
        return found

    legs = {}

    def begin_legs(g, summed):
        for k in range(4):
            if not summed:
                pair_sum(g, k)
            if k == 0:
                legs[g] = [
                    sends(g, 4, 0, top, 4, peers[1]),
                    sends(g, 5, 0, bottom, 5, peers[2]),
                ]
            elif k == 1:
                legs[g].append(sends(g, 6, 1, top, 2, peers[1]))
            elif k == 2:
                legs[g].append(sends(g, 7, 2, bottom, 3, peers[2]))

    def second_legs(g):
        d_x, d_y, x_top, y_bottom = legs[g]
        for i in arrays:
            d_x[i].wait_recv()

        def add_y(block):
            for i in arrays:
                mine, extra = keep(g, i, 0), keep(g, i, 4)
                mine[2, block] = (
                    mine[2, block].astype(f32) + extra[block, :].astype(f32)
                ).astype(b16)

        each(0, half, add_y)
        y_top = sends(g, 8, 2, top, 3, peers[2])
        for i in arrays:
            d_y[i].wait_recv()

        def add_x(block):
            low = pl.ds(pl.multiple_of(block.start - half, 16), 16)
            for i in arrays:
                mine, extra = keep(g, i, 0), keep(g, i, 5)
                mine[1, block] = (
                    mine[1, block].astype(f32) + extra[low, :].astype(f32)
                ).astype(b16)

        each(half, half, add_x)
        x_bottom = sends(g, 9, 1, bottom, 2, peers[1])
        legs[g] = [x_top, y_bottom, y_top, x_bottom]

    begin_legs(sets - 1, False)
    if sets == 2:
        for k in range(4):
            pair_sum(0, k)
    for to_x, to_y, to_core, x_relay, y_relay, x_core, y_core, d_core in small:
        to_x.wait_recv()
        x_relay.start()
        x_core.start()
        to_y.wait_recv()
        y_relay.start()
        y_core.start()
    for to_far, to_near, relayed in along:
        to_far.wait_recv()
        relayed.start()
    second_legs(sets - 1)
    if sets == 2:
        begin_legs(0, True)
    for to_x, to_y, to_core, x_relay, y_relay, x_core, y_core, d_core in small:
        x_relay.wait_recv()
        y_relay.wait_recv()
        d_core.start()
    across = []
    for g in order:
        if g == 0 and sets == 2:
            second_legs(0)
        for i in arrays:
            for came in legs[g]:
                came[i].wait_recv()

        def finish(block):
            for i in arrays:
                total = (
                    total_ref(g, i)[block, :]
                    + keep(g, i, 2)[block, :].astype(f32)
                    + keep(g, i, 3)[block, :].astype(f32)
                )
                if g == 0:
                    outs[i][block, :] = total
                else:
                    held[i][13][block, :] = total.astype(b16)

        each(0, rows, finish)
        if g == 1:
            for i in arrays:
                across.append(copy(21 * i + 20, held[i][13], held[i][14], peers[3]))
                across[-1].start()
    if sets == 2:
        for i in arrays:
            across[i].wait_recv()

        def add_z(block):
            for i in arrays:
                outs[i][block, :] = outs[i][block, :] + held[i][14][block, :].astype(f32)

        each(0, rows, add_z)
    for done in list(swaps.values()) + sent + across:
        done.wait_send()
    for copied in swapped + here:
        copied.wait()
    for group in small:
        for at in (2, 5, 6, 7):
            group[at].wait_recv()
        for copied in group:
            copied.wait_send()
    for to_far, to_near, relayed in along:
        to_near.wait_recv()
        relayed.wait_recv()
        for copied in (to_far, to_near, relayed):
            copied.wait_send()


def plane_scatter(number, *parts, sets=1, swaps=(), gathers=(), lines=(), after=()):
    if lax.axis_size("expert") != 8:
        return [
            lax.psum_scatter(part, "expert", scatter_dimension=0, tiled=True).astype(f32)
            for part in parts
        ] + [lax.all_gather(v, "expert", axis=0) for v in gathers] + [
            lax.all_gather(v, "dp", axis=0) for v in lines
        ]
    count = len(parts)
    others = list(swaps) + list(gathers) + list(lines) + list(after)
    moved = len(others) - len(after)
    sems = 21 * count + len(swaps) + 8 * len(gathers) + 3 * len(lines)
    rows = parts[0].shape[0] // (8 * sets)
    scratch = []
    for part in parts:
        columns = part.shape[1]
        for g in range(sets):
            scratch += [pltpu.VMEM((4, rows, columns), b16)] * 2
            scratch += [pltpu.VMEM((rows, columns), b16)] * 2
            scratch += [pltpu.VMEM((rows // 2, columns), b16)] * 2
        if sets == 2:
            scratch += [pltpu.VMEM((rows, columns), f32)]
            scratch += [pltpu.VMEM((rows, columns), b16)] * 2
    return pl.pallas_call(
        partial(
            scatter_kernel, sets, count, len(swaps), len(gathers), len(lines), len(after)
        ),
        out_shape=[jax.ShapeDtypeStruct((rows, part.shape[1]), f32) for part in parts]
        + [jax.ShapeDtypeStruct(v.shape, v.dtype) for v in swaps]
        + [jax.ShapeDtypeStruct((8,) + v.shape, v.dtype) for v in gathers]
        + [jax.ShapeDtypeStruct((4,) + v.shape, v.dtype) for v in lines],
        in_specs=[pl.BlockSpec(memory_space=pl.ANY)] * (count + len(others)),
        out_specs=[pl.BlockSpec(memory_space=pltpu.VMEM)] * count
        + [pl.BlockSpec(memory_space=pl.ANY)] * moved,
        scratch_shapes=scratch
        + [
            pltpu.SemaphoreType.DMA((sems,)),
            pltpu.SemaphoreType.DMA((sems,)),
            pltpu.SemaphoreType.DMA((8 * count + len(gathers) + len(lines),)),
        ],
        compiler_params=pltpu.CompilerParams(collective_id=number, has_side_effects=True),
        cost_estimate=pl.CostEstimate(flops=0, bytes_accessed=1024, transcendentals=0),
    )(*[part.reshape(8 * sets, rows, part.shape[1]) for part in parts], *others)


def rms_scale(value, gain):
    return value * lax.rsqrt(jnp.mean(value * value, axis=-1, keepdims=True) + epsilon) * gain


def rms_back(value, gain, grad):
    scale = lax.rsqrt(jnp.mean(value * value, axis=-1, keepdims=True) + epsilon)
    unit = value * scale
    inward = grad * gain
    back = scale * (inward - unit * jnp.mean(inward * unit, axis=-1, keepdims=True))
    return back, jnp.sum(grad * unit, axis=0)


def dot(a, b):
    return jnp.dot(a, b, preferred_element_type=f32)


def dot_nt(a, b):
    return lax.dot_general(a, b, NT, preferred_element_type=f32)


def dot_tn(a, b):
    return lax.dot_general(a, b, (((0,), (0,)), ((), ())), preferred_element_type=f32)


def silu_parts(value):
    sigma = jax.nn.sigmoid(value)
    return value * sigma, sigma * (1.0 + value * (1.0 - sigma))


def dense_gates(logits, route_ids):
    experts = logits.shape[1]
    ids = jnp.arange(experts, dtype=jnp.int32)
    named = jnp.any(route_ids[:, :, None] == ids, axis=1)
    top = jnp.max(jnp.where(named, logits, -jnp.inf), axis=1, keepdims=True)
    weight = jnp.where(named, jnp.exp(jnp.where(named, logits - top, 0.0)), 0.0)
    return weight / jnp.sum(weight, axis=1, keepdims=True)


def tie(*values):
    return lax.optimization_barrier(values)


def exchange(value, axis, distance):
    size = lax.axis_size(axis)
    return lax.ppermute(value, axis, [(i, i ^ distance) for i in range(size)])


def total_of(value, axes):
    for axis in axes:
        distance = 1
        while distance < lax.axis_size(axis):
            value = value + exchange(value, axis, distance)
            distance *= 2
    return value


def merge_kernel(near, parts, experts, tags, lowest_ref, select_ref, *refs):
    rows_refs, (small_ref, weight_ref) = refs[:parts], refs[parts : parts + 2]
    tag_refs, outs = refs[parts + 2 : parts + 2 + tags], refs[len(refs) - 1 - bool(tags) :]
    slots = select_ref.shape[1] // parts
    picked = [select_ref[0, k * slots : (k + 1) * slots, :] for k in range(parts)]
    total = sum(dot_tn(picked[k], rows_refs[k][0]) for k in range(parts))
    first = pl.program_id(0) < near

    @pl.when(first)
    def _():
        outs[0][...] = (total + dot(small_ref[...], weight_ref[...])).astype(b16)

    @pl.when(jnp.logical_not(first))
    def _():
        outs[0][...] = total.astype(b16)

    if tags:
        lane = lax.broadcasted_iota(jnp.int32, (slots, LANES), 1)
        tail = jnp.zeros((LEN, LANES), f32)
        for k in range(tags):
            value = jnp.broadcast_to(tag_refs[k][0], (slots, LANES))
            high = value.astype(b16)
            fine = (value - high.astype(f32)).astype(b16)
            column = lowest_ref[0] + k
            wide = jnp.where(
                lane == column,
                high.astype(f32),
                jnp.where(lane == column + experts, fine.astype(f32), 0.0),
            )
            tail = tail + dot_tn(picked[k], wide.astype(b16))
        outs[1][...] = tail.astype(b16)


def merge(select, parts, small, weight, experts=0, lowest=None, tags=(), after=()):
    seqs, slots, unused = select.shape
    slots = slots // len(parts)
    width = weight.shape[1]
    near = small.shape[0] // LEN
    each = lambda n: pl.BlockSpec((1, slots, n), lambda s, low: (s, 0, 0))
    token = lambda n: pl.BlockSpec((LEN, n), lambda s, low: (s, 0))
    lowest = jnp.zeros((1,), jnp.int32) if lowest is None else lowest.reshape(1)
    outs = [jax.ShapeDtypeStruct((seqs * LEN, width), b16)]
    outs += [jax.ShapeDtypeStruct((seqs * LEN, LANES), b16)] if tags else []

    def kernel(*refs):
        used = 2 + len(parts) + 2 + len(tags)
        merge_kernel(near, len(parts), experts, len(tags), *refs[:used], *refs[used + len(after) :])

    return pl.pallas_call(
        kernel,
        grid_spec=pltpu.PrefetchScalarGridSpec(
            num_scalar_prefetch=1,
            grid=(seqs,),
            in_specs=[pl.BlockSpec((1,) + select.shape[1:], lambda s, low: (s, 0, 0))]
            + [each(width)] * len(parts)
            + [
                pl.BlockSpec(
                    (LEN, small.shape[1]), lambda s, low: (jnp.minimum(s, near - 1), 0)
                ),
                pl.BlockSpec(weight.shape, lambda s, low: (0, 0)),
            ]
            + [each(1)] * len(tags)
            + [pl.BlockSpec(memory_space=pl.ANY)] * len(after),
            out_specs=[token(v.shape[1]) for v in outs],
        ),
        out_shape=outs,
        compiler_params=pltpu.CompilerParams(vmem_limit_bytes=32 << 20),
        cost_estimate=pl.CostEstimate(flops=0, bytes_accessed=1024, transcendentals=0),
    )(
        lowest,
        select,
        *[v.reshape(seqs, slots, width) for v in parts],
        small,
        weight,
        *[v.reshape(seqs, slots, 1) for v in tags],
        *after,
    )


def spread_kernel(parts, select_ref, rows_ref, *out_refs):
    slots = select_ref.shape[1] // parts
    rows = dot(select_ref[0], rows_ref[...]).astype(b16)
    for k in range(parts):
        out_refs[k][0] = rows[k * slots : (k + 1) * slots]


def spread(select, rows, parts):
    seqs, slots, unused = select.shape
    slots = slots // parts
    width = rows.shape[1]
    outs = pl.pallas_call(
        partial(spread_kernel, parts),
        grid=(seqs,),
        in_specs=[
            pl.BlockSpec((1,) + select.shape[1:], lambda s: (s, 0, 0)),
            rows_of(width),
        ],
        out_specs=[pl.BlockSpec((1, slots, width), lambda s: (s, 0, 0))] * parts,
        out_shape=[jax.ShapeDtypeStruct((seqs, slots, width), b16)] * parts,
        compiler_params=pltpu.CompilerParams(vmem_limit_bytes=32 << 20),
        cost_estimate=pl.CostEstimate(flops=0, bytes_accessed=1024, transcendentals=0),
    )(select, rows)
    return [v.reshape(seqs * slots, width) for v in outs]


def expert_kernel(
    x_ref,
    dy_ref,
    gate_ref,
    bank_ref,
    out_ref,
    back_ref,
    dgate_ref,
    wide_ref,
    tall_ref,
    down_ref,
    wide_sum,
    tall_sum,
):
    hidden = tall_ref.shape[0]
    third = x_ref.shape[1] // 3
    part = hidden // 4

    @pl.when(pl.program_id(0) == 0)
    def _():
        for i in range(4):
            for k in range(3):
                down_ref[i * part : (i + 1) * part, k * third : (k + 1) * third] = bank_ref[
                    (3 * i + k) * part : (3 * i + k + 1) * part, 2 * hidden :
                ]
        wide_sum[...] = jnp.zeros_like(wide_sum)
        tall_sum[...] = jnp.zeros_like(tall_sum)

    x, gate = x_ref[...], gate_ref[...]
    pre = dot(x, bank_ref[:, : 2 * hidden])
    lin = pre[:, hidden:]
    sigma = sigmoid(pre[:, :hidden])
    soft = pre[:, :hidden] * sigma
    slope = sigma * (1.0 + pre[:, :hidden] * (1.0 - sigma))
    hid = (soft * lin).astype(b16)
    made = dot(hid, down_ref[...]).astype(b16).astype(f32)
    dy = dy_ref[...].astype(f32)
    dgate_ref[...] = jnp.sum(made * dy, axis=1, keepdims=True)
    out_ref[...] = (made * gate).astype(b16)
    dmade = (dy * gate).astype(b16)
    dhid = dot_nt(dmade, down_ref[...])
    dpre = jnp.concatenate([dhid * lin * slope, dhid * soft], axis=1).astype(b16)
    back_ref[...] = dot_nt(dpre, bank_ref[:, : 2 * hidden]).astype(b16)
    wide_sum[...] += dot_tn(x, dpre)
    tall_sum[...] += dot_tn(hid, dmade)

    @pl.when(pl.program_id(0) == pl.num_programs(0) - 1)
    def _():
        wide_ref[...] = wide_sum[...].astype(b16)
        tall_ref[...] = tall_sum[...].astype(b16)


def expert(x, dy, gate, bank, hidden, after=()):
    rows, width = x.shape
    block = 256
    per = pl.BlockSpec((block, width), lambda s: (s, 0))
    one = pl.BlockSpec((block, 1), lambda s: (s, 0))

    def kernel(*refs):
        expert_kernel(*refs[:4], *refs[4 + len(after) :])

    return pl.pallas_call(
        kernel,
        grid=(rows // block,),
        in_specs=[
            per,
            per,
            one,
            pl.BlockSpec(bank.shape, lambda s: (0, 0), pipeline_mode=pl.Buffered(1)),
        ]
        + [pl.BlockSpec(memory_space=pl.ANY)] * len(after),
        out_specs=[per, per, one, fixed(width, 2 * hidden), fixed(hidden, width)],
        out_shape=[
            jax.ShapeDtypeStruct((rows, width), b16),
            jax.ShapeDtypeStruct((rows, width), b16),
            jax.ShapeDtypeStruct((rows, 1), f32),
            jax.ShapeDtypeStruct((width, 2 * hidden), b16),
            jax.ShapeDtypeStruct((hidden, width), b16),
        ],
        scratch_shapes=[
            pltpu.VMEM((hidden, width), b16),
            pltpu.VMEM((width, 2 * hidden), f32),
            pltpu.VMEM((hidden, width), f32),
        ],
        compiler_params=pltpu.CompilerParams(vmem_limit_bytes=48 << 20),
        cost_estimate=pl.CostEstimate(flops=0, bytes_accessed=1024, transcendentals=0),
    )(x, dy, gate, bank, *after)


def shared_kernel(
    x_ref, dy_ref, wide_ref, tall_ref, hid_ref, dpre_ref, wide_out, tall_out, wide_sum, tall_sum
):
    hidden = tall_ref.shape[0]

    @pl.when(pl.program_id(0) == 0)
    def _():
        wide_sum[...] = jnp.zeros_like(wide_sum)
        tall_sum[...] = jnp.zeros_like(tall_sum)

    x, dy = x_ref[...], dy_ref[...]
    pre = dot(x, wide_ref[...])
    lin = pre[:, hidden:]
    sigma = sigmoid(pre[:, :hidden])
    soft = pre[:, :hidden] * sigma
    slope = sigma * (1.0 + pre[:, :hidden] * (1.0 - sigma))
    hid = (soft * lin).astype(b16)
    dhid = dot_nt(dy, tall_ref[...])
    dpre = jnp.concatenate([dhid * lin * slope, dhid * soft], axis=1).astype(b16)
    hid_ref[...] = hid
    dpre_ref[...] = dpre
    wide_sum[...] += dot_tn(x, dpre)
    tall_sum[...] += dot_tn(hid, dy)

    @pl.when(pl.program_id(0) == pl.num_programs(0) - 1)
    def _():
        wide_out[...] = wide_sum[...].astype(b16)
        tall_out[...] = tall_sum[...].astype(b16)


def shared_expert(x, dy, wide, tall, rows, after=()):
    width, hidden = x.shape[1], tall.shape[0]
    block = 256
    per = lambda n: pl.BlockSpec((block, n), lambda s: (s, 0))

    def kernel(*refs):
        shared_kernel(*refs[:4], *refs[4 + len(after) :])

    return pl.pallas_call(
        kernel,
        grid=(rows // block,),
        in_specs=[per(width), per(width), fixed(*wide.shape), fixed(*tall.shape)]
        + [pl.BlockSpec(memory_space=pl.ANY)] * len(after),
        out_specs=[per(hidden), per(2 * hidden), fixed(*wide.shape), fixed(*tall.shape)],
        out_shape=[
            jax.ShapeDtypeStruct((rows, hidden), b16),
            jax.ShapeDtypeStruct((rows, 2 * hidden), b16),
            jax.ShapeDtypeStruct(wide.shape, b16),
            jax.ShapeDtypeStruct(tall.shape, b16),
        ],
        scratch_shapes=[pltpu.VMEM(wide.shape, f32), pltpu.VMEM(tall.shape, f32)],
        compiler_params=pltpu.CompilerParams(vmem_limit_bytes=32 << 20),
        cost_estimate=pl.CostEstimate(flops=0, bytes_accessed=1024, transcendentals=0),
    )(x, dy, wide, tall, *after)


def bank_kernel(parity_ref, gate_ref, up_ref, down_ref, out_ref):
    columns = gate_ref.shape[2]
    rows = down_ref.shape[1]
    out_ref[0, 0, :, :columns] = gate_ref[0]
    out_ref[0, 0, :, columns : 2 * columns] = up_ref[0]
    for k in range(3):
        out_ref[0, 0, k * rows : (k + 1) * rows, 2 * columns :] = down_ref[
            0, :, k * columns : (k + 1) * columns
        ]


def bank_rows(parity, gate, up, down):
    local, rows, columns = gate.shape
    half = local // 2
    which = lambda side, e, p: ((p[0] + side) % 2 * half + e, 0, 0)
    block = lambda v: pl.BlockSpec((1,) + v.shape[1:], which)
    return pl.pallas_call(
        bank_kernel,
        grid_spec=pltpu.PrefetchScalarGridSpec(
            num_scalar_prefetch=1,
            grid=(2, half),
            in_specs=[block(gate), block(up), block(down)],
            out_specs=pl.BlockSpec(
                (1, 1, rows, 3 * columns), lambda side, e, p: (side, e, 0, 0)
            ),
        ),
        out_shape=jax.ShapeDtypeStruct((2, half, rows, 3 * columns), b16),
        cost_estimate=pl.CostEstimate(flops=0, bytes_accessed=1024, transcendentals=0),
    )(parity.reshape(1), gate, up, down)


def plain_expert(x, dy, gate, bank, planes):
    width = x.shape[1]
    hidden = bank.shape[1] // 3
    gate_up = bank[:, : 2 * hidden]
    down = bank[:, 2 * hidden :].reshape(planes, 3, hidden // planes, width // 3)
    down = down.transpose(0, 2, 1, 3).reshape(hidden, width)
    pre = dot(x, gate_up)
    soft, slope = silu_parts(pre[:, :hidden])
    lin = pre[:, hidden:]
    hid = (soft * lin).astype(b16)
    made = dot(hid, down).astype(b16).astype(f32)
    dy = dy.astype(f32)
    dmade = (dy * gate).astype(b16)
    dhid = dot_nt(dmade, down)
    dpre = jnp.concatenate([dhid * lin * slope, dhid * soft], axis=1).astype(b16)
    return (
        (made * gate).astype(b16),
        dot_nt(dpre, gate_up).astype(b16),
        jnp.sum(made * dy, axis=1, keepdims=True),
        dot_tn(x, dpre).astype(b16),
        dot_tn(hid, dmade).astype(b16),
    )


class Heads:
    def __init__(self, planes, plane, out_rows, width):
        self.planes, self.plane, self.width = planes, plane, width
        self.each = H // plane
        self.padded = -(-self.each // 2) * 2
        own = 2 * out_rows
        self.owned = own % width == 0 and planes % 2 == 0 and self.padded == self.each
        self.run = own // width if self.owned else self.each

    def group(self, value, size):
        lead = value.shape[:-1]
        if self.owned:
            value = value.reshape(lead + (2, self.planes // 2, self.plane // 2, self.run * size))
            n = len(lead)
            value = jnp.transpose(value, tuple(range(n)) + (n + 2, n, n + 1, n + 3))
        value = value.reshape(lead + (self.plane, self.each * size))
        pad = (self.padded - self.each) * size
        return jnp.pad(value, [(0, 0)] * (len(lead) + 1) + [(0, pad)]) if pad else value

    def ungroup(self, value, size):
        lead = value.shape[:-2]
        value = value[..., : self.each * size]
        if self.owned:
            value = value.reshape(lead + (self.plane // 2, 2, self.planes // 2, self.run * size))
            n = len(lead)
            value = jnp.transpose(value, tuple(range(n)) + (n + 1, n + 2, n, n + 3))
        return value.reshape(lead + (H * size,))


def body(
    block_input,
    out_grad,
    routes,
    norm_in,
    in_proj,
    conv_weight,
    conv_bias,
    step_bias,
    log_rate,
    skip_gain,
    mixer_gain,
    out_proj,
    norm_mid,
    router,
    shared_gate,
    shared_up,
    shared_down,
    expert_gate,
    expert_up,
    expert_down,
):
    both = ("dp", "expert")
    planes, plane = lax.axis_size("dp"), lax.axis_size("expert")
    at = lax.axis_index("expert")
    core = at % 2
    micro, length, width = block_input.shape
    picks = routes.shape[-1]
    local = expert_gate.shape[0]
    experts = local * plane
    sets = 2 if planes == 4 and plane == 8 else 1
    place = lax.axis_index("dp")
    odd = place % 2 == 1
    taken = local // sets
    capacity = 3 * length * picks // (2 * experts)
    slots = -(-capacity // 8) * 8
    tokens = micro * length
    shard = in_proj.shape[0]
    out_rows = out_proj.shape[0]
    inner = out_rows * planes * plane
    hr = shared_down.shape[0]
    fs = hr * planes
    ehidden = expert_gate.shape[2]
    gather = lambda v, axes: lax.all_gather(v, axes, axis=0, tiled=True)
    scatter = lambda v, axes: lax.psum_scatter(v, axes, scatter_dimension=0, tiled=True)
    heads = Heads(planes, plane, out_rows, inner // H)
    size = heads.width
    wide = heads.padded * size
    states = conv_weight.shape[1] - inner
    main = 2 * wide + states + LANES

    signal = in_proj[:, inner : 2 * inner]
    maps = in_proj[:, 2 * inner : 2 * inner + states]
    steps = in_proj[:, 2 * inner + states :]
    common = jnp.concatenate([norm_in[:, None], norm_mid[:, None], router], axis=1)
    spare = LANES - heads.padded - common.shape[1]
    repeat = lambda v: jnp.broadcast_to(v[:, None, :], (shard, plane, v.shape[1]))
    split = lambda v: v.reshape(shard, planes, plane, hr).transpose(0, 2, 1, 3).reshape(shard, plane, fs)
    sent = jnp.concatenate(
        [
            heads.group(in_proj[:, :inner], size),
            heads.group(signal, size),
            repeat(maps),
            heads.group(steps, 1),
            repeat(common),
            jnp.zeros((shard, plane, spare), b16),
            split(shared_gate),
            split(shared_up),
        ],
        axis=2,
    ).transpose(1, 0, 2)
    came = lax.all_to_all(sent, "expert", split_axis=0, concat_axis=0, tiled=True)

    third = width // 3
    part = expert_down.shape[1]
    stacked = lambda v: jnp.concatenate([v[:, k * third : (k + 1) * third] for k in range(3)], axis=0)
    ends, gives = None, []
    if sets == 2:
        ends = [[0, 2], [1, 3]]
        sides = bank_rows((place % 2).astype(jnp.int32), expert_gate, expert_up, expert_down)
        gives = [sides]
    else:
        banks = [
            jnp.concatenate([expert_gate[e], expert_up[e], stacked(expert_down[e])], axis=1)
            for e in range(local)
        ]

    own_routes = jnp.pad(routes.reshape(tokens, picks).astype(b16), ((0, 0), (0, LANES - picks)))
    flat_in = block_input.reshape(tokens, width)
    grad_low = out_grad.reshape(tokens, width)
    flat_in, came = tie(flat_in, came)
    all_in, all_grad, all_routes, *swapped = plane_gather(
        0, flat_in, grad_low, own_routes, sets=(1, sets, sets), swaps=gives
    )
    if sets == 2:
        banks = [v.reshape(-1, v.shape[2]) for v in swapped]
    proj = gather(came.reshape(plane * shard, -1), "dp")
    in_w = proj[:, :main]
    gate_up = proj[:, main:]
    first = 2 * wide + states + heads.padded
    gain_in = proj[:, first].astype(f32)
    gain_mid = proj[:, first + 1].astype(f32)
    route_proj = proj[:, first + 2 : first + 2 + experts]
    all_routes = all_routes[:, :picks].astype(jnp.int32)
    near = all_in.shape[0]
    count = all_grad.shape[0]
    seqs = count // LEN

    out_shard = jnp.concatenate(
        [
            jnp.concatenate([out_proj, mixer_gain[:, None]], axis=1),
            jnp.pad(shared_down, ((0, 0), (0, 1))),
        ],
        axis=0,
    )
    out_shard = jnp.pad(out_shard, ((0, 0), (0, LANES - 1)))
    half = planes // 2
    if heads.owned:
        out_all = gather(out_shard, "dp").reshape(planes, out_rows + hr, -1)
        down_w = out_all[:, out_rows:, :width].reshape(fs, width)
        pieces = out_all[:, :out_rows].reshape(2, half, out_rows, -1)
        low = core == 0
        keep = jnp.where(low, pieces[0], pieces[1])
        other = exchange(jnp.where(low, pieces[1], pieces[0]), "expert", 1)
        out_w = jnp.stack([jnp.where(low, keep, other), jnp.where(low, other, keep)], axis=1)
        out_w = out_w.reshape(wide, -1)
    else:
        down_w = gather(shared_down, "dp")
        out_all = gather(out_shard[:out_rows], both)
        out_w = lax.dynamic_slice_in_dim(out_all, at * heads.each * size, heads.each * size, 0)
        out_w = jnp.pad(out_w, ((0, wide - heads.each * size), (0, 0)))
    gain_mix = out_w[:, width]
    out_w = out_w[:, :width]

    pick_own = lambda v: lax.dynamic_index_in_dim(v, at, v.ndim - 2, keepdims=False)
    lane_pad = lambda v: jnp.pad(v.astype(f32), (0, LANES - v.shape[0])).reshape(1, LANES)
    own_lanes = lambda v: jnp.concatenate(
        [pick_own(heads.group(v[:, :inner], size)), v[:, inner:]], axis=1
    ).astype(f32)
    params = (
        own_lanes(conv_weight),
        own_lanes(conv_bias[None]),
        lane_pad(pick_own(heads.group(step_bias, 1))),
        lane_pad(pick_own(heads.group(log_rate, 1))),
        pick_own(heads.group(jnp.repeat(skip_gain, size), size)).astype(f32).reshape(1, -1),
        gain_mix.astype(f32).reshape(1, -1),
    )

    normed = rms_scale(all_in.astype(f32), gain_in).astype(b16)
    merged = dot(normed, in_w)
    mixed, joined, square = mix_forward(merged, params)
    square = jnp.sum(square, axis=1, keepdims=True)
    square_high = square.astype(b16)
    square_low = (square - square_high.astype(f32)).astype(b16)
    lane = jnp.arange(LANES)[None]
    tail = jnp.where(lane == 2 * at, square_high, jnp.where(lane == 2 * at + 1, square_low, 0))
    summed, squares = plane_scatter(2, dot(mixed, out_w).astype(b16), tail.astype(b16))
    scale = lax.rsqrt(jnp.sum(squares, axis=1, keepdims=True) / inner + epsilon)
    mixer_out = scale * summed
    start = flat_in.astype(f32)
    grad_out = grad_low.astype(f32)
    middle = start + mixer_out
    routed = rms_scale(middle, gain_mid).astype(b16)
    whole = [
        lax.all_gather(banks[e], "dp", axis=0, tiled=True, axis_index_groups=ends)
        for e in range(taken)
    ]
    if sets == 2:
        routed, whole[0] = tie(routed, whole[0])
    (all_routed,) = plane_gather(3, routed, sets=sets)

    lowest = at * local + (place % sets) * taken
    mine = lowest + jnp.arange(taken, dtype=jnp.int32)
    marks = jnp.any(all_routes[:, :, None] == mine, axis=1).reshape(seqs, LEN, taken)
    earlier = jnp.arange(LEN)[:, None] > jnp.arange(LEN)[None, :]
    rank = jnp.einsum(
        "ts,nse->net", earlier.astype(b16), marks.astype(b16), preferred_element_type=f32
    ).astype(jnp.int32)
    places = jnp.arange(slots, dtype=jnp.int32)
    chosen = (rank[:, :, None, :] == places[None, None, :, None]) & (
        marks.transpose(0, 2, 1)[:, :, None, :]
    )
    select = chosen.astype(b16)
    gates_all = dense_gates(dot(all_routed, route_proj), all_routes)
    gates_mine = lax.dynamic_slice_in_dim(gates_all, lowest, taken, axis=1)
    gates_mine = gates_mine.reshape(seqs, LEN, taken).transpose(0, 2, 1)
    slot_gates = jnp.sum(jnp.where(chosen, gates_mine[:, :, None, :], 0.0), axis=-1)

    select = select.reshape(seqs, taken * slots, LEN)
    rows_in = spread(select, all_routed, taken)
    rows_grad = spread(select, all_grad, taken)
    outs, backs, dgates, sums = [], [], [], []
    tied = []
    for e in range(taken):
        gate = slot_gates[:, e].reshape(seqs * slots, 1)
        if sets == 2:
            out, grad, dgate, *made_grads = expert(
                rows_in[e], rows_grad[e], gate, whole[e], ehidden, after=tied
            )
        else:
            out, grad, dgate, *made_grads = plain_expert(
                rows_in[e], rows_grad[e], gate, whole[e], planes
            )
        outs.append(out)
        backs.append(grad)
        dgates.append(dgate)
        sums.append(
            [
                lax.psum_scatter(
                    v, "dp", scatter_dimension=0, tiled=True, axis_index_groups=ends
                )
                for v in made_grads
            ]
        )
        if e == 0:
            hid, dpre, shared_grad, down_grad = shared_expert(
                all_routed, all_grad, gate_up, down_w, near, after=made_grads
            )
            tied = [hid, dpre, shared_grad, down_grad]
    back_part, back_gates = merge(
        select, backs, dpre, gate_up.T, experts, lowest, tags=dgates
    )
    back, back_gates = plane_scatter(
        4, back_part, back_gates, sets=sets, after=made_grads
    )

    gates = dense_gates(dot(routed, route_proj), routes.reshape(tokens, picks))
    dgate = back_gates[:, :experts] + back_gates[:, experts : 2 * experts]
    dlogits = (gates * (dgate - jnp.sum(gates * dgate, axis=1, keepdims=True))).astype(b16)
    droute = back + dot_nt(dlogits, route_proj)
    dmid_part, mid_gain_grad = rms_back(middle, gain_mid, droute)
    dmid = grad_out + dmid_part

    def small_rows(weight_grad, bias_grad, skip_grad, head_grad):
        spot = lambda v, size: heads.ungroup(
            lax.dynamic_update_slice_in_dim(
                jnp.zeros(v.shape[:-1] + (plane, v.shape[-1]), f32), v[..., None, :], at, v.ndim - 1
            ),
            size,
        )
        taps = jnp.concatenate([weight_grad, bias_grad], axis=0)
        taps = jnp.concatenate([spot(taps[:, :wide], size), taps[:, wide:]], axis=1)
        skip_grad = jnp.sum(skip_grad.reshape(heads.padded, size), axis=1)
        head_rows = jnp.concatenate([head_grad[:2, : heads.padded], skip_grad[None]], axis=0)
        head_rows = spot(head_rows, 1).reshape(1, -1)
        head_rows = jnp.pad(head_rows, ((0, 0), (0, taps.shape[1] - head_rows.shape[1])))
        rows = jnp.concatenate([taps, head_rows], axis=0)
        return jnp.pad(rows, ((0, 16 - rows.shape[0]), (0, 0)))

    scaled = (dmid * scale).astype(b16)
    inward = scale * jnp.sum(scaled.astype(f32) * mixer_out, axis=1, keepdims=True) / inner
    inward_high = inward.astype(b16)
    inward_low = (inward - inward_high.astype(f32)).astype(b16)
    tail = jnp.where(lane == 0, inward_high, jnp.where(lane == 1, inward_low, 0)).astype(b16)
    shared_sum = scatter(shared_grad, "dp")
    all_mid, all_inward = plane_gather(6, scaled, tail, after=sums[0][1:])
    kept, sent = [], []
    if sets == 2:
        for group in sums:
            for v in group:
                rows = v.shape[0] // 2
                kept.append(jnp.where(odd, v[rows:], v[:rows]))
                sent.append(jnp.where(odd, v[:rows], v[rows:]))
    swapped = [exchange(v, "dp", 1) for v in sent]
    all_inward = all_inward[:, :1].astype(f32) + all_inward[:, 1:2].astype(f32)
    dmerged, weight_grad, bias_grad, skip_grad, head_grad = mix_backward(
        merged, joined, dot_nt(all_mid, out_w), all_inward, params
    )
    taps_of = small_rows(weight_grad, bias_grad, skip_grad, head_grad)
    dnormed, taps_of = plane_scatter(
        7,
        dot_nt(dmerged, in_w).astype(b16),
        gathers=[taps_of],
        after=[shared_sum],
    )
    taps_of = jnp.sum(taps_of, axis=0)
    out_part = merge(select, outs, hid, down_w, after=[dnormed])[0]
    out_part, dnormed = tie(out_part, dnormed)
    out_sum, small = plane_scatter(5, out_part, sets=sets, lines=[taps_of], after=swapped)
    small = jnp.sum(small, axis=0)

    unsplit = lambda v: (
        v.reshape(plane, shard, planes, hr).transpose(1, 2, 0, 3).reshape(shard, planes * plane * hr)
    )
    out_w_grad = dot_tn(mixed, all_mid).astype(b16)
    if heads.owned:
        parts = out_w_grad.reshape(half, 2, out_rows, width)
        keep = jnp.where(low, parts[:, 0], parts[:, 1])
        other = exchange(jnp.where(low, parts[:, 1], parts[:, 0]), "expert", 1)
        out_parts = jnp.concatenate([jnp.where(low, keep, other), jnp.where(low, other, keep)])
        rows = jnp.concatenate([out_parts, down_grad.reshape(planes, hr, width)], axis=1)
        rows = scatter(rows.reshape(planes * (out_rows + hr), width), "dp").astype(f32)
        out_w_grad, down_grad = rows[:out_rows], rows[out_rows:]
    else:
        rows = lax.dynamic_update_slice_in_dim(
            jnp.zeros((inner, width), b16), out_w_grad[: heads.each * size], at * heads.each * size, 0
        )
        out_w_grad = scatter(rows, both).astype(f32)
        down_grad = scatter(down_grad, "dp").astype(f32)

    extra = jnp.concatenate(
        [
            jnp.zeros((width, heads.padded + 1), f32),
            mid_gain_grad[:, None],
            dot_tn(routed, dlogits),
            jnp.zeros((width, spare), f32),
        ],
        axis=1,
    )
    in_w_grad = dot_tn(normed, dmerged)
    in_w_grad = jnp.concatenate([in_w_grad[:, :-LANES], in_w_grad[:, -LANES:] + extra], axis=1)
    in_w_grad = jnp.concatenate([scatter(in_w_grad.astype(b16), "dp"), shared_sum], axis=1)
    in_w_grad = lax.all_to_all(
        in_w_grad.reshape(plane, shard, -1), "expert", split_axis=0, concat_axis=0, tiled=True
    ).astype(f32)
    in_w_grad, shared_grad = in_w_grad[:, :, :main], in_w_grad[:, :, main:]
    by_row = in_w_grad.transpose(1, 0, 2)
    step_part = 2 * wide + states
    in_grad = jnp.concatenate(
        [
            heads.ungroup(by_row[:, :, :wide], size),
            heads.ungroup(by_row[:, :, wide : 2 * wide], size),
            jnp.sum(by_row[:, :, 2 * wide : step_part], axis=1),
            heads.ungroup(by_row[:, :, step_part : step_part + heads.padded], 1),
        ],
        axis=1,
    )
    shared_common = jnp.sum(by_row[:, :, first:], axis=1)
    gain_in_grad = jnp.sum(in_proj.astype(f32) * in_grad, axis=1) / norm_in.astype(f32)
    gain_mix_grad = jnp.sum(out_proj.astype(f32) * out_w_grad, axis=1) / mixer_gain.astype(f32)

    bank_grads = []
    for e in range(taken):
        if sets == 1:
            bank_grads.append([v.astype(f32) for v in sums[e]])
            continue
        pair = [
            (jnp.where(odd, came, keep), jnp.where(odd, keep, came))
            for keep, came in zip(kept[2 * e : 2 * e + 2], swapped[2 * e : 2 * e + 2])
        ]
        bank_grads.append([v.astype(f32) for v, _ in pair])
        bank_grads.append([v.astype(f32) for _, v in pair])
    bank_grads = bank_grads[::2] + bank_grads[1::2] if sets == 2 else bank_grads
    dstart, unused = rms_back(start, gain_in, dnormed)
    shape = block_input.shape
    return (
        (middle + out_sum).astype(b16).reshape(shape),
        (dmid + dstart).reshape(shape),
        gain_in_grad,
        in_grad,
        small[:4],
        small[4],
        small[5, :H],
        small[5, H : 2 * H],
        small[5, 2 * H : 3 * H],
        gain_mix_grad,
        out_w_grad,
        shared_common[:, 1],
        shared_common[:, 2 : 2 + experts],
        unsplit(shared_grad[:, :, :fs].transpose(0, 1, 2)),
        unsplit(shared_grad[:, :, fs:]),
        down_grad,
        jnp.stack([v[:, :ehidden] for v, _ in bank_grads]),
        jnp.stack([v[:, ehidden:] for v, _ in bank_grads]),
        jnp.stack([v for _, v in bank_grads]),
    )


def solution(mesh):
    both = ("dp", "expert")
    rows, matrix, bank = P(both), P(both, None), P("expert", "dp", None)
    token = P(None, both, None)
    in_specs = (token, token, token, rows, matrix, P(), P(), P(), P(), P(), rows, matrix, rows)
    in_specs = in_specs + (matrix, matrix, matrix, matrix, bank, bank, bank)
    out_specs = (token, token, rows, matrix, P(), P(), P(), P(), P(), rows, matrix, rows)
    out_specs = out_specs + (matrix, matrix, matrix, matrix, bank, bank, bank)
    return jax.shard_map(body, mesh=mesh, in_specs=in_specs, out_specs=out_specs, check_vma=False)
```
